32 devices in a mesh: rep: 8 (over z, y), section: 4 (over x, core).
Axes of the slice: x: 2, y: 2, z: 4, core: 2. Of those that a mesh axis runs over, the one named last changes fastest.
Arguments:
- layer_input: bfloat16 [4096, 1024], P(('rep', 'section')), may hold values from -6 to 6
- utt_frames: int32 [32, 4], P(('rep', 'section')), may hold values from 1 to 64, 128 in all within a row
- w_pointwise1: bfloat16 [1024, 2048], replicated, may hold values from -0.1875 to 0.1875
- conv_taps: bfloat16 [9, 1024], replicated, may hold values from -2 to 2
- conv_scale: float32 [1024], replicated, may hold values from 0.5 to 2
- conv_shift: float32 [1024], replicated, may hold values from -1 to 1
- w_pointwise2: bfloat16 [1024, 1024], replicated, may hold values from -0.1875 to 0.1875
- adj_grad: bfloat16 [2048, 8192], P('rep', 'section'), may hold values from -6 to 6
- proj_weight: bfloat16 [1024, 8192], P('rep', 'section'), may hold values from -0.0625 to 0.0625
- adj_target: int32 [2048, 1], replicated, may hold values from 0 to 7; in each aligned block of 64 rows (0 to 63, 64 to 127, ...) at most 16 rows name the same one
- adj_frame: int32 [2048], replicated, may hold values from 0 to 127
Outputs:
- input_grad: bfloat16 [4096, 1024], P(('rep', 'section'))
- w1_grad: float32 [1024, 2048], P(('rep', 'section'))
- w2_grad: float32 [1024, 1024], P(('rep', 'section'))
- taps_grad: float32 [1024, 9], P(('rep', 'section'))
The draws below stay inside these ranges and needn't reach their ends.
Inputs may be any that keep to these rules, and one draw needn't show every extreme that they name: `utt_frames`: each row holds the frame counts of 4 utterances packed in order into one shard; the row sums to 128. `adj_target`: in each aligned block of 64 rows at most 16 rows name the same replica.
All inputs are finite; a program needn't handle non-finite values.
Results may differ from the reference program's by a relative error of at most 0.0075.
Values may be sent and summed in bfloat16 or wider, within the bound.
No kernel may reach another device: no remote copies, remote signals or barrier semaphores. Data moves between devices by JAX's collectives and lax.ppermute only.
A program may use at most 128 MiB of HBM per device.

```python
import math
import jax
import jax.numpy as jnp
import numpy as np
from jax import lax

D = 1024
EMB = 8192
TAPS = 9
ROWS_DEV = 128
ADJ_DEV = 256
UTT_DEV = 4
REPLICAS = 8
SECTIONS = 4
SHARDS = 32
FRAMES = 4096
ADJ = 2048
QUARTER = 64
CAP = 16
UTT_MOST = 64


def with_ends(values, rng, low, top_value):
    longest = values.shape.index(max(values.shape))
    spots = []
    for shift in (0, 1):
        where = [jax.random.randint(jax.random.fold_in(rng, axis), (), 0, length) for axis, length in enumerate(values.shape)]
        where[longest] = (where[longest] + shift) % values.shape[longest]
        spots.append(tuple(where))
    return values.at[spots[0]].set(low).at[spots[1]].set(top_value)


def with_spikes(values, rng, source, target, parts, factor):
    owner, partner = [(jnp.arange(values.shape[dim]) // (values.shape[dim] // parts)).reshape([-1 if axis == dim else 1 for axis in range(values.ndim)]) for dim in (source, target)]
    chosen = jax.random.permutation(rng, parts)[partner]
    strong = (owner == chosen) | (owner == (partner + parts // 2) % parts)
    return jnp.where(strong, factor * values, values)


def level_of(key, extent, cuts, least, top_value):
    loudness = 1.0
    for dim, parts in cuts:
        heights = jax.random.uniform(jax.random.fold_in(jax.random.fold_in(key, 6), dim), (parts,), jnp.float32, least / len(cuts), top_value / len(cuts))
        loudness = loudness * jnp.repeat(jnp.exp(heights), extent[dim] // parts).reshape((-1,) + (1,) * (len(extent) - 1 - dim))
    return loudness


def length_profile(number_of, total, most, skew):
    weights = [(1 << 20) // math.isqrt(grade ** skew) + 1 for grade in range(2, number_of + 1)]
    surplus, counts = total - most - (number_of - 1), [1] * (number_of - 1)
    while surplus > 0:
        free = [i for i in range(number_of - 1) if counts[i] < most]
        mass, left = sum([weights[i] for i in free]), surplus
        for i in free:
            extra = min(most - counts[i], max(1, left * weights[i] // mass), surplus)
            counts[i] = counts[i] + extra
            surplus = surplus - extra
    return np.array([most] + counts)


def uneven_parts(stream_key, number_of, total, most, skew):
    if number_of == 2:
        one = jax.random.randint(stream_key, (), max(1, total - most), min(most, total - 1) + 1)
        return jnp.stack([one, total - one])
    sizes = jnp.asarray(length_profile(number_of, total, most, skew), jnp.int32)
    couples = (number_of - 1) // 2
    donor, receiver = sizes[1:1 + 2 * couples:2], sizes[2:2 + 2 * couples:2]
    room = jnp.minimum(donor - 1, most - receiver)
    moved = jax.random.randint(jax.random.fold_in(stream_key, 1), (couples,), 0, 1 << 20) % (room + 1)
    sizes = sizes.at[1:1 + 2 * couples:2].set(donor - moved).at[2:2 + 2 * couples:2].set(receiver + moved)
    return sizes[jax.random.permutation(jax.random.fold_in(stream_key, 2), number_of)]


def routed_block(own_key, own, number, rows, amount, top, bound, lean):
    sequence = jax.random.permutation(own_key, amount)
    heavy_load, usual = portions_of(amount, rows * top, bound, lean, True), portions_of(amount, rows * top, bound, lean, False)
    places = jnp.arange(amount)

    def named(sizes, offset_by):
        used = int((sizes > 0).sum())
        fixed = max(1, used // 4)
        moved = fixed + (places - fixed + offset_by * (used - fixed)) % max(1, amount - fixed)
        return jnp.zeros((amount,), jnp.int32).at[sequence[jnp.where(places < fixed, places, moved)]].set(jnp.asarray(sizes, jnp.int32))

    sizes = jnp.where(number % 4 == 0, named(heavy_load, number // 4), named(usual, number - number // 4 - 1))
    mixed = jax.random.permutation(jax.random.fold_in(own, 3), amount)
    giver, sink = mixed[0:amount // 2 * 2:2], mixed[1:amount // 2 * 2:2]
    slack = jnp.minimum(sizes[giver] - 1, bound - sizes[sink]) // 2
    slack = jnp.where((giver == sequence[0]) | (sink == sequence[0]) | (sizes[sink] == 0), 0, jnp.maximum(slack, 0))
    moved = jax.random.randint(jax.random.fold_in(own, 4), (amount // 2,), 0, 1 << 20) % (slack + 1)
    sizes = sizes.at[giver].add(-moved).at[sink].add(moved)
    items = jnp.searchsorted(jnp.cumsum(sizes), jnp.arange(rows * top), side="right").astype(jnp.int32)
    grid = items.reshape(top, rows).T
    grid = grid[jax.random.permutation(jax.random.fold_in(own, 1), rows)]
    offset_by = jax.random.randint(jax.random.fold_in(own, 2), (rows, 1), 0, top)
    return jnp.take_along_axis(grid, (jnp.arange(top)[None, :] + offset_by) % top, axis=1)


def portions_of(number_of, total, limit, slope, full):
    weights = [(1 << 20) // math.isqrt(grade ** slope) + 1 for grade in range(1, number_of + 1)]
    largest = limit if full else min(limit, max(-(-total // number_of), total * weights[0] // sum(weights)))
    least = 1 if total - largest >= number_of - 1 else 0
    holding, rest = [largest] + [least] * (number_of - 1), total - largest - least * (number_of - 1)
    while rest > 0:
        candidates = [i for i in range(1, number_of) if holding[i] < largest] or [i for i in range(1, number_of) if holding[i] < limit]
        whole, left = sum([weights[i] for i in candidates]), rest
        for i in candidates:
            extra = min(limit - holding[i], max(1, left * weights[i] // whole), rest)
            holding[i] = holding[i] + extra
            rest = rest - extra
    return np.array(holding)


def bell_draw(key, shape, deviation, limit, cuts=(), kind=jnp.bfloat16):
    factor_of = level_of(key, shape, cuts, -0.22, 0.18) if cuts else 1.0
    entries = jax.random.normal(key, shape, jnp.float32) * deviation * factor_of
    return jnp.minimum(jnp.maximum(entries, -limit), limit).astype(kind)


def bell_draw_with(key, dims, width, most, shards, heavy, kind=jnp.bfloat16):
    array = width * jax.random.normal(key, dims, jnp.float32)
    if shards:
        array = array * level_of(key, dims, shards, -0.22, 0.18)
    return jnp.clip(with_spikes(array, jax.random.fold_in(key, 3), *heavy), -most, most).astype(kind)


def setup_inputs(seed: int = 0) -> dict:
    seeds = jax.random.split(jax.random.key(seed), 12)
    layer_input = bell_draw_with(seeds[0], (FRAMES, D), 1.0, 6.0, ((0, 32),), (0, 1, 32, 2.75))
    utt_frames = jax.vmap(lambda own: uneven_parts(own, UTT_DEV, ROWS_DEV, UTT_MOST, 2))(jax.random.split(seeds[1], SHARDS)).reshape((SHARDS, UTT_DEV)).astype(jnp.int32)
    w_pointwise1 = bell_draw(seeds[2], (D, 2 * D), D ** -0.5, 0.1875)
    conv_taps = bell_draw(seeds[3], (TAPS, D), TAPS ** -0.5, 2.0)
    conv_scale = jnp.clip(jnp.exp(jax.random.uniform(seeds[4], (D,), jnp.float32, math.log(0.5), math.log(2.0))), 0.5, 2.0)
    conv_shift = jnp.clip(jax.random.uniform(seeds[5], (D,), jnp.float32, -1.0, 1.0), -1.0, 1.0)
    w_pointwise2 = bell_draw(seeds[6], (D, D), D ** -0.5, 0.1875)
    adj_grad = bell_draw(seeds[7], (ADJ, EMB), 1.0, 6.0, ((0, 8), (1, 4)))
    proj_weight = bell_draw(seeds[8], (D, EMB), EMB ** -0.5, 0.0625, ((0, 8), (1, 4)))
    adj_target_keys = jax.random.split(jax.random.fold_in(seeds[9], 1), ADJ // QUARTER)
    adj_target_turns = jax.random.permutation(jax.random.fold_in(seeds[9], 3), ADJ // QUARTER)
    adj_target = jax.vmap(lambda own, number: routed_block(jax.random.fold_in(seeds[9], 2), own, number, QUARTER, REPLICAS, 1, CAP, 2))(adj_target_keys, adj_target_turns).reshape((ADJ, 1))
    adj_frame = with_ends(jax.random.randint(seeds[10], (ADJ,), 0, ROWS_DEV), jax.random.fold_in(seeds[10], 1), 0, ROWS_DEV - 1).astype(jnp.int32)
    return {"layer_input": layer_input, "utt_frames": utt_frames, "w_pointwise1": w_pointwise1, "conv_taps": conv_taps, "conv_scale": conv_scale, "conv_shift": conv_shift, "w_pointwise2": w_pointwise2, "adj_grad": adj_grad, "proj_weight": proj_weight, "adj_target": adj_target, "adj_frame": adj_frame}


def shard_backward(layer_input, lengths, grad_out, w_one, conv_taps, conv_scale, conv_shift, w_two):
    row_count, feat_width = layer_input.shape
    taps_count = conv_taps.shape[0]
    half_span = taps_count // 2
    utt_ends = jnp.cumsum(lengths)
    position = lax.broadcasted_iota(jnp.int32, (row_count, lengths.shape[0]), 0)
    segment = lax.optimization_barrier(jnp.sum((position >= utt_ends[None, :]).astype(jnp.int32), axis=1))
    padded_seg = jnp.pad(segment, (half_span, half_span), constant_values=-1)
    as_float = layer_input.astype(jnp.float32)
    row_mean = lax.optimization_barrier(jnp.mean(as_float, axis=1, keepdims=True))
    centred = as_float - row_mean
    inverse = lax.rsqrt(lax.optimization_barrier(jnp.mean(centred * centred, axis=1, keepdims=True)) + 1e-05)
    standard = centred * inverse
    normed = standard.astype(jnp.bfloat16)
    mixed = jnp.dot(normed, w_one, preferred_element_type=jnp.float32)
    linear = mixed[:, :feat_width]
    gate_prob = jax.nn.sigmoid(mixed[:, feat_width:])
    gated = (linear * gate_prob).astype(jnp.bfloat16)
    padded_gated = jnp.pad(gated, ((half_span, half_span), (0, 0))).astype(jnp.float32)
    tap_values = conv_taps.astype(jnp.float32)
    conv_sum = jnp.zeros((row_count, feat_width), jnp.float32)
    for k in range(taps_count):
        same_utt = padded_seg[k:k + row_count] == segment
        window = jnp.where(same_utt[:, None], padded_gated[k:k + row_count], jnp.float32(0.0))
        conv_sum = conv_sum + tap_values[k] * window
    pre_act = conv_sum * conv_scale + conv_shift
    act_prob = jax.nn.sigmoid(pre_act)
    activated = (pre_act * act_prob).astype(jnp.bfloat16)
    contract_rows = (((0,), (0,)), ((), ()))
    contract_cols = (((1,), (1,)), ((), ()))
    w2_term = lax.dot_general(activated, grad_out, contract_rows, preferred_element_type=jnp.float32)
    grad_act = lax.dot_general(grad_out, w_two, contract_cols, preferred_element_type=jnp.float32)
    grad_conv = grad_act * act_prob * (1.0 + pre_act * (1.0 - act_prob)) * conv_scale
    padded_grad = jnp.pad(grad_conv, ((half_span, half_span), (0, 0)))
    grad_gated = jnp.zeros((row_count, feat_width), jnp.float32)
    columns = []
    for k in range(taps_count):
        same_utt = padded_seg[k:k + row_count] == segment
        window = jnp.where(same_utt[:, None], padded_gated[k:k + row_count], jnp.float32(0.0))
        columns.append(lax.optimization_barrier(jnp.sum(window * grad_conv, axis=0)))
        back_start = 2 * half_span - k
        back_same = padded_seg[back_start:back_start + row_count] == segment
        grad_gated = grad_gated + tap_values[k] * jnp.where(back_same[:, None], padded_grad[back_start:back_start + row_count], jnp.float32(0.0))
    taps_term = jnp.stack(columns, axis=1)
    grad_mixed = jnp.concatenate([grad_gated * gate_prob, grad_gated * linear * gate_prob * (1.0 - gate_prob)], axis=1).astype(jnp.bfloat16)
    w1_term = lax.dot_general(normed, grad_mixed, contract_rows, preferred_element_type=jnp.float32)
    grad_norm = lax.dot_general(grad_mixed, w_one, contract_cols, preferred_element_type=jnp.float32)
    grad_input = inverse * (grad_norm - lax.optimization_barrier(jnp.mean(grad_norm, axis=1, keepdims=True)) - standard * lax.optimization_barrier(jnp.mean(grad_norm * standard, axis=1, keepdims=True)))
    input_grad = (grad_out.astype(jnp.float32) + grad_input).astype(jnp.bfloat16)
    return (input_grad, w1_term, w2_term, taps_term)

def reference(layer_input, utt_frames, w_pointwise1, conv_taps, conv_scale, conv_shift, w_pointwise2, adj_grad, proj_weight, adj_target, adj_frame):
    feat_grad = jnp.dot(adj_grad, proj_weight.T, preferred_element_type=jnp.float32).astype(jnp.bfloat16)
    row_index = jnp.arange(ADJ, dtype=jnp.int32)
    quarter_of = row_index % ADJ_DEV // QUARTER
    frame_target = (adj_target[:, 0] * SECTIONS + quarter_of) * ROWS_DEV + adj_frame
    grad_out = jnp.zeros((FRAMES, D), jnp.float32).at[frame_target].add(feat_grad.astype(jnp.float32)).astype(jnp.bfloat16)
    shard_inputs = layer_input.reshape(SHARDS, ROWS_DEV, D)
    shard_grads = grad_out.reshape(SHARDS, ROWS_DEV, D)

    def advance(totals, pieces):
        shard_x, lengths, shard_g = pieces
        result, w1_term, w2_term, taps_term = shard_backward(shard_x, lengths, shard_g, w_pointwise1, conv_taps, conv_scale, conv_shift, w_pointwise2)
        return ((totals[0] + w1_term, totals[1] + w2_term, totals[2] + taps_term), result)
    initial = (jnp.zeros((D, 2 * D), jnp.float32), jnp.zeros((D, D), jnp.float32), jnp.zeros((D, TAPS), jnp.float32))
    totals_out, results = lax.scan(advance, initial, (shard_inputs, utt_frames, shard_grads))
    return (results.reshape(FRAMES, D), totals_out[0], totals_out[1], totals_out[2])
```

```python
import jax
import jax.numpy as jnp
from jax import lax
from jax.sharding import PartitionSpec as P

BF = jnp.bfloat16
F32 = jnp.float32
ROWS = (((0,), (0,)), ((), ()))
COLS = (((1,), (1,)), ((), ()))


def xor_perm(count, mask):
    return [(i, i ^ mask) for i in range(count)]


def forward_part(layer_input, lengths, w_one, conv_taps, conv_scale, conv_shift):
    row_count, feat_width = layer_input.shape
    taps_count = conv_taps.shape[0]
    half_span = taps_count // 2
    ends = [lengths[0]]
    for j in range(1, lengths.shape[0]):
        ends.append(ends[-1] + lengths[j])
    position = lax.broadcasted_iota(jnp.int32, (row_count,), 0)
    segment = sum((position >= e).astype(jnp.int32) for e in ends)
    padded_seg = jnp.pad(segment, (half_span, half_span), constant_values=-1)
    as_float = layer_input.astype(F32)
    row_mean = jnp.mean(as_float, axis=1, keepdims=True)
    centred = as_float - row_mean
    inverse = lax.rsqrt(jnp.mean(centred * centred, axis=1, keepdims=True) + 1e-05)
    standard = centred * inverse
    normed = standard.astype(BF)
    mixed = jnp.dot(normed, w_one, preferred_element_type=F32)
    linear = mixed[:, :feat_width]
    gate_prob = jax.nn.sigmoid(mixed[:, feat_width:])
    gated = (linear * gate_prob).astype(BF)
    padded_gated = jnp.pad(gated, ((half_span, half_span), (0, 0))).astype(F32)
    tap_values = conv_taps.astype(F32)
    conv_sum = jnp.zeros((row_count, feat_width), F32)
    for k in range(taps_count):
        same_utt = padded_seg[k : k + row_count] == segment
        window = jnp.where(same_utt[:, None], padded_gated[k : k + row_count], 0.0)
        conv_sum = conv_sum + tap_values[k] * window
    pre_act = conv_sum * conv_scale + conv_shift
    act_prob = jax.nn.sigmoid(pre_act)
    activated = (pre_act * act_prob).astype(BF)
    slope = act_prob * (1.0 + pre_act * (1.0 - act_prob)) * conv_scale
    return standard, inverse, normed, linear, gate_prob, padded_gated, padded_seg, segment, activated, slope


def shards(
    layer_input,
    utt_frames,
    w_pointwise1,
    conv_taps,
    conv_scale,
    conv_shift,
    w_pointwise2,
    adj_grad,
    proj_weight,
    adj_target,
    adj_frame,
):
    reps = lax.axis_size("rep")
    sections = lax.axis_size("section")
    rep_here = lax.axis_index("rep")
    sec_here = lax.axis_index("section")
    block_rows = adj_grad.shape[0]
    quarter = block_rows // sections
    frame_rows, feat = layer_input.shape
    taps_count = conv_taps.shape[0]
    half_span = taps_count // 2
    capacity = max(2, 2 * quarter // reps)
    outer = reps // 2
    pair_here = rep_here % 2
    outer_here = rep_here // 2
    piece = proj_weight.shape[0]

    adj_other = lax.ppermute(adj_grad, "rep", xor_perm(reps, 1))
    blocks = [proj_weight]
    for k in range(1, outer):
        blocks.append(
            lax.ppermute(
                proj_weight,
                "rep",
                [(i, ((i // 2 + k) % outer) * 2 + i % 2) for i in range(reps)],
            )
        )

    targets = adj_target[:, 0].reshape(reps, sections, quarter)
    frames = adj_frame.reshape(reps, sections, quarter)
    sec_targets = lax.dynamic_index_in_dim(targets, sec_here, 1, keepdims=False)
    sec_frames = lax.dynamic_index_in_dim(frames, sec_here, 1, keepdims=False)
    row_a = lax.broadcasted_iota(jnp.int32, (quarter, quarter), 0)
    row_b = lax.broadcasted_iota(jnp.int32, (quarter, quarter), 1)
    same = (sec_targets[:, :, None] == sec_targets[:, None, :]) & (row_b < row_a)[None]
    rank = jnp.sum(same.astype(jnp.int32), axis=2)
    mine = sec_targets == rep_here
    slots = lax.broadcasted_iota(jnp.int32, (1, capacity, 1), 1)
    hit = mine[:, None, :] & (rank[:, None, :] == slots)
    slot_frames = jnp.sum(jnp.where(hit, sec_frames[:, None, :] + 1, 0), axis=2) - 1

    def packing(block):
        tgt = lax.dynamic_index_in_dim(sec_targets, block, 0, keepdims=False)
        rnk = lax.dynamic_index_in_dim(rank, block, 0, keepdims=False)
        slot_of = tgt * capacity + rnk
        ids = lax.broadcasted_iota(jnp.int32, (reps * capacity, quarter), 0)
        return (slot_of[None, :] == ids).astype(BF)

    pack_own = packing(rep_here)
    pack_other = packing(jnp.bitwise_xor(rep_here, 1))

    standard, inverse, normed, linear, gate_prob, padded_gated, padded_seg, segment, activated, slope = forward_part(
        layer_input, utt_frames[0], w_pointwise1, conv_taps, conv_scale, conv_shift
    )
    part_rows = feat // (reps * sections)

    def by_section(values):
        return values.reshape(frame_rows, reps, sections, part_rows).transpose(2, 0, 1, 3).reshape(
            sections, frame_rows, reps * part_rows
        )

    early = jnp.concatenate([by_section(normed), by_section(activated)], axis=2)
    early_parts = []
    for k in range(sections):
        piece_k = lax.dynamic_index_in_dim(early, jnp.bitwise_xor(sec_here, k), 0, keepdims=False)
        early_parts.append(lax.ppermute(piece_k, "section", xor_perm(sections, k)) if k else piece_k)

    partial = []
    for k in range(outer):
        own = lax.dot_general(adj_grad, blocks[k], COLS, preferred_element_type=F32)
        other = lax.dot_general(adj_other, blocks[k], COLS, preferred_element_type=F32)
        partial.append(jnp.stack([own, other]).astype(BF))
    partial = jnp.stack(partial, axis=2)
    partial = partial.reshape(2, sections, quarter, outer * piece).transpose(1, 0, 2, 3)
    arrived = lax.all_to_all(partial, "section", split_axis=0, concat_axis=0, tiled=True)
    feat_grad = jnp.sum(arrived.astype(F32), axis=0).astype(BF)
    packed = jnp.stack(
        [
            jnp.dot(pack_own, feat_grad[0], preferred_element_type=F32).astype(BF),
            jnp.dot(pack_other, feat_grad[1], preferred_element_type=F32).astype(BF),
        ]
    )
    packed = packed.reshape(2, reps, capacity, outer, piece)
    packed = jnp.concatenate([packed[:, :, :, :1], packed[:, :, :, :0:-1]], axis=3)
    packed = jnp.roll(packed, outer_here, axis=3)
    outgoing = packed.transpose(1, 0, 2, 3, 4).reshape(reps, 2 * capacity, outer * piece)
    incoming = lax.all_to_all(outgoing, "rep", split_axis=0, concat_axis=0, tiled=True)
    incoming = incoming.reshape(outer, 2, 2 * capacity, outer * piece)
    slot_frames = slot_frames.reshape(outer, 2, capacity)
    frame_ids = lax.broadcasted_iota(jnp.int32, (frame_rows, outer * 2 * capacity), 0)
    halves = []
    for p in range(2):
        order = jnp.stack([slot_frames[:, p], slot_frames[:, 1 - p]], axis=1).reshape(1, -1)
        pick = (frame_ids == order).astype(BF)
        halves.append(
            jnp.dot(pick, incoming[:, p].reshape(-1, outer * piece), preferred_element_type=F32)
            .astype(BF)
            .reshape(frame_rows, outer, piece)
        )
    grad_out = jnp.stack(halves, axis=2).reshape(frame_rows, feat)

    def gather(values):
        from_two = lax.ppermute(values, "section", xor_perm(sections, 2))
        from_one = lax.ppermute(values, "section", xor_perm(sections, 1))
        from_three = lax.ppermute(from_two, "section", xor_perm(sections, 1))
        return [values, from_one, from_two, from_three]

    grad_out_all = gather(grad_out)

    grad_act = lax.dot_general(grad_out, w_pointwise2, COLS, preferred_element_type=F32)
    grad_conv = grad_act * slope
    padded_grad = jnp.pad(grad_conv, ((half_span, half_span), (0, 0)))
    grad_gated = jnp.zeros((frame_rows, feat), F32)
    tap_values = conv_taps.astype(F32)
    columns = []
    for k in range(taps_count):
        same_utt = padded_seg[k : k + frame_rows] == segment
        window = jnp.where(same_utt[:, None], padded_gated[k : k + frame_rows], 0.0)
        columns.append(jnp.sum(window * grad_conv, axis=0))
        back = 2 * half_span - k
        back_same = padded_seg[back : back + frame_rows] == segment
        grad_gated = grad_gated + tap_values[k] * jnp.where(
            back_same[:, None], padded_grad[back : back + frame_rows], 0.0
        )
    taps_rows = 16
    taps_term = jnp.pad(jnp.stack(columns, axis=0), ((0, taps_rows - taps_count), (0, 0))).astype(BF)
    first = grad_gated * gate_prob
    grad_mixed = jnp.concatenate([first, first * linear * (1.0 - gate_prob)], axis=1).astype(BF)
    late = jnp.concatenate([grad_mixed, jnp.pad(taps_term.reshape(taps_rows // 2, 2 * feat), ((0, 8), (0, 0)))], axis=0)
    late_all = gather(late)

    w1_part = sum(
        lax.dot_general(e[:, : reps * part_rows], g[:frame_rows], ROWS, preferred_element_type=F32)
        for e, g in zip(early_parts, late_all)
    )
    w2_part = sum(
        lax.dot_general(e[:, reps * part_rows :], g, ROWS, preferred_element_type=F32)
        for e, g in zip(early_parts, grad_out_all)
    )
    taps_sum = sum(g[frame_rows : frame_rows + taps_rows // 2].astype(F32) for g in late_all).reshape(taps_rows, feat)
    taps_sum = lax.dynamic_index_in_dim(
        taps_sum.reshape(taps_rows, reps, sections, part_rows), sec_here, 2, keepdims=False
    )
    taps_part = jnp.pad(
        taps_sum.transpose(1, 2, 0).reshape(reps * part_rows, taps_rows), ((0, 0), (0, 128 - taps_rows))
    )
    parts = jnp.concatenate([w1_part, w2_part, taps_part], axis=1).astype(BF)
    width = parts.shape[1]
    swapped = lax.all_to_all(
        parts.reshape(reps, part_rows, width), "rep", split_axis=0, concat_axis=0, tiled=True
    )
    total = jnp.sum(swapped.astype(F32), axis=0)

    grad_norm = lax.dot_general(grad_mixed, w_pointwise1, COLS, preferred_element_type=F32)
    grad_input = inverse * (
        grad_norm
        - jnp.mean(grad_norm, axis=1, keepdims=True)
        - standard * jnp.mean(grad_norm * standard, axis=1, keepdims=True)
    )
    input_grad = (grad_out.astype(F32) + grad_input).astype(BF)
    return (
        input_grad,
        total[:, : 2 * feat],
        total[:, 2 * feat : 3 * feat],
        total[:, 3 * feat : 3 * feat + taps_count],
    )


def solution(mesh):
    spread = P(("rep", "section"), None)
    return jax.shard_map(
        shards,
        mesh=mesh,
        in_specs=(spread, spread, P(), P(), P(), P(), P(), P("rep", "section"), P("rep", "section"), P(), P()),
        out_specs=(spread, spread, spread, spread),
        check_vma=False,
    )
```

```python
import jax
import jax.numpy as jnp
from jax import lax
from jax.experimental import pallas as pl
from jax.experimental.pallas import tpu as pltpu
from jax.sharding import PartitionSpec as P

BF = jnp.bfloat16
F32 = jnp.float32
ROWS = (((0,), (0,)), ((), ()))
COLS = (((1,), (1,)), ((), ()))


def xor_perm(count, mask):
    return [(i, i ^ mask) for i in range(count)]


def size_of(axis):
    if isinstance(axis, tuple):
        return lax.axis_size(axis[0]) * lax.axis_size(axis[1])
    return lax.axis_size(axis)


def swap(axis, values, mask):
    return lax.ppermute(values, axis, xor_perm(size_of(axis), mask))


def xor_order(items, place):
    step = 1
    while step < len(items):
        flip = jnp.bitwise_and(place, step) > 0
        items = [jnp.where(flip, items[i ^ step], items[i]) for i in range(len(items))]
        step *= 2
    return items


def local_call(body, ids, operands, outs, scratch=(), flops=0, name=None):
    moved = sum(o.size * o.dtype.itemsize for o in operands) + sum(
        o.size * o.dtype.itemsize for o in outs
    )
    return pl.pallas_call(
        body,
        out_shape=tuple(outs),
        in_specs=[pl.BlockSpec(memory_space=pltpu.SMEM)] + [pl.BlockSpec(memory_space=pltpu.VMEM)] * len(operands),
        out_specs=tuple(pl.BlockSpec(memory_space=pltpu.VMEM) for _ in outs),
        scratch_shapes=list(scratch),
        compiler_params=pltpu.CompilerParams(vmem_limit_bytes=24 * 1024 * 1024),
        cost_estimate=pl.CostEstimate(flops=flops, bytes_accessed=moved, transcendentals=0),
        name=name,
    )(ids, *operands)


def like(shape, dtype):
    return jax.ShapeDtypeStruct(shape, dtype)


def aligned(index, size):
    return pl.ds(pl.multiple_of(index * size, size), size)


def forward_kernel(
    ids, x, w_one, taps, scale, shift,
    standard, inverse, linear, gate_prob, gated, slope, masks, mine, theirs, wide, flipped,
):
    core = ids[3]
    frame_rows, feat = x.shape
    taps_count = taps.shape[0]
    half = taps_count // 2
    utterances = ids.shape[0] - 4
    ends = [ids[4]]
    for u in range(1, utterances):
        ends.append(ends[-1] + ids[4 + u])
    position = lax.broadcasted_iota(jnp.int32, (frame_rows, 128), 0)

    def segment(at):
        return sum(jnp.where(at >= e, 1, 0) for e in ends)

    here = segment(position)
    for k in range(taps_count):
        at = position + (k - half)
        good = (segment(at) == here) & (at >= 0) & (at < frame_rows)
        masks[k] = jnp.where(good, 1.0, 0.0)
    as_float = x[...].astype(F32)
    centred = as_float - jnp.mean(as_float, axis=1, keepdims=True)
    inv = lax.rsqrt(jnp.mean(centred * centred, axis=1, keepdims=True) + 1e-05)
    inverse[...] = jnp.broadcast_to(inv, inverse.shape)
    standard[...] = centred * inv
    normed = standard[...].astype(BF)
    edge = jnp.zeros((8, feat), F32)
    wide[0:8, :] = edge
    wide[8 + frame_rows : 16 + frame_rows, :] = edge
    step = 256
    for c in range(feat // step):
        cols = slice(c * step, (c + 1) * step)
        lin = jnp.dot(normed, w_one[:, cols], preferred_element_type=F32)
        gate = jax.nn.sigmoid(
            jnp.dot(normed, w_one[:, feat + c * step : feat + (c + 1) * step], preferred_element_type=F32)
        )
        linear[:, cols] = lin
        gate_prob[:, cols] = gate
        product = (lin * gate).astype(BF)
        gated[:, cols] = product
        wide[8 : 8 + frame_rows, cols] = product.astype(F32)
    for c in range(feat // 128):
        cols = slice(c * 128, (c + 1) * 128)
        total = jnp.zeros((frame_rows, 128), F32)
        for k in range(taps_count):
            start = 8 + k - half
            total = total + taps[k : k + 1, cols] * (wide[start : start + frame_rows, cols] * masks[k])
        pre = total * scale[:, cols] + shift[:, cols]
        prob = jax.nn.sigmoid(pre)
        slope[:, cols] = prob * (1.0 + pre * (1.0 - prob)) * scale[:, cols]
        flipped[0, cols, :] = normed[:, cols].astype(F32).T
        flipped[1, cols, :] = (pre * prob).astype(BF).astype(F32).T
    groups = mine.shape[0] // feat * 16
    part = feat // (2 * groups)
    for h in range(2):
        for g in range(groups):
            at = slice(h * (feat // 2) + g * part, h * (feat // 2) + (g + 1) * part)
            mine[at, :] = flipped[h, aligned(2 * g + core, part), :].astype(BF)
            theirs[at, :] = flipped[h, aligned(2 * g + 1 - core, part), :].astype(BF)


def partial_kernel(ids, *refs):
    own_rows, other_rows, *blocks = refs[:-5]
    outs, rows = refs[-5:-1], refs[-1]
    sec, z = ids[0], ids[1]
    quarter = outs[0].shape[0] // 2
    piece = blocks[0].shape[0]
    if len(blocks) == 2:
        middle = (z == 1) | (z == 2)
        lots = [jnp.where(middle, blocks[0][...], blocks[1][...])]
    else:
        lots = [jnp.concatenate([blocks[0][...], blocks[1][...]], axis=0), blocks[2][...]]
    first = 0
    for lot in lots:
        last = first + lot.shape[0]
        for w, a in enumerate((own_rows, other_rows)):
            rows[w, :, first:last] = lax.dot_general(a[...], lot, COLS, preferred_element_type=F32)
        first = last
    for m, out in enumerate(outs):
        q = jnp.bitwise_xor(sec, m)
        for w in range(2):
            out[w * quarter : (w + 1) * quarter, :] = rows[w, aligned(q, quarter), :].astype(out.dtype)


def packing_kernel(ids, own, r1, r2, r3, own_last, l1, l2, l3, pack, out):
    total = own[...] + r1[...].astype(F32) + r2[...].astype(F32) + r3[...].astype(F32)
    last = own_last[...] + l1[...].astype(F32) + l2[...].astype(F32) + l3[...].astype(F32)
    piece = last.shape[1]
    parts = xor_order([total[:, k * piece : (k + 1) * piece] for k in range(3)] + [last], ids[1])
    rows = jnp.concatenate(parts, axis=1).astype(BF)
    out[...] = jnp.dot(pack[...], rows, preferred_element_type=F32).astype(BF)


def module_kernel(
    ids, incoming, order, w_two, slope, gated, masks, gate_prob, linear, taps, halves,
    grad_out, grad_mixed, p0, p2, p4, p6, wide_gated, wide_grad,
):
    place = ids[2]
    frame_rows, feat = grad_out.shape
    taps_count = taps.shape[0]
    half = taps_count // 2
    sources, slots, width = incoming.shape
    outer = sources // 2
    piece = width // outer
    frame_ids = lax.broadcasted_iota(jnp.int32, (frame_rows, outer * slots), 0)
    for p in range(2):
        pick = (frame_ids == order[p : p + 1, :]).astype(F32).astype(BF)
        rows = jnp.concatenate([incoming[2 * o + p] for o in range(outer)], axis=0)
        got = jnp.dot(pick, rows, preferred_element_type=F32).astype(BF)
        for o in range(outer):
            first = (2 * o + p) * piece
            grad_out[:, first : first + piece] = got[:, o * piece : (o + 1) * piece]
    edge = jnp.zeros((8, feat), F32)
    for wide in (wide_gated, wide_grad):
        wide[0:8, :] = edge
        wide[8 + frame_rows : 16 + frame_rows, :] = edge
    wide_gated[8 : 8 + frame_rows, :] = gated[...].astype(F32)
    grad_act = lax.dot_general(grad_out[...], w_two[...], COLS, preferred_element_type=F32)
    wide_grad[8 : 8 + frame_rows, :] = grad_act * slope[...]
    step = 128
    tap_rows = []
    for c in range(feat // step):
        cols = slice(c * step, (c + 1) * step)
        grad_conv = wide_grad[8 : 8 + frame_rows, cols]
        total = jnp.zeros((frame_rows, step), F32)
        columns = []
        for k in range(taps_count):
            start = 8 + k - half
            window = wide_gated[start : start + frame_rows, cols] * masks[k]
            columns.append(jnp.sum(window * grad_conv, axis=0, keepdims=True))
            start = 8 + half - k
            back = 2 * half - k
            total = total + taps[k : k + 1, cols] * (
                wide_grad[start : start + frame_rows, cols] * masks[back]
            )
        tap_rows.append(jnp.concatenate(columns + [jnp.zeros((16 - taps_count, step), F32)], axis=0))
        gate = gate_prob[:, cols]
        first = total * gate
        grad_mixed[:, c * step : (c + 1) * step] = first.astype(BF)
        grad_mixed[:, feat + c * step : feat + (c + 1) * step] = (first * linear[:, cols] * (1.0 - gate)).astype(BF)
    tap_rows = jnp.concatenate(tap_rows, axis=1).astype(BF)
    tap_halves = jnp.dot(tap_rows, halves[...], preferred_element_type=F32)
    tap_halves = tap_halves.astype(BF)
    w1_cols, w2_cols = feat // 2, feat // 4
    for mask, out in enumerate((p0, p2, p4, p6)):
        q = jnp.bitwise_xor(place, mask)
        out[0:frame_rows, 0:w1_cols] = grad_mixed[:, aligned(q, w1_cols)]
        out[0:frame_rows, w1_cols:] = grad_out[:, aligned(q, w2_cols)]
        for h in range(2):
            tap_at = slice(frame_rows + 16 * h, frame_rows + 16 * (h + 1))
            out[tap_at, 0:w1_cols] = tap_halves[:, h * w1_cols : (h + 1) * w1_cols]
            out[tap_at, w1_cols:] = jnp.zeros((16, w2_cols), BF)


def weights_kernel(ids, e0, e1, e2, e3, e4, e5, e6, e7, g0, g1, g2, g3, g4, g5, g6, g7, own, s1, s2, s3, rows, tap_sum):
    z, core = ids[1], ids[3]
    frame_rows = e0.shape[1]
    half = e0.shape[0] // 2
    w1_cols = half
    tap_sum[...] = sum(
        g[aligned(core + frame_rows // 16, 16), 0:w1_cols].astype(F32) for g in (g0, g1, g2, g3, g4, g5, g6, g7))
    pairs = ((e0, e1, g0, g1), (e2, e3, g2, g3), (e4, e5, g4, g5), (e6, e7, g6, g7))
    for cols, first in ((slice(0, w1_cols), 0), (slice(w1_cols, g0.shape[1]), half)):
        total = None
        for ea, eb, ga, gb in pairs:
            both = jnp.concatenate([ga[0:frame_rows, cols], gb[0:frame_rows, cols]], axis=0)
            feats = jnp.concatenate([ea[first : first + half, :], eb[first : first + half, :]], axis=1)
            term = jnp.dot(feats, both, preferred_element_type=F32)
            total = term if total is None else total + term
        rows[:, cols] = total
    block = half // 4
    for m, out in enumerate((own, s1, s2, s3)):
        o = jnp.bitwise_xor(z, m)
        out[0:block, :] = rows[aligned(o, block), :].astype(out.dtype)
        out[block:, 0:block] = tap_sum[:, aligned(o, block)].astype(out.dtype)
        out[block:, block:] = jnp.zeros((out.shape[0] - block, out.shape[1] - block), out.dtype)


def sum_kernel(ids, own, r1, r2, r3, mine, f1, f2, f3, taps, rows):
    place = ids[2]
    block = taps.shape[1]
    rows[...] = own[...] + r1[...].astype(F32) + r2[...].astype(F32) + r3[...].astype(F32)
    part = block // 4
    for m, out in enumerate((mine, f1, f2, f3)):
        out[...] = rows[aligned(jnp.bitwise_xor(place, m), part), :].astype(out.dtype)
    taps[...] = rows[block:, 0:block]


def assembly_kernel(ids, mine, r1, r2, r3, w1, w2):
    place = ids[2]
    w1_cols, w2_cols = w1.shape[1] // 4, w2.shape[1] // 4
    for m, part in enumerate((mine, r1, r2, r3)):
        q = jnp.bitwise_xor(place, m)
        w1[:, aligned(q, w1_cols)] = part[:, 0:w1_cols].astype(F32)
        w2[:, aligned(q, w2_cols)] = part[:, w1_cols:].astype(F32)


def forward_part(layer_input, lengths, w_one, conv_taps, conv_scale, conv_shift):
    row_count, feat_width = layer_input.shape
    taps_count = conv_taps.shape[0]
    half_span = taps_count // 2
    ends = [lengths[0]]
    for j in range(1, lengths.shape[0]):
        ends.append(ends[-1] + lengths[j])
    position = lax.broadcasted_iota(jnp.int32, (row_count,), 0)
    segment = sum((position >= e).astype(jnp.int32) for e in ends)
    padded_seg = jnp.pad(segment, (half_span, half_span), constant_values=-1)
    as_float = layer_input.astype(F32)
    row_mean = jnp.mean(as_float, axis=1, keepdims=True)
    centred = as_float - row_mean
    inverse = lax.rsqrt(jnp.mean(centred * centred, axis=1, keepdims=True) + 1e-05)
    standard = centred * inverse
    normed = standard.astype(BF)
    mixed = jnp.dot(normed, w_one, preferred_element_type=F32)
    linear = mixed[:, :feat_width]
    gate_prob = jax.nn.sigmoid(mixed[:, feat_width:])
    gated = (linear * gate_prob).astype(BF)
    padded_gated = jnp.pad(gated, ((half_span, half_span), (0, 0))).astype(F32)
    tap_values = conv_taps.astype(F32)
    conv_sum = jnp.zeros((row_count, feat_width), F32)
    for k in range(taps_count):
        same_utt = padded_seg[k : k + row_count] == segment
        window = jnp.where(same_utt[:, None], padded_gated[k : k + row_count], 0.0)
        conv_sum = conv_sum + tap_values[k] * window
    pre_act = conv_sum * conv_scale + conv_shift
    act_prob = jax.nn.sigmoid(pre_act)
    activated = (pre_act * act_prob).astype(BF)
    slope = act_prob * (1.0 + pre_act * (1.0 - act_prob)) * conv_scale
    return standard, inverse, normed, linear, gate_prob, padded_gated, padded_seg, segment, activated, slope


def plain_shards(
    layer_input,
    utt_frames,
    w_pointwise1,
    conv_taps,
    conv_scale,
    conv_shift,
    w_pointwise2,
    adj_grad,
    proj_weight,
    adj_target,
    adj_frame,
):
    reps = lax.axis_size("rep")
    sections = lax.axis_size("section")
    rep_here = lax.axis_index("rep")
    sec_here = lax.axis_index("section")
    block_rows = adj_grad.shape[0]
    quarter = block_rows // sections
    frame_rows, feat = layer_input.shape
    taps_count = conv_taps.shape[0]
    half_span = taps_count // 2
    capacity = max(2, 2 * quarter // reps)
    outer = reps // 2
    pair_here = rep_here % 2
    outer_here = rep_here // 2
    piece = proj_weight.shape[0]

    adj_other = swap("rep", adj_grad, 1)
    blocks = [proj_weight] + [swap("rep", proj_weight, 2 * k) for k in range(1, outer)]

    targets = adj_target[:, 0].reshape(reps, sections, quarter)
    frames = adj_frame.reshape(reps, sections, quarter)
    sec_targets = lax.dynamic_index_in_dim(targets, sec_here, 1, keepdims=False)
    sec_frames = lax.dynamic_index_in_dim(frames, sec_here, 1, keepdims=False)
    row_a = lax.broadcasted_iota(jnp.int32, (quarter, quarter), 0)
    row_b = lax.broadcasted_iota(jnp.int32, (quarter, quarter), 1)
    same = (sec_targets[:, :, None] == sec_targets[:, None, :]) & (row_b < row_a)[None]
    rank = jnp.sum(same.astype(jnp.int32), axis=2)
    mine = sec_targets == rep_here
    slots = lax.broadcasted_iota(jnp.int32, (1, capacity, 1), 1)
    hit = mine[:, None, :] & (rank[:, None, :] == slots)
    slot_frames = jnp.sum(jnp.where(hit, sec_frames[:, None, :] + 1, 0), axis=2) - 1

    pair_blocks = jnp.stack([rep_here, jnp.bitwise_xor(rep_here, 1)])
    pair_targets = jnp.concatenate([lax.dynamic_index_in_dim(sec_targets, pair_blocks[w], 0, keepdims=False) for w in range(2)])
    pair_rank = jnp.concatenate([lax.dynamic_index_in_dim(rank, pair_blocks[w], 0, keepdims=False) for w in range(2)])
    member = lax.broadcasted_iota(jnp.int32, (2 * quarter,), 0) // quarter
    slot_of = (pair_targets * 2 + member) * capacity + pair_rank
    slot_ids = lax.broadcasted_iota(jnp.int32, (reps * 2 * capacity, 2 * quarter), 0)
    pack = (slot_of[None, :] == slot_ids).astype(BF)

    standard, inverse, normed, linear, gate_prob, padded_gated, padded_seg, segment, activated, slope = forward_part(
        layer_input, utt_frames[0], w_pointwise1, conv_taps, conv_scale, conv_shift
    )
    part_rows = feat // (reps * sections)

    here = rep_here * sections + sec_here
    core = here % 2
    place = (here // 2) % 4
    BOTH = ("rep", "section")

    def core_halves(values):
        return values.reshape(frame_rows, reps * sections // 2, 2, part_rows).transpose(2, 0, 1, 3).reshape(
            2, frame_rows, feat // 2
        )

    halves = jnp.concatenate([core_halves(normed), core_halves(activated)], axis=2)
    mine_half = lax.dynamic_index_in_dim(halves, core, 0, keepdims=False)
    their_half = lax.dynamic_index_in_dim(halves, 1 - core, 0, keepdims=False)
    chip_half = jnp.concatenate([mine_half, swap(BOTH, their_half, 1)], axis=0)
    early = {0: chip_half}
    for m in (2, 4, 6):
        early[m] = swap(BOTH, chip_half, m)
    near = early[0]
    straight = jnp.concatenate([early[m][:frame_rows] for m in (2, 4, 6)], axis=0)
    across = jnp.concatenate([early[m][frame_rows:] for m in (2, 4, 6)], axis=0)

    adj_pair = jnp.concatenate([adj_grad, adj_other], axis=0)

    def section_sum(lot):
        terms = [lax.dot_general(adj_pair, b, COLS, preferred_element_type=F32).astype(BF) for b in lot]
        terms = jnp.concatenate(terms, axis=1).reshape(2, sections, quarter, len(lot) * piece)
        total = lax.dynamic_index_in_dim(terms, sec_here, 1, keepdims=False).astype(F32)
        for m in range(1, sections):
            given = lax.dynamic_index_in_dim(terms, jnp.bitwise_xor(sec_here, m), 1, keepdims=False)
            total = total + swap("section", given, m).astype(F32)
        total = total.astype(BF).reshape(2 * quarter, len(lot) * piece)
        return [total[:, i * piece : (i + 1) * piece] for i in range(len(lot))]

    feat_grad = section_sum(blocks[:-1]) + section_sum(blocks[-1:])
    feat_grad = jnp.concatenate(xor_order(feat_grad, outer_here), axis=1)
    packed = jnp.dot(pack, feat_grad, preferred_element_type=F32).astype(BF)
    outgoing = packed.reshape(reps, 2 * capacity, outer * piece)
    incoming = lax.all_to_all(outgoing, "rep", split_axis=0, concat_axis=0, tiled=True)
    incoming = incoming.reshape(outer, 2, 2 * capacity, outer * piece)
    slot_frames = slot_frames.reshape(outer, 2, capacity)
    frame_ids = lax.broadcasted_iota(jnp.int32, (frame_rows, outer * 2 * capacity), 0)
    out_halves = []
    for p in range(2):
        order = jnp.stack([slot_frames[:, p], slot_frames[:, 1 - p]], axis=1).reshape(1, -1)
        pick = (frame_ids == order).astype(BF)
        out_halves.append(
            jnp.dot(pick, incoming[:, p].reshape(-1, outer * piece), preferred_element_type=F32)
            .astype(BF)
            .reshape(frame_rows, outer, piece)
        )
    grad_out = jnp.stack(out_halves, axis=2).reshape(frame_rows, feat)

    def weight_grad(first_col, values):
        width = values.shape[1] // 4
        lots = [values[:, q * width : (q + 1) * width] for q in range(4)]
        lots = xor_order(lots, place)
        got = {0: lots[0]}
        for m in (2, 4, 6):
            got[m] = swap(BOTH, lots[m // 2], m)
        for m in (0, 2, 4, 6):
            got[m + 1] = swap(BOTH, got[m], 1)
        cols = slice(first_col, first_col + feat // 2)
        part = lax.dot_general(near[:, cols], jnp.concatenate([got[0], got[1]]), ROWS, preferred_element_type=F32)
        part += lax.dot_general(
            straight[:, cols], jnp.concatenate([got[m] for m in (2, 4, 6)]), ROWS, preferred_element_type=F32
        )
        part += lax.dot_general(
            across[:, cols], jnp.concatenate([got[m] for m in (3, 5, 7)]), ROWS, preferred_element_type=F32
        )
        part = part.reshape(outer, 4 * part_rows, width)
        total = lax.dynamic_index_in_dim(part, outer_here, 0, keepdims=False)
        sent = part.astype(BF)
        for m in range(1, outer):
            given = lax.dynamic_index_in_dim(sent, jnp.bitwise_xor(outer_here, m), 0, keepdims=False)
            total = total + swap(BOTH, given, 8 * m).astype(F32)
        total = total.astype(BF)
        lots = xor_order([total[q * part_rows : (q + 1) * part_rows] for q in range(4)], place)
        lots = [lots[0]] + [swap(BOTH, lots[m], 2 * m) for m in (1, 2, 3)]
        return jnp.concatenate(xor_order(lots, place), axis=1).astype(F32)

    w2_grad = weight_grad(feat // 2, grad_out)

    grad_act = lax.dot_general(grad_out, w_pointwise2, COLS, preferred_element_type=F32)
    grad_conv = grad_act * slope
    padded_grad = jnp.pad(grad_conv, ((half_span, half_span), (0, 0)))
    grad_gated = jnp.zeros((frame_rows, feat), F32)
    tap_values = conv_taps.astype(F32)
    columns = []
    for k in range(taps_count):
        same_utt = padded_seg[k : k + frame_rows] == segment
        window = jnp.where(same_utt[:, None], padded_gated[k : k + frame_rows], 0.0)
        columns.append(jnp.sum(window * grad_conv, axis=0))
        back = 2 * half_span - k
        back_same = padded_seg[back : back + frame_rows] == segment
        grad_gated = grad_gated + tap_values[k] * jnp.where(
            back_same[:, None], padded_grad[back : back + frame_rows], 0.0
        )
    first = grad_gated * gate_prob
    grad_mixed = jnp.concatenate([first, first * linear * (1.0 - gate_prob)], axis=1).astype(BF)
    w1_grad = weight_grad(0, grad_mixed)
    taps_term = jnp.stack(columns, axis=0).reshape(taps_count, reps * sections, part_rows)
    taps_term = jnp.pad(taps_term.transpose(1, 0, 2), ((0, 0), (0, 16 - taps_count), (0, 0))).astype(BF)
    taps_all = lax.all_to_all(taps_term, BOTH, split_axis=0, concat_axis=0, tiled=True)
    taps_grad = jnp.sum(taps_all.astype(F32), axis=0)[:taps_count].T

    grad_norm = lax.dot_general(grad_mixed, w_pointwise1, COLS, preferred_element_type=F32)
    grad_input = inverse * (
        grad_norm
        - jnp.mean(grad_norm, axis=1, keepdims=True)
        - standard * jnp.mean(grad_norm * standard, axis=1, keepdims=True)
    )
    input_grad = (grad_out.astype(F32) + grad_input).astype(BF)
    return input_grad, w1_grad, w2_grad, taps_grad


def line_shards(
    layer_input,
    utt_frames,
    w_pointwise1,
    conv_taps,
    conv_scale,
    conv_shift,
    w_pointwise2,
    adj_grad,
    proj_weight,
    adj_target,
    adj_frame,
):
    reps = lax.axis_size("rep")
    sections = lax.axis_size("section")
    rep_here = lax.axis_index("rep")
    sec_here = lax.axis_index("section")
    block_rows = adj_grad.shape[0]
    quarter = block_rows // sections
    frame_rows, feat = layer_input.shape
    taps_count = conv_taps.shape[0]
    half_span = taps_count // 2
    capacity = max(2, 2 * quarter // reps)
    outer = reps // 2
    pair_here = rep_here % 2
    outer_here = rep_here // 2
    piece = proj_weight.shape[0]

    two = swap("rep", proj_weight, 4)
    one = swap("rep", proj_weight, 2)
    adj_other = swap("rep", adj_grad, 1)
    proj_again, two = lax.optimization_barrier((proj_weight, two))
    inner = lax.ppermute(proj_again, "rep", [(o * 2 + p, (3 - o) * 2 + p) for o in (1, 2) for p in (0, 1)])
    ends = lax.ppermute(two, "rep", [(o * 2 + p, (o ^ 1) * 2 + p) for o in (1, 2) for p in (0, 1)])

    targets = adj_target[:, 0].reshape(reps, sections, quarter)
    frames = adj_frame.reshape(reps, sections, quarter)
    sec_targets = lax.dynamic_index_in_dim(targets, sec_here, 1, keepdims=False)
    sec_frames = lax.dynamic_index_in_dim(frames, sec_here, 1, keepdims=False)
    row_a = lax.broadcasted_iota(jnp.int32, (quarter, quarter), 0)
    row_b = lax.broadcasted_iota(jnp.int32, (quarter, quarter), 1)
    same = (sec_targets[:, :, None] == sec_targets[:, None, :]) & (row_b < row_a)[None]
    rank = jnp.sum(same.astype(jnp.int32), axis=2)
    mine = sec_targets == rep_here
    slots = lax.broadcasted_iota(jnp.int32, (1, capacity, 1), 1)
    hit = mine[:, None, :] & (rank[:, None, :] == slots)
    slot_frames = jnp.sum(jnp.where(hit, sec_frames[:, None, :] + 1, 0), axis=2) - 1

    pair_blocks = jnp.stack([rep_here, jnp.bitwise_xor(rep_here, 1)])
    pair_targets = jnp.concatenate([lax.dynamic_index_in_dim(sec_targets, pair_blocks[w], 0, keepdims=False) for w in range(2)])
    pair_rank = jnp.concatenate([lax.dynamic_index_in_dim(rank, pair_blocks[w], 0, keepdims=False) for w in range(2)])
    member = lax.broadcasted_iota(jnp.int32, (2 * quarter,), 0) // quarter
    slot_of = (pair_targets * 2 + member) * capacity + pair_rank
    slot_ids = lax.broadcasted_iota(jnp.int32, (reps * 2 * capacity, 2 * quarter), 0)
    pack = (slot_of[None, :] == slot_ids).astype(BF)

    part_rows = feat // (reps * sections)

    here = rep_here * sections + sec_here
    core = here % 2
    place = (here // 2) % 4
    BOTH = ("rep", "section")

    ids = jnp.stack([sec_here, outer_here, place, core]).astype(jnp.int32)
    ids = jnp.concatenate([ids, utt_frames[0]])
    tap_values = conv_taps.astype(F32)
    square = like((frame_rows, feat), F32)
    half_t = like((feat, frame_rows), BF)
    standard, inverse, linear, gate_prob, gated, slope, masks, mine_half, their_half = local_call(
        forward_kernel,
        ids,
        (layer_input, w_pointwise1, tap_values, conv_scale.reshape(1, -1), conv_shift.reshape(1, -1)),
        [square, like((frame_rows, 128), F32), square, square, like((frame_rows, feat), BF), square]
        + [like((taps_count, frame_rows, 128), F32), half_t, half_t],
        [pltpu.VMEM((frame_rows + 16, feat), F32), pltpu.VMEM((2, feat, frame_rows), F32)],
        flops=4 * frame_rows * feat * feat,
        name="forward",
    )
    inverse = inverse[:, :1]
    early = [mine_half] + [swap(BOTH, their_half if m % 2 else mine_half, m) for m in range(1, 8)]

    rows = 2 * quarter

    def products(name, *lot):
        cols = piece * (3 if len(lot) == 3 else 1)
        sums = local_call(
            partial_kernel,
            ids,
            (adj_grad, adj_other, *lot),
            [like((rows, cols), F32)] + [like((rows, cols), BF)] * 3,
            [pltpu.VMEM((2, block_rows, cols), F32)],
            flops=4 * block_rows * adj_grad.shape[1] * cols,
            name=name,
        )
        return [sums[0]] + [swap("section", sums[m], m) for m in (1, 2, 3)]

    two, early[1:4] = lax.optimization_barrier((two, early[1:4]))
    lot_one = products("products", proj_weight, one, two)
    inner, ends, lot_one[0] = lax.optimization_barrier((inner, ends, lot_one[0]))
    lot_two = products("last_products", inner, ends)
    lot_two[0], early[4:] = lax.optimization_barrier((lot_two[0], early[4:]))
    lane = outer * piece
    (packed,) = local_call(
        packing_kernel,
        ids,
        (*lot_one, *lot_two, pack),
        [like((reps * 2 * capacity, lane), BF)],
        name="packing",
        flops=2 * pack.size * lane,
    )
    outgoing = packed.reshape(reps, 2 * capacity, lane)
    incoming = lax.all_to_all(outgoing, "rep", split_axis=0, concat_axis=0, tiled=True)
    slot_frames = slot_frames.reshape(outer, 2, capacity)
    order = jnp.stack([jnp.stack([slot_frames[:, p], slot_frames[:, 1 - p]], axis=1).reshape(-1) for p in range(2)])
    channel = lax.broadcasted_iota(jnp.int32, (feat, feat), 0)
    column = lax.broadcasted_iota(jnp.int32, (feat, feat), 1)
    group = channel // part_rows
    moved = (group % 2) * (feat // 2) + (group // 2) * part_rows + channel % part_rows
    to_halves = (moved == column).astype(BF)
    late = like((frame_rows + 32, 3 * feat // 4), BF)
    lot = like((frame_rows + 16, 3 * feat // 4), BF)
    wide = pltpu.VMEM((frame_rows + 16, feat), F32)
    grad_out, grad_mixed, p0, p2, p4, p6 = local_call(
        module_kernel,
        ids,
        (incoming, order, w_pointwise2, slope, gated, masks, gate_prob, linear, tap_values, to_halves),
        [like((frame_rows, feat), BF), like((frame_rows, 2 * feat), BF)] + [late] * 4,
        [wide, wide],
        flops=2 * frame_rows * feat * feat + 60 * frame_rows * feat,
        name="module",
    )
    got = [p0, swap(BOTH, p0, 1)]
    far = [swap(BOTH, p, m) for m, p in ((2, p2), (4, p4), (6, p6))]
    for p in far:
        got += [p, swap(BOTH, p, 1)]
    sums = local_call(
        weights_kernel,
        ids,
        (*early, *got),
        [like(lot.shape, F32)] + [lot] * 3,
        [pltpu.VMEM((feat // 2, 3 * feat // 4), F32), pltpu.VMEM((16, feat // 2), F32)],
        flops=2 * 8 * frame_rows * (feat // 2) * (3 * feat // 4),
        name="weights",
    )
    given = [swap(BOTH, sums[m], 8 * m) for m in (1, 2, 3)]
    final = (part_rows, 3 * feat // 4)
    mine_part, f1, f2, f3, tap_part = local_call(
        sum_kernel,
        ids,
        (sums[0], *given),
        [like(final, F32)] + [like(final, BF)] * 3 + [like((16, 4 * part_rows), F32)],
        [pltpu.VMEM(lot.shape, F32)],
        name="sums",
    )
    given = [swap(BOTH, f, 2 * m) for m, f in ((1, f1), (2, f2), (3, f3))]
    w1_grad, w2_grad = local_call(
        assembly_kernel,
        ids,
        (mine_part, *given),
        [like((part_rows, 2 * feat), F32), like((part_rows, feat), F32)],
        name="assembly",
    )
    taps_grad = lax.dynamic_index_in_dim(tap_part.reshape(16, 4, part_rows), place, 1, keepdims=False)[:taps_count].T

    grad_norm = lax.dot_general(grad_mixed, w_pointwise1, COLS, preferred_element_type=F32)
    grad_input = inverse * (
        grad_norm
        - jnp.mean(grad_norm, axis=1, keepdims=True)
        - standard * jnp.mean(grad_norm * standard, axis=1, keepdims=True)
    )
    input_grad = (grad_out.astype(F32) + grad_input).astype(BF)
    return input_grad, w1_grad, w2_grad, taps_grad


def shards(layer_input, *rest):
    if lax.axis_size("rep") == 8 and lax.axis_size("section") == 4:
        return line_shards(layer_input, *rest)
    return plain_shards(layer_input, *rest)


def solution(mesh):
    spread = P(("rep", "section"), None)
    return jax.shard_map(
        shards,
        mesh=mesh,
        in_specs=(spread, spread, P(), P(), P(), P(), P(), P("rep", "section"), P("rep", "section"), P(), P()),
        out_specs=(spread, spread, spread, spread),
        check_vma=False,
    )
```

```python
import jax
import jax.numpy as jnp
from jax import lax
from jax.experimental import pallas as pl
from jax.experimental.pallas import tpu as pltpu
from jax.sharding import PartitionSpec as P

BF = jnp.bfloat16
F32 = jnp.float32
ROWS = (((0,), (0,)), ((), ()))
COLS = (((1,), (1,)), ((), ()))


def xor_perm(count, mask):
    return [(i, i ^ mask) for i in range(count)]


def size_of(axis):
    if isinstance(axis, tuple):
        return lax.axis_size(axis[0]) * lax.axis_size(axis[1])
    return lax.axis_size(axis)


def swap(axis, values, mask):
    return lax.ppermute(values, axis, xor_perm(size_of(axis), mask))


def xor_order(items, place):
    step = 1
    while step < len(items):
        flip = jnp.bitwise_and(place, step) > 0
        items = [jnp.where(flip, items[i ^ step], items[i]) for i in range(len(items))]
        step *= 2
    return items


def local_call(body, ids, operands, outs, scratch=(), flops=0, name=None, stay=(), leave=()):
    moved = sum(o.size * o.dtype.itemsize for o in operands) + sum(
        o.size * o.dtype.itemsize for o in outs
    )
    vmem, other = pl.BlockSpec(memory_space=pltpu.VMEM), pl.BlockSpec(memory_space=pl.ANY)
    return pl.pallas_call(
        body,
        out_shape=tuple(outs),
        in_specs=[pl.BlockSpec(memory_space=pltpu.SMEM)]
        + [other if i in stay else vmem for i in range(len(operands))],
        out_specs=tuple(other if i in leave else vmem for i in range(len(outs))),
        scratch_shapes=list(scratch),
        compiler_params=pltpu.CompilerParams(vmem_limit_bytes=(40 if stay or leave else 24) * 1024 * 1024),
        cost_estimate=pl.CostEstimate(flops=flops, bytes_accessed=moved, transcendentals=0),
        name=name,
    )(ids, *operands)


def like(shape, dtype):
    return jax.ShapeDtypeStruct(shape, dtype)


def aligned(index, size):
    return pl.ds(pl.multiple_of(index * size, size), size)


def routing_kernel(ids, targets, frames, pack, pick):
    here = ids[4]
    width = targets.shape[1]
    slots, rows = pack.shape
    quarter = rows // 2
    blocks = width // quarter
    capacity = slots // (2 * blocks)
    shape = (width, width)
    first, second = lax.broadcasted_iota(jnp.int32, shape, 0), lax.broadcasted_iota(jnp.int32, shape, 1)
    before = ((first < second) & (first // quarter == second // quarter)).astype(F32).astype(BF)
    names = lax.broadcasted_iota(jnp.int32, (blocks, width), 0)
    hits = (names == targets[...]).astype(F32)
    earlier = jnp.dot(hits.astype(BF), before, preferred_element_type=F32)
    rank = jnp.sum(hits * earlier, axis=0, keepdims=True)
    slot = targets[...].astype(F32) * (2 * capacity) + rank
    shape = (width, rows)
    row, col = lax.broadcasted_iota(jnp.int32, shape, 0), lax.broadcasted_iota(jnp.int32, shape, 1)
    wanted = jnp.bitwise_xor(here, col // quarter) * quarter + col % quarter
    take = (row == wanted).astype(F32).astype(BF)
    slot_of = jnp.dot(jnp.broadcast_to(slot, (8, width)).astype(BF), take, preferred_element_type=F32)[0:1, :]
    slot_of = slot_of.astype(jnp.int32) + lax.broadcasted_iota(jnp.int32, (1, rows), 1) // quarter * capacity
    slot_ids = lax.broadcasted_iota(jnp.int32, (slots, rows), 0)
    pack[...] = (slot_of == slot_ids).astype(F32).astype(BF)
    frame_rows = pick.shape[1]
    frame_ids = lax.broadcasted_iota(jnp.int32, (frame_rows, width), 0)
    at_frame = (frame_ids == frames[...]).astype(F32).astype(BF)
    block = lax.broadcasted_iota(jnp.int32, (1, width), 1) // quarter
    rank = rank.astype(jnp.int32)
    slot_ids = lax.broadcasted_iota(jnp.int32, (blocks * capacity, width), 0)
    for p in range(2):
        held = jnp.where(targets[...] == here, jnp.bitwise_xor(block, p) * capacity + rank, -1)
        in_slot = (slot_ids == held).astype(F32).astype(BF)
        pick[p] = lax.dot_general(at_frame, in_slot, COLS, preferred_element_type=F32).astype(BF)


def fill_masks(ids, masks):
    taps_count, frame_rows, _ = masks.shape
    ends = [ids[5]]
    for u in range(1, ids.shape[0] - 5):
        ends.append(ends[-1] + ids[5 + u])
    position = lax.broadcasted_iota(jnp.int32, masks.shape[1:], 0)

    def segment(at):
        return sum(jnp.where(at >= e, 1, 0) for e in ends)

    here = segment(position)
    for k in range(taps_count):
        at = position + (k - taps_count // 2)
        good = (segment(at) == here) & (at >= 0) & (at < frame_rows)
        masks[k] = jnp.where(good, 1.0, 0.0)


def clear_edges(wide):
    edge = jnp.zeros((8, wide.shape[1]), F32)
    wide[0:8, :] = edge
    wide[wide.shape[0] - 8 :, :] = edge


def standardise(x):
    as_float = x[...].astype(F32)
    centred = as_float - jnp.mean(as_float, axis=1, keepdims=True)
    inverse = lax.rsqrt(jnp.mean(centred * centred, axis=1, keepdims=True) + 1e-05)
    return centred * inverse, inverse


def forward_kernel(ids, x, w_one, taps, scale, shift, acts, sends, kept, wide, masks, flipped, halves, sems):
    frame_rows, feat = x.shape
    taps_count = taps.shape[0]
    half = taps_count // 2
    fill_masks(ids, masks)
    normed = standardise(x)[0].astype(BF)
    clear_edges(wide)
    step = 256
    for c in range(feat // step):
        cols = slice(c * step, (c + 1) * step)
        lin = jnp.dot(normed, w_one[:, cols], preferred_element_type=F32)
        gate = jax.nn.sigmoid(
            jnp.dot(normed, w_one[:, feat + c * step : feat + (c + 1) * step], preferred_element_type=F32)
        )
        kept[0, :, cols] = lin
        kept[1, :, cols] = gate
        wide[8 : 8 + frame_rows, cols] = (lin * gate).astype(BF).astype(F32)
    for c in range(feat // 128):
        cols = slice(c * 128, (c + 1) * 128)
        total = jnp.zeros((frame_rows, 128), F32)
        for k in range(taps_count):
            start = 8 + k - half
            total = total + taps[k : k + 1, cols] * (wide[start : start + frame_rows, cols] * masks[k])
        pre = total * scale[:, cols] + shift[:, cols]
        prob = jax.nn.sigmoid(pre)
        kept[2, :, cols] = prob * (1.0 + pre * (1.0 - prob)) * scale[:, cols]
        flipped[0, cols, :] = normed[:, cols].astype(F32).T
        flipped[1, cols, :] = (pre * prob).astype(BF).astype(F32).T
    out_acts = pltpu.make_async_copy(kept, acts, sems.at[0])
    out_acts.start()
    part = feat // 32
    for h in range(2):
        for g in range(32):
            to = h * (feat // 2) + (g // 2) * part
            halves[g % 2, to : to + part, :] = flipped[h, g * part : (g + 1) * part, :].astype(BF)
    copies = [pltpu.make_async_copy(halves.at[g % 2], sends.at[g], sems.at[1 + g]) for g in range(8)]
    for copy in copies:
        copy.start()
    out_acts.wait()
    for copy in copies:
        copy.wait()


def partial_kernel(ids, *refs):
    own_rows, other_rows, *blocks = refs[:-8]
    outs, (rows, own_copy, block_copy, sems) = refs[-8:-4], refs[-4:]
    sec, z = ids[0], ids[1]
    fetch = [pltpu.make_async_copy(own_rows, own_copy, sems.at[0])]
    if len(blocks) == 3:
        fetch.append(pltpu.make_async_copy(blocks[0], block_copy, sems.at[1]))
    for copy in fetch:
        copy.start()
    quarter = outs[0].shape[0] // 2
    if len(blocks) == 2:
        middle = (z == 1) | (z == 2)
        lots = [(0, lambda: jnp.where(middle, blocks[0][...], blocks[1][...]))]
    else:
        lots = [
            (1, lambda: jnp.concatenate([blocks[1][...], blocks[2][...]], axis=0)),
            (0, lambda: block_copy[...]),
        ]
    steps = [(1, other_rows, lots[0]), (0, own_copy, lots[0])] + [
        (w, a, lot) for lot in lots[1:] for w, a in ((1, other_rows), (0, own_copy))
    ]
    for n, (w, a, (at, lot)) in enumerate(steps):
        if n == 1:
            for copy in fetch:
                copy.wait()
        lot = lot()
        first = at * block_copy.shape[0]
        rows[w, :, first : first + lot.shape[0]] = lax.dot_general(a[...], lot, COLS, preferred_element_type=F32)
    for m, out in enumerate(outs):
        q = jnp.bitwise_xor(sec, m)
        for w in range(2):
            out[w * quarter : (w + 1) * quarter, :] = rows[w, aligned(q, quarter), :].astype(out.dtype)


def packing_kernel(ids, own, r1, r2, r3, own_last, l1, l2, l3, pack, out):
    total = own[...] + r1[...].astype(F32) + r2[...].astype(F32) + r3[...].astype(F32)
    last = own_last[...] + l1[...].astype(F32) + l2[...].astype(F32) + l3[...].astype(F32)
    piece = last.shape[1]
    parts = xor_order([total[:, k * piece : (k + 1) * piece] for k in range(3)] + [last], ids[1])
    rows = jnp.concatenate(parts, axis=1).astype(BF)
    out[...] = jnp.dot(pack[...], rows, preferred_element_type=F32).astype(BF)


def module_kernel(
    ids, incoming, pick, taps, w_two, acts,
    grad_out, grad_mixed, p0, p2, p4, p6, wide_gated, wide_grad, masks, w_here, kept, sems,
):
    place = ids[2]
    fetch_w = pltpu.make_async_copy(w_two, w_here, sems.at[0])
    fetch_w.start()
    fetch_acts = pltpu.make_async_copy(acts, kept, sems.at[1])
    fetch_acts.start()
    frame_rows, feat = grad_out.shape
    taps_count = taps.shape[0]
    half = taps_count // 2
    sources, slots, width = incoming.shape
    outer = sources // 2
    piece = width // outer
    fill_masks(ids, masks)
    clear_edges(wide_gated)
    clear_edges(wide_grad)
    for p in range(2):
        rows = jnp.concatenate([incoming[2 * o + p] for o in range(outer)], axis=0)
        got = jnp.dot(pick[p], rows, preferred_element_type=F32).astype(BF)
        for o in range(outer):
            first = (2 * o + p) * piece
            grad_out[:, first : first + piece] = got[:, o * piece : (o + 1) * piece]
    fetch_acts.wait()
    fetch_w.wait()
    here = slice(8, 8 + frame_rows)
    step = 256
    for c in range(feat // step):
        cols = slice(c * step, (c + 1) * step)
        wide_gated[here, cols] = (kept[0, :, cols] * kept[1, :, cols]).astype(BF).astype(F32)
        grad_act = lax.dot_general(grad_out[...], w_here[cols, :], COLS, preferred_element_type=F32)
        wide_grad[here, cols] = grad_act * kept[2, :, cols]
    step = 128
    tap_rows = []
    for c in range(feat // step):
        cols = slice(c * step, (c + 1) * step)
        grad_conv = wide_grad[here, cols]
        total = jnp.zeros((frame_rows, step), F32)
        columns = []
        for k in range(taps_count):
            start = 8 + k - half
            window = wide_gated[start : start + frame_rows, cols] * masks[k]
            columns.append(jnp.sum(window * grad_conv, axis=0, keepdims=True))
            start = 8 + half - k
            back = 2 * half - k
            total = total + taps[k : k + 1, cols] * (wide_grad[start : start + frame_rows, cols] * masks[back])
        tap_rows.append(jnp.concatenate(columns + [jnp.zeros((16 - taps_count, step), F32)], axis=0))
        gate = kept[1, :, cols]
        first = total * gate
        grad_mixed[:, c * step : (c + 1) * step] = first.astype(BF)
        grad_mixed[:, feat + c * step : feat + (c + 1) * step] = (first * kept[0, :, cols] * (1.0 - gate)).astype(BF)
    tap_rows = jnp.concatenate(tap_rows, axis=1).astype(BF)
    w1_cols, w2_cols = feat // 2, feat // 4
    for mask, out in enumerate((p0, p2, p4, p6)):
        q = jnp.bitwise_xor(place, mask)
        out[0:frame_rows, 0:w1_cols] = grad_mixed[:, aligned(q, w1_cols)]
        out[0:frame_rows, w1_cols:] = grad_out[:, aligned(q, w2_cols)]
        for h in range(2):
            tap_at = slice(frame_rows + 16 * h, frame_rows + 16 * (h + 1))
            out[tap_at, 0:w1_cols] = tap_rows[:, h * w1_cols : (h + 1) * w1_cols]
            out[tap_at, w1_cols:] = jnp.zeros((16, w2_cols), BF)


def weights_kernel(ids, early, g0, g1, g2, g3, g4, g5, g6, g7, own, s1, s2, s3, rows, tap_sum, feats, sems):
    z = ids[1]
    me = 2 * ids[2] + ids[3]
    copies = []
    for m in range(8):
        copies.append(pltpu.make_async_copy(early.at[jnp.bitwise_xor(me, m)], feats.at[m], sems.at[m]))
        copies[-1].start()
    gots = (g0, g1, g2, g3, g4, g5, g6, g7)
    frame_rows = feats.shape[2]
    half = feats.shape[1] // 2
    w1_cols = half
    tap_sum[...] = sum(g[frame_rows:, 0:w1_cols].astype(F32) for g in gots)
    for copy in copies:
        copy.wait()
    for cols, first in ((slice(0, w1_cols), 0), (slice(w1_cols, g0.shape[1]), half)):
        total = None
        for m in range(0, 8, 2):
            both = jnp.concatenate([gots[m][0:frame_rows, cols], gots[m + 1][0:frame_rows, cols]], axis=0)
            pair = jnp.concatenate([feats[m, first : first + half, :], feats[m + 1, first : first + half, :]], axis=1)
            term = jnp.dot(pair, both, preferred_element_type=F32)
            total = term if total is None else total + term
        rows[:, cols] = total
    block = half // 4
    for m, out in enumerate((own, s1, s2, s3)):
        o = jnp.bitwise_xor(z, m)
        out[0:block, :] = rows[aligned(o, block), :].astype(out.dtype)
        out[block:, 0 : 2 * block] = tap_sum[aligned(o // 2, 16), aligned(o % 2, 2 * block)].astype(out.dtype)
        out[block:, 2 * block :] = jnp.zeros((out.shape[0] - block, out.shape[1] - 2 * block), out.dtype)


def tail_kernel(ids, x, grad_mixed, w_one, grad_out, out):
    standard, inverse = standardise(x)
    grad_norm = lax.dot_general(grad_mixed[...], w_one[...], COLS, preferred_element_type=F32)
    grad_input = inverse * (
        grad_norm
        - jnp.mean(grad_norm, axis=1, keepdims=True)
        - standard * jnp.mean(grad_norm * standard, axis=1, keepdims=True)
    )
    out[...] = (grad_out[...].astype(F32) + grad_input).astype(BF)


def sum_kernel(ids, own, r1, r2, r3, mine, f1, f2, f3, taps, rows):
    place = ids[2]
    part = mine.shape[0]
    rows[...] = own[...] + r1[...].astype(F32) + r2[...].astype(F32) + r3[...].astype(F32)
    for m, out in enumerate((mine, f1, f2, f3)):
        out[...] = rows[aligned(jnp.bitwise_xor(place, m), part), :].astype(out.dtype)
    taps[...] = rows[4 * part :, 0 : 8 * part]


def assembly_kernel(ids, mine, r1, r2, r3, w1, w2):
    place = ids[2]
    w1_cols, w2_cols = w1.shape[1] // 4, w2.shape[1] // 4
    for m, part in enumerate((mine, r1, r2, r3)):
        q = jnp.bitwise_xor(place, m)
        w1[:, aligned(q, w1_cols)] = part[:, 0:w1_cols].astype(F32)
        w2[:, aligned(q, w2_cols)] = part[:, w1_cols:].astype(F32)


def forward_part(layer_input, lengths, w_one, conv_taps, conv_scale, conv_shift):
    row_count, feat_width = layer_input.shape
    taps_count = conv_taps.shape[0]
    half_span = taps_count // 2
    ends = [lengths[0]]
    for j in range(1, lengths.shape[0]):
        ends.append(ends[-1] + lengths[j])
    position = lax.broadcasted_iota(jnp.int32, (row_count,), 0)
    segment = sum((position >= e).astype(jnp.int32) for e in ends)
    padded_seg = jnp.pad(segment, (half_span, half_span), constant_values=-1)
    as_float = layer_input.astype(F32)
    row_mean = jnp.mean(as_float, axis=1, keepdims=True)
    centred = as_float - row_mean
    inverse = lax.rsqrt(jnp.mean(centred * centred, axis=1, keepdims=True) + 1e-05)
    standard = centred * inverse
    normed = standard.astype(BF)
    mixed = jnp.dot(normed, w_one, preferred_element_type=F32)
    linear = mixed[:, :feat_width]
    gate_prob = jax.nn.sigmoid(mixed[:, feat_width:])
    gated = (linear * gate_prob).astype(BF)
    padded_gated = jnp.pad(gated, ((half_span, half_span), (0, 0))).astype(F32)
    tap_values = conv_taps.astype(F32)
    conv_sum = jnp.zeros((row_count, feat_width), F32)
    for k in range(taps_count):
        same_utt = padded_seg[k : k + row_count] == segment
        window = jnp.where(same_utt[:, None], padded_gated[k : k + row_count], 0.0)
        conv_sum = conv_sum + tap_values[k] * window
    pre_act = conv_sum * conv_scale + conv_shift
    act_prob = jax.nn.sigmoid(pre_act)
    activated = (pre_act * act_prob).astype(BF)
    slope = act_prob * (1.0 + pre_act * (1.0 - act_prob)) * conv_scale
    return standard, inverse, normed, linear, gate_prob, padded_gated, padded_seg, segment, activated, slope


def plain_shards(
    layer_input,
    utt_frames,
    w_pointwise1,
    conv_taps,
    conv_scale,
    conv_shift,
    w_pointwise2,
    adj_grad,
    proj_weight,
    adj_target,
    adj_frame,
):
    reps = lax.axis_size("rep")
    sections = lax.axis_size("section")
    rep_here = lax.axis_index("rep")
    sec_here = lax.axis_index("section")
    block_rows = adj_grad.shape[0]
    quarter = block_rows // sections
    frame_rows, feat = layer_input.shape
    taps_count = conv_taps.shape[0]
    half_span = taps_count // 2
    capacity = max(2, 2 * quarter // reps)
    outer = reps // 2
    pair_here = rep_here % 2
    outer_here = rep_here // 2
    piece = proj_weight.shape[0]

    adj_other = swap("rep", adj_grad, 1)
    blocks = [proj_weight] + [swap("rep", proj_weight, 2 * k) for k in range(1, outer)]

    targets = adj_target[:, 0].reshape(reps, sections, quarter)
    frames = adj_frame.reshape(reps, sections, quarter)
    sec_targets = lax.dynamic_index_in_dim(targets, sec_here, 1, keepdims=False)
    sec_frames = lax.dynamic_index_in_dim(frames, sec_here, 1, keepdims=False)
    row_a = lax.broadcasted_iota(jnp.int32, (quarter, quarter), 0)
    row_b = lax.broadcasted_iota(jnp.int32, (quarter, quarter), 1)
    same = (sec_targets[:, :, None] == sec_targets[:, None, :]) & (row_b < row_a)[None]
    rank = jnp.sum(same.astype(jnp.int32), axis=2)
    mine = sec_targets == rep_here
    slots = lax.broadcasted_iota(jnp.int32, (1, capacity, 1), 1)
    hit = mine[:, None, :] & (rank[:, None, :] == slots)
    slot_frames = jnp.sum(jnp.where(hit, sec_frames[:, None, :] + 1, 0), axis=2) - 1

    pair_blocks = jnp.stack([rep_here, jnp.bitwise_xor(rep_here, 1)])
    pair_targets = jnp.concatenate([lax.dynamic_index_in_dim(sec_targets, pair_blocks[w], 0, keepdims=False) for w in range(2)])
    pair_rank = jnp.concatenate([lax.dynamic_index_in_dim(rank, pair_blocks[w], 0, keepdims=False) for w in range(2)])
    member = lax.broadcasted_iota(jnp.int32, (2 * quarter,), 0) // quarter
    slot_of = (pair_targets * 2 + member) * capacity + pair_rank
    slot_ids = lax.broadcasted_iota(jnp.int32, (reps * 2 * capacity, 2 * quarter), 0)
    pack = (slot_of[None, :] == slot_ids).astype(BF)

    standard, inverse, normed, linear, gate_prob, padded_gated, padded_seg, segment, activated, slope = forward_part(
        layer_input, utt_frames[0], w_pointwise1, conv_taps, conv_scale, conv_shift
    )
    part_rows = feat // (reps * sections)

    here = rep_here * sections + sec_here
    core = here % 2
    place = (here // 2) % 4
    BOTH = ("rep", "section")

    def core_halves(values):
        return values.reshape(frame_rows, reps * sections // 2, 2, part_rows).transpose(2, 0, 1, 3).reshape(
            2, frame_rows, feat // 2
        )

    halves = jnp.concatenate([core_halves(normed), core_halves(activated)], axis=2)
    mine_half = lax.dynamic_index_in_dim(halves, core, 0, keepdims=False)
    their_half = lax.dynamic_index_in_dim(halves, 1 - core, 0, keepdims=False)
    chip_half = jnp.concatenate([mine_half, swap(BOTH, their_half, 1)], axis=0)
    early = {0: chip_half}
    for m in (2, 4, 6):
        early[m] = swap(BOTH, chip_half, m)
    near = early[0]
    straight = jnp.concatenate([early[m][:frame_rows] for m in (2, 4, 6)], axis=0)
    across = jnp.concatenate([early[m][frame_rows:] for m in (2, 4, 6)], axis=0)

    adj_pair = jnp.concatenate([adj_grad, adj_other], axis=0)

    def section_sum(lot):
        terms = [lax.dot_general(adj_pair, b, COLS, preferred_element_type=F32).astype(BF) for b in lot]
        terms = jnp.concatenate(terms, axis=1).reshape(2, sections, quarter, len(lot) * piece)
        total = lax.dynamic_index_in_dim(terms, sec_here, 1, keepdims=False).astype(F32)
        for m in range(1, sections):
            given = lax.dynamic_index_in_dim(terms, jnp.bitwise_xor(sec_here, m), 1, keepdims=False)
            total = total + swap("section", given, m).astype(F32)
        total = total.astype(BF).reshape(2 * quarter, len(lot) * piece)
        return [total[:, i * piece : (i + 1) * piece] for i in range(len(lot))]

    feat_grad = section_sum(blocks[:-1]) + section_sum(blocks[-1:])
    feat_grad = jnp.concatenate(xor_order(feat_grad, outer_here), axis=1)
    packed = jnp.dot(pack, feat_grad, preferred_element_type=F32).astype(BF)
    outgoing = packed.reshape(reps, 2 * capacity, outer * piece)
    incoming = lax.all_to_all(outgoing, "rep", split_axis=0, concat_axis=0, tiled=True)
    incoming = incoming.reshape(outer, 2, 2 * capacity, outer * piece)
    slot_frames = slot_frames.reshape(outer, 2, capacity)
    frame_ids = lax.broadcasted_iota(jnp.int32, (frame_rows, outer * 2 * capacity), 0)
    out_halves = []
    for p in range(2):
        order = jnp.stack([slot_frames[:, p], slot_frames[:, 1 - p]], axis=1).reshape(1, -1)
        pick = (frame_ids == order).astype(BF)
        out_halves.append(
            jnp.dot(pick, incoming[:, p].reshape(-1, outer * piece), preferred_element_type=F32)
            .astype(BF)
            .reshape(frame_rows, outer, piece)
        )
    grad_out = jnp.stack(out_halves, axis=2).reshape(frame_rows, feat)

    def weight_grad(first_col, values):
        width = values.shape[1] // 4
        lots = [values[:, q * width : (q + 1) * width] for q in range(4)]
        lots = xor_order(lots, place)
        got = {0: lots[0]}
        for m in (2, 4, 6):
            got[m] = swap(BOTH, lots[m // 2], m)
        for m in (0, 2, 4, 6):
            got[m + 1] = swap(BOTH, got[m], 1)
        cols = slice(first_col, first_col + feat // 2)
        part = lax.dot_general(near[:, cols], jnp.concatenate([got[0], got[1]]), ROWS, preferred_element_type=F32)
        part += lax.dot_general(
            straight[:, cols], jnp.concatenate([got[m] for m in (2, 4, 6)]), ROWS, preferred_element_type=F32
        )
        part += lax.dot_general(
            across[:, cols], jnp.concatenate([got[m] for m in (3, 5, 7)]), ROWS, preferred_element_type=F32
        )
        part = part.reshape(outer, 4 * part_rows, width)
        total = lax.dynamic_index_in_dim(part, outer_here, 0, keepdims=False)
        sent = part.astype(BF)
        for m in range(1, outer):
            given = lax.dynamic_index_in_dim(sent, jnp.bitwise_xor(outer_here, m), 0, keepdims=False)
            total = total + swap(BOTH, given, 8 * m).astype(F32)
        total = total.astype(BF)
        lots = xor_order([total[q * part_rows : (q + 1) * part_rows] for q in range(4)], place)
        lots = [lots[0]] + [swap(BOTH, lots[m], 2 * m) for m in (1, 2, 3)]
        return jnp.concatenate(xor_order(lots, place), axis=1).astype(F32)

    w2_grad = weight_grad(feat // 2, grad_out)

    grad_act = lax.dot_general(grad_out, w_pointwise2, COLS, preferred_element_type=F32)
    grad_conv = grad_act * slope
    padded_grad = jnp.pad(grad_conv, ((half_span, half_span), (0, 0)))
    grad_gated = jnp.zeros((frame_rows, feat), F32)
    tap_values = conv_taps.astype(F32)
    columns = []
    for k in range(taps_count):
        same_utt = padded_seg[k : k + frame_rows] == segment
        window = jnp.where(same_utt[:, None], padded_gated[k : k + frame_rows], 0.0)
        columns.append(jnp.sum(window * grad_conv, axis=0))
        back = 2 * half_span - k
        back_same = padded_seg[back : back + frame_rows] == segment
        grad_gated = grad_gated + tap_values[k] * jnp.where(
            back_same[:, None], padded_grad[back : back + frame_rows], 0.0
        )
    first = grad_gated * gate_prob
    grad_mixed = jnp.concatenate([first, first * linear * (1.0 - gate_prob)], axis=1).astype(BF)
    w1_grad = weight_grad(0, grad_mixed)
    taps_term = jnp.stack(columns, axis=0).reshape(taps_count, reps * sections, part_rows)
    taps_term = jnp.pad(taps_term.transpose(1, 0, 2), ((0, 0), (0, 16 - taps_count), (0, 0))).astype(BF)
    taps_all = lax.all_to_all(taps_term, BOTH, split_axis=0, concat_axis=0, tiled=True)
    taps_grad = jnp.sum(taps_all.astype(F32), axis=0)[:taps_count].T

    grad_norm = lax.dot_general(grad_mixed, w_pointwise1, COLS, preferred_element_type=F32)
    grad_input = inverse * (
        grad_norm
        - jnp.mean(grad_norm, axis=1, keepdims=True)
        - standard * jnp.mean(grad_norm * standard, axis=1, keepdims=True)
    )
    input_grad = (grad_out.astype(F32) + grad_input).astype(BF)
    return input_grad, w1_grad, w2_grad, taps_grad


def line_shards(
    layer_input,
    utt_frames,
    w_pointwise1,
    conv_taps,
    conv_scale,
    conv_shift,
    w_pointwise2,
    adj_grad,
    proj_weight,
    adj_target,
    adj_frame,
):
    reps = lax.axis_size("rep")
    sections = lax.axis_size("section")
    rep_here = lax.axis_index("rep")
    sec_here = lax.axis_index("section")
    block_rows = adj_grad.shape[0]
    quarter = block_rows // sections
    frame_rows, feat = layer_input.shape
    taps_count = conv_taps.shape[0]
    half_span = taps_count // 2
    capacity = max(2, 2 * quarter // reps)
    outer = reps // 2
    pair_here = rep_here % 2
    outer_here = rep_here // 2
    piece = proj_weight.shape[0]

    two = swap("rep", proj_weight, 4)
    one = swap("rep", proj_weight, 2)
    adj_other = swap("rep", adj_grad, 1)
    proj_again, two, layer_later = lax.optimization_barrier((proj_weight, two, layer_input))
    inner = lax.ppermute(proj_again, "rep", [(o * 2 + p, (3 - o) * 2 + p) for o in (1, 2) for p in (0, 1)])
    ends = lax.ppermute(two, "rep", [(o * 2 + p, (o ^ 1) * 2 + p) for o in (1, 2) for p in (0, 1)])

    targets = adj_target[:, 0].reshape(reps, sections, quarter)
    frames = adj_frame.reshape(reps, sections, quarter)
    sec_targets = lax.dynamic_index_in_dim(targets, sec_here, 1, keepdims=False)
    sec_frames = lax.dynamic_index_in_dim(frames, sec_here, 1, keepdims=False)
    part_rows = feat // (reps * sections)

    here = rep_here * sections + sec_here
    core = here % 2
    place = (here // 2) % 4
    BOTH = ("rep", "section")

    ids = jnp.stack([sec_here, outer_here, place, core, rep_here]).astype(jnp.int32)
    ids = jnp.concatenate([ids, utt_frames[0]])
    pack, pick = local_call(
        routing_kernel,
        ids,
        (sec_targets.reshape(1, -1), sec_frames.reshape(1, -1)),
        [like((reps * 2 * capacity, 2 * quarter), BF), like((2, frame_rows, reps * capacity), BF)],
        name="routing",
    )
    tap_values = conv_taps.astype(F32)
    square = (frame_rows, feat)
    group = 8
    dma = pltpu.SemaphoreType.DMA
    wide = pltpu.VMEM((frame_rows + 16, feat), F32)
    mask_space = pltpu.VMEM((taps_count, frame_rows, 128), F32)
    acts, sends = local_call(
        forward_kernel,
        ids,
        (layer_later, w_pointwise1, tap_values, conv_scale.reshape(1, -1), conv_shift.reshape(1, -1)),
        [like((3, *square), F32), like((group, feat, frame_rows), BF)],
        [
            pltpu.VMEM((3, *square), F32),
            wide,
            mask_space,
            pltpu.VMEM((2, feat, frame_rows), F32),
            pltpu.VMEM((2, feat, frame_rows), BF),
            dma((1 + group,)),
        ],
        flops=4 * frame_rows * feat * feat,
        name="forward",
        leave=(0, 1),
    )
    early = lax.all_to_all(
        sends,
        BOTH,
        split_axis=0,
        concat_axis=0,
        axis_index_groups=[[g * group + m for m in range(group)] for g in range(reps * sections // group)],
        tiled=True,
    )

    rows = 2 * quarter

    def products(name, *lot):
        cols = piece * (3 if len(lot) == 3 else 1)
        sums = local_call(
            partial_kernel,
            ids,
            (adj_grad, adj_other, *lot),
            [like((rows, cols), F32)] + [like((rows, cols), BF)] * 3,
            [pltpu.VMEM((2, block_rows, cols), F32), pltpu.VMEM(adj_grad.shape, BF), pltpu.VMEM(proj_weight.shape, BF), dma((2,))],
            stay=(0, 2) if len(lot) == 3 else (0,),
            flops=4 * block_rows * adj_grad.shape[1] * cols,
            name=name,
        )
        return [sums[0]] + [swap("section", sums[m], m) for m in (1, 2, 3)]

    lot_one = products("products", proj_weight, one, two)
    inner, ends, lot_one = lax.optimization_barrier((inner, ends, lot_one))
    lot_two = products("last_products", inner, ends)
    lot_two, early = lax.optimization_barrier((lot_two, early))
    lane = outer * piece
    (packed,) = local_call(
        packing_kernel,
        ids,
        (*lot_one, *lot_two, pack),
        [like((reps * 2 * capacity, lane), BF)],
        name="packing",
        flops=2 * pack.size * lane,
    )
    outgoing = packed.reshape(reps, 2 * capacity, lane)
    incoming = lax.all_to_all(outgoing, "rep", split_axis=0, concat_axis=0, tiled=True)
    late = like((frame_rows + 32, 3 * feat // 4), BF)
    lot = like((frame_rows + 16, 3 * feat // 4), BF)
    grad_out, grad_mixed, p0, p2, p4, p6 = local_call(
        module_kernel,
        ids,
        (incoming, pick, tap_values, w_pointwise2, acts),
        [like(square, BF), like((frame_rows, 2 * feat), BF)] + [late] * 4,
        [wide, wide, mask_space, pltpu.VMEM((feat, feat), BF), pltpu.VMEM((3, *square), F32), dma((2,))],
        flops=2 * frame_rows * feat * feat + 60 * frame_rows * feat,
        name="module",
        stay=(3, 4),
    )
    got = [p0, swap(BOTH, p0, 1)]
    far = [swap(BOTH, p, m) for m, p in ((2, p2), (4, p4), (6, p6))]
    for p in far:
        got += [p, swap(BOTH, p, 1)]
    sums = local_call(
        weights_kernel,
        ids,
        (early, *got),
        [like(lot.shape, F32)] + [lot] * 3,
        [
            pltpu.VMEM((feat // 2, 3 * feat // 4), F32),
            pltpu.VMEM((32, feat // 2), F32),
            pltpu.VMEM((group, feat, frame_rows), BF),
            dma((group,)),
        ],
        stay=(0,),
        flops=2 * 8 * frame_rows * (feat // 2) * (3 * feat // 4),
        name="weights",
    )
    given = [swap(BOTH, sums[m], 8 * m) for m in (1, 2, 3)]
    final = (part_rows, 3 * feat // 4)
    mine_part, f1, f2, f3, tap_part = local_call(
        sum_kernel,
        ids,
        (sums[0], *given),
        [like(final, F32)] + [like(final, BF)] * 3 + [like((16, 8 * part_rows), F32)],
        [pltpu.VMEM(lot.shape, F32)],
        name="sums",
    )
    given = [swap(BOTH, f, 2 * m) for m, f in ((1, f1), (2, f2), (3, f3))]
    w1_grad, w2_grad = local_call(
        assembly_kernel,
        ids,
        (mine_part, *given),
        [like((part_rows, 2 * feat), F32), like((part_rows, feat), F32)],
        name="assembly",
    )
    here_taps = lax.dynamic_index_in_dim(
        tap_part.reshape(16, 8, part_rows), 2 * place + core, 1, keepdims=False
    )
    taps_grad = here_taps[:taps_count].T
    (input_grad,) = local_call(
        tail_kernel,
        ids,
        (layer_input, grad_mixed, w_pointwise1, grad_out),
        [like(square, BF)],
        flops=4 * frame_rows * feat * feat,
        name="tail",
    )
    return input_grad, w1_grad, w2_grad, taps_grad


def shards(layer_input, *rest):
    if lax.axis_size("rep") == 8 and lax.axis_size("section") == 4:
        return line_shards(layer_input, *rest)
    return plain_shards(layer_input, *rest)


def solution(mesh):
    spread = P(("rep", "section"), None)
    return jax.shard_map(
        shards,
        mesh=mesh,
        in_specs=(spread, spread, P(), P(), P(), P(), P(), P("rep", "section"), P("rep", "section"), P(), P()),
        out_specs=(spread, spread, spread, spread),
        check_vma=False,
    )
```

```python
import jax
import jax.numpy as jnp
from jax import lax
from jax.experimental import pallas as pl
from jax.experimental.pallas import tpu as pltpu
from jax.sharding import PartitionSpec as P

BF = jnp.bfloat16
F32 = jnp.float32
ROWS = (((0,), (0,)), ((), ()))
COLS = (((1,), (1,)), ((), ()))


def xor_perm(count, mask):
    return [(i, i ^ mask) for i in range(count)]


def size_of(axis):
    if isinstance(axis, tuple):
        return lax.axis_size(axis[0]) * lax.axis_size(axis[1])
    return lax.axis_size(axis)


def swap(axis, values, mask):
    return lax.ppermute(values, axis, xor_perm(size_of(axis), mask))


def xor_order(items, place):
    step = 1
    while step < len(items):
        flip = jnp.bitwise_and(place, step) > 0
        items = [jnp.where(flip, items[i ^ step], items[i]) for i in range(len(items))]
        step *= 2
    return items


def local_call(body, ids, operands, outs, scratch=(), flops=0, name=None, stay=(), leave=()):
    moved = sum(o.size * o.dtype.itemsize for o in operands) + sum(
        o.size * o.dtype.itemsize for o in outs
    )
    vmem, other = pl.BlockSpec(memory_space=pltpu.VMEM), pl.BlockSpec(memory_space=pltpu.HBM)
    return pl.pallas_call(
        body,
        out_shape=tuple(outs),
        in_specs=[pl.BlockSpec(memory_space=pltpu.SMEM)]
        + [other if i in stay else vmem for i in range(len(operands))],
        out_specs=tuple(other if i in leave else vmem for i in range(len(outs))),
        scratch_shapes=list(scratch),
        compiler_params=pltpu.CompilerParams(vmem_limit_bytes=(40 if stay or leave else 24) * 1024 * 1024),
        cost_estimate=pl.CostEstimate(flops=flops, bytes_accessed=moved, transcendentals=0),
        name=name,
    )(ids, *operands)


def like(shape, dtype):
    return jax.ShapeDtypeStruct(shape, dtype)


def aligned(index, size):
    return pl.ds(pl.multiple_of(index * size, size), size)


def routing_kernel(ids, targets, frames, pack, pick):
    here = ids[4]
    width = targets.shape[1]
    slots, rows = pack.shape
    quarter = rows // 2
    blocks = width // quarter
    capacity = slots // (2 * blocks)
    shape = (width, width)
    first, second = lax.broadcasted_iota(jnp.int32, shape, 0), lax.broadcasted_iota(jnp.int32, shape, 1)
    before = ((first < second) & (first // quarter == second // quarter)).astype(F32).astype(BF)
    names = lax.broadcasted_iota(jnp.int32, (blocks, width), 0)
    hits = (names == targets[...]).astype(F32)
    earlier = jnp.dot(hits.astype(BF), before, preferred_element_type=F32)
    rank = jnp.sum(hits * earlier, axis=0, keepdims=True)
    slot = targets[...].astype(F32) * (2 * capacity) + rank
    shape = (width, rows)
    row, col = lax.broadcasted_iota(jnp.int32, shape, 0), lax.broadcasted_iota(jnp.int32, shape, 1)
    wanted = jnp.bitwise_xor(here, col // quarter) * quarter + col % quarter
    take = (row == wanted).astype(F32).astype(BF)
    slot_of = jnp.dot(jnp.broadcast_to(slot, (8, width)).astype(BF), take, preferred_element_type=F32)[0:1, :]
    slot_of = slot_of.astype(jnp.int32) + lax.broadcasted_iota(jnp.int32, (1, rows), 1) // quarter * capacity
    slot_ids = lax.broadcasted_iota(jnp.int32, (slots, rows), 0)
    pack[...] = (slot_of == slot_ids).astype(F32).astype(BF)
    frame_rows = pick.shape[1]
    frame_ids = lax.broadcasted_iota(jnp.int32, (frame_rows, width), 0)
    at_frame = (frame_ids == frames[...]).astype(F32).astype(BF)
    block = lax.broadcasted_iota(jnp.int32, (1, width), 1) // quarter
    rank = rank.astype(jnp.int32)
    slot_ids = lax.broadcasted_iota(jnp.int32, (blocks * capacity, width), 0)
    for p in range(2):
        held = jnp.where(targets[...] == here, jnp.bitwise_xor(block, p) * capacity + rank, -1)
        in_slot = (slot_ids == held).astype(F32).astype(BF)
        pick[p] = lax.dot_general(at_frame, in_slot, COLS, preferred_element_type=F32).astype(BF)


def fill_masks(ids, masks):
    taps_count, frame_rows, _ = masks.shape
    ends = [ids[5]]
    for u in range(1, ids.shape[0] - 5):
        ends.append(ends[-1] + ids[5 + u])
    position = lax.broadcasted_iota(jnp.int32, masks.shape[1:], 0)

    def segment(at):
        return sum(jnp.where(at >= e, 1, 0) for e in ends)

    here = segment(position)
    for k in range(taps_count):
        at = position + (k - taps_count // 2)
        good = (segment(at) == here) & (at >= 0) & (at < frame_rows)
        masks[k] = jnp.where(good, 1.0, 0.0)


def clear_edges(wide):
    edge = jnp.zeros((8, wide.shape[1]), F32)
    wide[0:8, :] = edge
    wide[wide.shape[0] - 8 :, :] = edge


def standardise(x):
    as_float = x[...].astype(F32)
    centred = as_float - jnp.mean(as_float, axis=1, keepdims=True)
    inverse = lax.rsqrt(jnp.mean(centred * centred, axis=1, keepdims=True) + 1e-05)
    return centred * inverse, inverse


def forward_kernel(ids, x, w_one, taps, scale, shift, acts, sends, kept, wide, masks, flipped, halves, sems):
    frame_rows, feat = x.shape
    taps_count = taps.shape[0]
    half = taps_count // 2
    fill_masks(ids, masks)
    normed = standardise(x)[0].astype(BF)
    clear_edges(wide)
    step = 256
    for c in range(feat // step):
        cols = slice(c * step, (c + 1) * step)
        lin = jnp.dot(normed, w_one[:, cols], preferred_element_type=F32)
        gate = jax.nn.sigmoid(
            jnp.dot(normed, w_one[:, feat + c * step : feat + (c + 1) * step], preferred_element_type=F32)
        )
        kept[0, :, cols] = lin
        kept[1, :, cols] = gate
        wide[8 : 8 + frame_rows, cols] = (lin * gate).astype(BF).astype(F32)
    for c in range(feat // 128):
        cols = slice(c * 128, (c + 1) * 128)
        total = jnp.zeros((frame_rows, 128), F32)
        for k in range(taps_count):
            start = 8 + k - half
            total = total + taps[k : k + 1, cols] * (wide[start : start + frame_rows, cols] * masks[k])
        pre = total * scale[:, cols] + shift[:, cols]
        prob = jax.nn.sigmoid(pre)
        kept[2, :, cols] = prob * (1.0 + pre * (1.0 - prob)) * scale[:, cols]
        flipped[0, cols, :] = normed[:, cols].astype(F32).T
        flipped[1, cols, :] = (pre * prob).astype(BF).astype(F32).T
    out_acts = pltpu.make_async_copy(kept, acts, sems.at[0])
    out_acts.start()
    part = feat // 32
    for h in range(2):
        for g in range(32):
            to = h * (feat // 2) + (g // 2) * part
            halves[g % 2, to : to + part, :] = flipped[h, g * part : (g + 1) * part, :].astype(BF)
    copies = [pltpu.make_async_copy(halves.at[g % 2], sends.at[g], sems.at[1 + g]) for g in range(8)]
    for copy in copies:
        copy.start()
    out_acts.wait()
    for copy in copies:
        copy.wait()


def partial_kernel(ids, *refs):
    own_rows, other_rows, *blocks = refs[:-8]
    outs, (rows, own_copy, block_copy, sems) = refs[-8:-4], refs[-4:]
    sec, z = ids[0], ids[1]
    fetch = [pltpu.make_async_copy(own_rows, own_copy, sems.at[0])]
    if len(blocks) == 3:
        fetch.append(pltpu.make_async_copy(blocks[0], block_copy, sems.at[1]))
    for copy in fetch:
        copy.start()
    quarter = outs[0].shape[0] // 2
    if len(blocks) == 2:
        middle = (z == 1) | (z == 2)
        lots = [(0, lambda: jnp.where(middle, blocks[0][...], blocks[1][...]))]
    else:
        lots = [
            (1, lambda: jnp.concatenate([blocks[1][...], blocks[2][...]], axis=0)),
            (0, lambda: block_copy[...]),
        ]
    steps = [(1, other_rows, lots[0]), (0, own_copy, lots[0])] + [
        (w, a, lot) for lot in lots[1:] for w, a in ((1, other_rows), (0, own_copy))
    ]
    for n, (w, a, (at, lot)) in enumerate(steps):
        if n == 1:
            for copy in fetch:
                copy.wait()
        lot = lot()
        first = at * block_copy.shape[0]
        rows[w, :, first : first + lot.shape[0]] = lax.dot_general(a[...], lot, COLS, preferred_element_type=F32)
    for m, out in enumerate(outs):
        q = jnp.bitwise_xor(sec, m)
        for w in range(2):
            out[w * quarter : (w + 1) * quarter, :] = rows[w, aligned(q, quarter), :].astype(out.dtype)


def packing_kernel(ids, own, r1, r2, r3, own_last, l1, l2, l3, pack, out):
    total = own[...] + r1[...].astype(F32) + r2[...].astype(F32) + r3[...].astype(F32)
    last = own_last[...] + l1[...].astype(F32) + l2[...].astype(F32) + l3[...].astype(F32)
    piece = last.shape[1]
    parts = xor_order([total[:, k * piece : (k + 1) * piece] for k in range(3)] + [last], ids[1])
    rows = jnp.concatenate(parts, axis=1).astype(BF)
    out[...] = jnp.dot(pack[...], rows, preferred_element_type=F32).astype(BF)


def module_kernel(
    ids, incoming, pick, taps, w_two, acts,
    grad_out, grad_mixed, p0, p2, p4, p6, wide_gated, wide_grad, masks, w_here, kept, sems,
):
    place = ids[2]
    fetch_w = pltpu.make_async_copy(w_two, w_here, sems.at[0])
    fetch_w.start()
    fetch_acts = pltpu.make_async_copy(acts, kept, sems.at[1])
    fetch_acts.start()
    frame_rows, feat = grad_out.shape
    taps_count = taps.shape[0]
    half = taps_count // 2
    sources, slots, width = incoming.shape
    outer = sources // 2
    piece = width // outer
    fill_masks(ids, masks)
    clear_edges(wide_gated)
    clear_edges(wide_grad)
    for p in range(2):
        rows = jnp.concatenate([incoming[2 * o + p] for o in range(outer)], axis=0)
        got = jnp.dot(pick[p], rows, preferred_element_type=F32).astype(BF)
        for o in range(outer):
            first = (2 * o + p) * piece
            grad_out[:, first : first + piece] = got[:, o * piece : (o + 1) * piece]
    fetch_acts.wait()
    fetch_w.wait()
    here = slice(8, 8 + frame_rows)
    step = 256
    for c in range(feat // step):
        cols = slice(c * step, (c + 1) * step)
        wide_gated[here, cols] = (kept[0, :, cols] * kept[1, :, cols]).astype(BF).astype(F32)
        grad_act = lax.dot_general(grad_out[...], w_here[cols, :], COLS, preferred_element_type=F32)
        wide_grad[here, cols] = grad_act * kept[2, :, cols]
    step = 128
    tap_rows = []
    for c in range(feat // step):
        cols = slice(c * step, (c + 1) * step)
        grad_conv = wide_grad[here, cols]
        total = jnp.zeros((frame_rows, step), F32)
        columns = []
        for k in range(taps_count):
            start = 8 + k - half
            window = wide_gated[start : start + frame_rows, cols] * masks[k]
            columns.append(jnp.sum(window * grad_conv, axis=0, keepdims=True))
            start = 8 + half - k
            back = 2 * half - k
            total = total + taps[k : k + 1, cols] * (wide_grad[start : start + frame_rows, cols] * masks[back])
        tap_rows.append(jnp.concatenate(columns + [jnp.zeros((16 - taps_count, step), F32)], axis=0))
        gate = kept[1, :, cols]
        first = total * gate
        grad_mixed[:, c * step : (c + 1) * step] = first.astype(BF)
        grad_mixed[:, feat + c * step : feat + (c + 1) * step] = (first * kept[0, :, cols] * (1.0 - gate)).astype(BF)
    tap_rows = jnp.concatenate(tap_rows, axis=1).astype(BF)
    w1_cols, w2_cols = feat // 2, feat // 4
    for mask, out in enumerate((p0, p2, p4, p6)):
        q = jnp.bitwise_xor(place, mask)
        out[0:frame_rows, 0:w1_cols] = grad_mixed[:, aligned(q, w1_cols)]
        out[0:frame_rows, w1_cols:] = grad_out[:, aligned(q, w2_cols)]
        for h in range(2):
            tap_at = slice(frame_rows + 16 * h, frame_rows + 16 * (h + 1))
            out[tap_at, 0:w1_cols] = tap_rows[:, h * w1_cols : (h + 1) * w1_cols]
            out[tap_at, w1_cols:] = jnp.zeros((16, w2_cols), BF)


def weights_kernel(ids, early, g0, g1, g2, g3, g4, g5, g6, g7, own, s1, s2, s3, rows, tap_sum, feats, sems):
    z = ids[1]
    me = 2 * ids[2] + ids[3]
    copies = []
    for m in range(8):
        copies.append(pltpu.make_async_copy(early.at[jnp.bitwise_xor(me, m)], feats.at[m], sems.at[m]))
        copies[-1].start()
    gots = (g0, g1, g2, g3, g4, g5, g6, g7)
    frame_rows = feats.shape[2]
    half = feats.shape[1] // 2
    w1_cols = half
    tap_sum[...] = sum(g[frame_rows:, 0:w1_cols].astype(F32) for g in gots)
    for copy in copies:
        copy.wait()
    for cols, first in ((slice(0, w1_cols), 0), (slice(w1_cols, g0.shape[1]), half)):
        total = None
        for m in range(0, 8, 2):
            both = jnp.concatenate([gots[m][0:frame_rows, cols], gots[m + 1][0:frame_rows, cols]], axis=0)
            pair = jnp.concatenate([feats[m, first : first + half, :], feats[m + 1, first : first + half, :]], axis=1)
            term = jnp.dot(pair, both, preferred_element_type=F32)
            total = term if total is None else total + term
        rows[:, cols] = total
    block = half // 4
    for m, out in enumerate((own, s1, s2, s3)):
        o = jnp.bitwise_xor(z, m)
        out[0:block, :] = rows[aligned(o, block), :].astype(out.dtype)
        out[block:, 0 : 2 * block] = tap_sum[aligned(o // 2, 16), aligned(o % 2, 2 * block)].astype(out.dtype)
        out[block:, 2 * block :] = jnp.zeros((out.shape[0] - block, out.shape[1] - 2 * block), out.dtype)


def tail_kernel(ids, x, grad_mixed, w_one, grad_out, out):
    standard, inverse = standardise(x)
    grad_norm = lax.dot_general(grad_mixed[...], w_one[...], COLS, preferred_element_type=F32)
    grad_input = inverse * (
        grad_norm
        - jnp.mean(grad_norm, axis=1, keepdims=True)
        - standard * jnp.mean(grad_norm * standard, axis=1, keepdims=True)
    )
    out[...] = (grad_out[...].astype(F32) + grad_input).astype(BF)


def sum_kernel(ids, own, r1, r2, r3, mine, f1, f2, f3, taps, rows):
    place = ids[2]
    part = mine.shape[0]
    rows[...] = own[...] + r1[...].astype(F32) + r2[...].astype(F32) + r3[...].astype(F32)
    for m, out in enumerate((mine, f1, f2, f3)):
        out[...] = rows[aligned(jnp.bitwise_xor(place, m), part), :].astype(out.dtype)
    taps[...] = rows[4 * part :, 0 : 8 * part]


def assembly_kernel(ids, mine, r1, r2, r3, w1, w2):
    place = ids[2]
    w1_cols, w2_cols = w1.shape[1] // 4, w2.shape[1] // 4
    for m, part in enumerate((mine, r1, r2, r3)):
        q = jnp.bitwise_xor(place, m)
        w1[:, aligned(q, w1_cols)] = part[:, 0:w1_cols].astype(F32)
        w2[:, aligned(q, w2_cols)] = part[:, w1_cols:].astype(F32)


def forward_part(layer_input, lengths, w_one, conv_taps, conv_scale, conv_shift):
    row_count, feat_width = layer_input.shape
    taps_count = conv_taps.shape[0]
    half_span = taps_count // 2
    ends = [lengths[0]]
    for j in range(1, lengths.shape[0]):
        ends.append(ends[-1] + lengths[j])
    position = lax.broadcasted_iota(jnp.int32, (row_count,), 0)
    segment = sum((position >= e).astype(jnp.int32) for e in ends)
    padded_seg = jnp.pad(segment, (half_span, half_span), constant_values=-1)
    as_float = layer_input.astype(F32)
    row_mean = jnp.mean(as_float, axis=1, keepdims=True)
    centred = as_float - row_mean
    inverse = lax.rsqrt(jnp.mean(centred * centred, axis=1, keepdims=True) + 1e-05)
    standard = centred * inverse
    normed = standard.astype(BF)
    mixed = jnp.dot(normed, w_one, preferred_element_type=F32)
    linear = mixed[:, :feat_width]
    gate_prob = jax.nn.sigmoid(mixed[:, feat_width:])
    gated = (linear * gate_prob).astype(BF)
    padded_gated = jnp.pad(gated, ((half_span, half_span), (0, 0))).astype(F32)
    tap_values = conv_taps.astype(F32)
    conv_sum = jnp.zeros((row_count, feat_width), F32)
    for k in range(taps_count):
        same_utt = padded_seg[k : k + row_count] == segment
        window = jnp.where(same_utt[:, None], padded_gated[k : k + row_count], 0.0)
        conv_sum = conv_sum + tap_values[k] * window
    pre_act = conv_sum * conv_scale + conv_shift
    act_prob = jax.nn.sigmoid(pre_act)
    activated = (pre_act * act_prob).astype(BF)
    slope = act_prob * (1.0 + pre_act * (1.0 - act_prob)) * conv_scale
    return standard, inverse, normed, linear, gate_prob, padded_gated, padded_seg, segment, activated, slope


def plain_shards(
    layer_input,
    utt_frames,
    w_pointwise1,
    conv_taps,
    conv_scale,
    conv_shift,
    w_pointwise2,
    adj_grad,
    proj_weight,
    adj_target,
    adj_frame,
):
    reps = lax.axis_size("rep")
    sections = lax.axis_size("section")
    rep_here = lax.axis_index("rep")
    sec_here = lax.axis_index("section")
    block_rows = adj_grad.shape[0]
    quarter = block_rows // sections
    frame_rows, feat = layer_input.shape
    taps_count = conv_taps.shape[0]
    half_span = taps_count // 2
    capacity = max(2, 2 * quarter // reps)
    outer = reps // 2
    pair_here = rep_here % 2
    outer_here = rep_here // 2
    piece = proj_weight.shape[0]

    adj_other = swap("rep", adj_grad, 1)
    blocks = [proj_weight] + [swap("rep", proj_weight, 2 * k) for k in range(1, outer)]

    targets = adj_target[:, 0].reshape(reps, sections, quarter)
    frames = adj_frame.reshape(reps, sections, quarter)
    sec_targets = lax.dynamic_index_in_dim(targets, sec_here, 1, keepdims=False)
    sec_frames = lax.dynamic_index_in_dim(frames, sec_here, 1, keepdims=False)
    row_a = lax.broadcasted_iota(jnp.int32, (quarter, quarter), 0)
    row_b = lax.broadcasted_iota(jnp.int32, (quarter, quarter), 1)
    same = (sec_targets[:, :, None] == sec_targets[:, None, :]) & (row_b < row_a)[None]
    rank = jnp.sum(same.astype(jnp.int32), axis=2)
    mine = sec_targets == rep_here
    slots = lax.broadcasted_iota(jnp.int32, (1, capacity, 1), 1)
    hit = mine[:, None, :] & (rank[:, None, :] == slots)
    slot_frames = jnp.sum(jnp.where(hit, sec_frames[:, None, :] + 1, 0), axis=2) - 1

    pair_blocks = jnp.stack([rep_here, jnp.bitwise_xor(rep_here, 1)])
    pair_targets = jnp.concatenate([lax.dynamic_index_in_dim(sec_targets, pair_blocks[w], 0, keepdims=False) for w in range(2)])
    pair_rank = jnp.concatenate([lax.dynamic_index_in_dim(rank, pair_blocks[w], 0, keepdims=False) for w in range(2)])
    member = lax.broadcasted_iota(jnp.int32, (2 * quarter,), 0) // quarter
    slot_of = (pair_targets * 2 + member) * capacity + pair_rank
    slot_ids = lax.broadcasted_iota(jnp.int32, (reps * 2 * capacity, 2 * quarter), 0)
    pack = (slot_of[None, :] == slot_ids).astype(BF)

    standard, inverse, normed, linear, gate_prob, padded_gated, padded_seg, segment, activated, slope = forward_part(
        layer_input, utt_frames[0], w_pointwise1, conv_taps, conv_scale, conv_shift
    )
    part_rows = feat // (reps * sections)

    here = rep_here * sections + sec_here
    core = here % 2
    place = (here // 2) % 4
    BOTH = ("rep", "section")

    def core_halves(values):
        return values.reshape(frame_rows, reps * sections // 2, 2, part_rows).transpose(2, 0, 1, 3).reshape(
            2, frame_rows, feat // 2
        )

    halves = jnp.concatenate([core_halves(normed), core_halves(activated)], axis=2)
    mine_half = lax.dynamic_index_in_dim(halves, core, 0, keepdims=False)
    their_half = lax.dynamic_index_in_dim(halves, 1 - core, 0, keepdims=False)
    chip_half = jnp.concatenate([mine_half, swap(BOTH, their_half, 1)], axis=0)
    early = {0: chip_half}
    for m in (2, 4, 6):
        early[m] = swap(BOTH, chip_half, m)
    near = early[0]
    straight = jnp.concatenate([early[m][:frame_rows] for m in (2, 4, 6)], axis=0)
    across = jnp.concatenate([early[m][frame_rows:] for m in (2, 4, 6)], axis=0)

    adj_pair = jnp.concatenate([adj_grad, adj_other], axis=0)

    def section_sum(lot):
        terms = [lax.dot_general(adj_pair, b, COLS, preferred_element_type=F32).astype(BF) for b in lot]
        terms = jnp.concatenate(terms, axis=1).reshape(2, sections, quarter, len(lot) * piece)
        total = lax.dynamic_index_in_dim(terms, sec_here, 1, keepdims=False).astype(F32)
        for m in range(1, sections):
            given = lax.dynamic_index_in_dim(terms, jnp.bitwise_xor(sec_here, m), 1, keepdims=False)
            total = total + swap("section", given, m).astype(F32)
        total = total.astype(BF).reshape(2 * quarter, len(lot) * piece)
        return [total[:, i * piece : (i + 1) * piece] for i in range(len(lot))]

    feat_grad = section_sum(blocks[:-1]) + section_sum(blocks[-1:])
    feat_grad = jnp.concatenate(xor_order(feat_grad, outer_here), axis=1)
    packed = jnp.dot(pack, feat_grad, preferred_element_type=F32).astype(BF)
    outgoing = packed.reshape(reps, 2 * capacity, outer * piece)
    incoming = lax.all_to_all(outgoing, "rep", split_axis=0, concat_axis=0, tiled=True)
    incoming = incoming.reshape(outer, 2, 2 * capacity, outer * piece)
    slot_frames = slot_frames.reshape(outer, 2, capacity)
    frame_ids = lax.broadcasted_iota(jnp.int32, (frame_rows, outer * 2 * capacity), 0)
    out_halves = []
    for p in range(2):
        order = jnp.stack([slot_frames[:, p], slot_frames[:, 1 - p]], axis=1).reshape(1, -1)
        pick = (frame_ids == order).astype(BF)
        out_halves.append(
            jnp.dot(pick, incoming[:, p].reshape(-1, outer * piece), preferred_element_type=F32)
            .astype(BF)
            .reshape(frame_rows, outer, piece)
        )
    grad_out = jnp.stack(out_halves, axis=2).reshape(frame_rows, feat)

    def weight_grad(first_col, values):
        width = values.shape[1] // 4
        lots = [values[:, q * width : (q + 1) * width] for q in range(4)]
        lots = xor_order(lots, place)
        got = {0: lots[0]}
        for m in (2, 4, 6):
            got[m] = swap(BOTH, lots[m // 2], m)
        for m in (0, 2, 4, 6):
            got[m + 1] = swap(BOTH, got[m], 1)
        cols = slice(first_col, first_col + feat // 2)
        part = lax.dot_general(near[:, cols], jnp.concatenate([got[0], got[1]]), ROWS, preferred_element_type=F32)
        part += lax.dot_general(
            straight[:, cols], jnp.concatenate([got[m] for m in (2, 4, 6)]), ROWS, preferred_element_type=F32
        )
        part += lax.dot_general(
            across[:, cols], jnp.concatenate([got[m] for m in (3, 5, 7)]), ROWS, preferred_element_type=F32
        )
        part = part.reshape(outer, 4 * part_rows, width)
        total = lax.dynamic_index_in_dim(part, outer_here, 0, keepdims=False)
        sent = part.astype(BF)
        for m in range(1, outer):
            given = lax.dynamic_index_in_dim(sent, jnp.bitwise_xor(outer_here, m), 0, keepdims=False)
            total = total + swap(BOTH, given, 8 * m).astype(F32)
        total = total.astype(BF)
        lots = xor_order([total[q * part_rows : (q + 1) * part_rows] for q in range(4)], place)
        lots = [lots[0]] + [swap(BOTH, lots[m], 2 * m) for m in (1, 2, 3)]
        return jnp.concatenate(xor_order(lots, place), axis=1).astype(F32)

    w2_grad = weight_grad(feat // 2, grad_out)

    grad_act = lax.dot_general(grad_out, w_pointwise2, COLS, preferred_element_type=F32)
    grad_conv = grad_act * slope
    padded_grad = jnp.pad(grad_conv, ((half_span, half_span), (0, 0)))
    grad_gated = jnp.zeros((frame_rows, feat), F32)
    tap_values = conv_taps.astype(F32)
    columns = []
    for k in range(taps_count):
        same_utt = padded_seg[k : k + frame_rows] == segment
        window = jnp.where(same_utt[:, None], padded_gated[k : k + frame_rows], 0.0)
        columns.append(jnp.sum(window * grad_conv, axis=0))
        back = 2 * half_span - k
        back_same = padded_seg[back : back + frame_rows] == segment
        grad_gated = grad_gated + tap_values[k] * jnp.where(
            back_same[:, None], padded_grad[back : back + frame_rows], 0.0
        )
    first = grad_gated * gate_prob
    grad_mixed = jnp.concatenate([first, first * linear * (1.0 - gate_prob)], axis=1).astype(BF)
    w1_grad = weight_grad(0, grad_mixed)
    taps_term = jnp.stack(columns, axis=0).reshape(taps_count, reps * sections, part_rows)
    taps_term = jnp.pad(taps_term.transpose(1, 0, 2), ((0, 0), (0, 16 - taps_count), (0, 0))).astype(BF)
    taps_all = lax.all_to_all(taps_term, BOTH, split_axis=0, concat_axis=0, tiled=True)
    taps_grad = jnp.sum(taps_all.astype(F32), axis=0)[:taps_count].T

    grad_norm = lax.dot_general(grad_mixed, w_pointwise1, COLS, preferred_element_type=F32)
    grad_input = inverse * (
        grad_norm
        - jnp.mean(grad_norm, axis=1, keepdims=True)
        - standard * jnp.mean(grad_norm * standard, axis=1, keepdims=True)
    )
    input_grad = (grad_out.astype(F32) + grad_input).astype(BF)
    return input_grad, w1_grad, w2_grad, taps_grad


def line_shards(
    layer_input,
    utt_frames,
    w_pointwise1,
    conv_taps,
    conv_scale,
    conv_shift,
    w_pointwise2,
    adj_grad,
    proj_weight,
    adj_target,
    adj_frame,
):
    reps = lax.axis_size("rep")
    sections = lax.axis_size("section")
    rep_here = lax.axis_index("rep")
    sec_here = lax.axis_index("section")
    block_rows = adj_grad.shape[0]
    quarter = block_rows // sections
    frame_rows, feat = layer_input.shape
    taps_count = conv_taps.shape[0]
    half_span = taps_count // 2
    capacity = max(2, 2 * quarter // reps)
    outer = reps // 2
    pair_here = rep_here % 2
    outer_here = rep_here // 2
    piece = proj_weight.shape[0]

    two = swap("rep", proj_weight, 4)
    one = swap("rep", proj_weight, 2)
    adj_other = swap("rep", adj_grad, 1)
    targets = adj_target[:, 0].reshape(reps, sections, quarter)
    frames = adj_frame.reshape(reps, sections, quarter)
    sec_targets = lax.dynamic_index_in_dim(targets, sec_here, 1, keepdims=False)
    sec_frames = lax.dynamic_index_in_dim(frames, sec_here, 1, keepdims=False)
    part_rows = feat // (reps * sections)

    here = rep_here * sections + sec_here
    core = here % 2
    place = (here // 2) % 4
    BOTH = ("rep", "section")

    ids = jnp.stack([sec_here, outer_here, place, core, rep_here]).astype(jnp.int32)
    ids = jnp.concatenate([ids, utt_frames[0]])
    pack, pick = local_call(
        routing_kernel,
        ids,
        (sec_targets.reshape(1, -1), sec_frames.reshape(1, -1)),
        [like((reps * 2 * capacity, 2 * quarter), BF), like((2, frame_rows, reps * capacity), BF)],
        name="routing",
    )
    proj_again, two, one, adj_other, pack, pick = lax.optimization_barrier(
        (proj_weight, two, one, adj_other, pack, pick)
    )
    inner = lax.ppermute(proj_again, "rep", [(o * 2 + p, (3 - o) * 2 + p) for o in (1, 2) for p in (0, 1)])
    ends = lax.ppermute(two, "rep", [(o * 2 + p, (o ^ 1) * 2 + p) for o in (1, 2) for p in (0, 1)])

    tap_values = conv_taps.astype(F32)
    square = (frame_rows, feat)
    group = 8
    dma = pltpu.SemaphoreType.DMA
    wide = pltpu.VMEM((frame_rows + 16, feat), F32)
    mask_space = pltpu.VMEM((taps_count, frame_rows, 128), F32)
    acts, sends = local_call(
        forward_kernel,
        ids,
        (layer_input, w_pointwise1, tap_values, conv_scale.reshape(1, -1), conv_shift.reshape(1, -1)),
        [like((3, *square), F32), like((group, feat, frame_rows), BF)],
        [
            pltpu.VMEM((3, *square), F32),
            wide,
            mask_space,
            pltpu.VMEM((2, feat, frame_rows), F32),
            pltpu.VMEM((2, feat, frame_rows), BF),
            dma((1 + group,)),
        ],
        flops=4 * frame_rows * feat * feat,
        name="forward",
        leave=(0, 1),
    )
    rows = 2 * quarter

    def products(name, *lot):
        cols = piece * (3 if len(lot) == 3 else 1)
        sums = local_call(
            partial_kernel,
            ids,
            (adj_grad, adj_other, *lot),
            [like((rows, cols), F32)] + [like((rows, cols), BF)] * 3,
            [pltpu.VMEM((2, block_rows, cols), F32), pltpu.VMEM(adj_grad.shape, BF), pltpu.VMEM(proj_weight.shape, BF), dma((2,))],
            stay=(0, 2) if len(lot) == 3 else (0,),
            flops=4 * block_rows * adj_grad.shape[1] * cols,
            name=name,
        )
        return [sums[0]] + [swap("section", sums[m], m) for m in (1, 2, 3)]

    lot_one = products("products", proj_weight, one, two)
    inner, ends, lot_one = lax.optimization_barrier((inner, ends, lot_one))
    lot_two = products("last_products", inner, ends)
    lot_two[0], sends = lax.optimization_barrier((lot_two[0], sends))
    early = lax.all_to_all(
        sends,
        BOTH,
        split_axis=0,
        concat_axis=0,
        axis_index_groups=[[g * group + m for m in range(group)] for g in range(reps * sections // group)],
        tiled=True,
    )
    lane = outer * piece
    (packed,) = local_call(
        packing_kernel,
        ids,
        (*lot_one, *lot_two, pack),
        [like((reps * 2 * capacity, lane), BF)],
        name="packing",
        flops=2 * pack.size * lane,
    )
    outgoing = packed.reshape(reps, 2 * capacity, lane)
    incoming = lax.all_to_all(outgoing, "rep", split_axis=0, concat_axis=0, tiled=True)
    incoming, early = lax.optimization_barrier((incoming, early))
    late = like((frame_rows + 32, 3 * feat // 4), BF)
    lot = like((frame_rows + 16, 3 * feat // 4), BF)
    grad_out, grad_mixed, p0, p2, p4, p6 = local_call(
        module_kernel,
        ids,
        (incoming, pick, tap_values, w_pointwise2, acts),
        [like(square, BF), like((frame_rows, 2 * feat), BF)] + [late] * 4,
        [wide, wide, mask_space, pltpu.VMEM((feat, feat), BF), pltpu.VMEM((3, *square), F32), dma((2,))],
        flops=2 * frame_rows * feat * feat + 60 * frame_rows * feat,
        name="module",
        stay=(3, 4),
    )
    got = [p0, swap(BOTH, p0, 1)]
    far = [swap(BOTH, p, m) for m, p in ((2, p2), (4, p4), (6, p6))]
    for p in far:
        got += [p, swap(BOTH, p, 1)]
    sums = local_call(
        weights_kernel,
        ids,
        (early, *got),
        [like(lot.shape, F32)] + [lot] * 3,
        [
            pltpu.VMEM((feat // 2, 3 * feat // 4), F32),
            pltpu.VMEM((32, feat // 2), F32),
            pltpu.VMEM((group, feat, frame_rows), BF),
            dma((group,)),
        ],
        stay=(0,),
        flops=2 * 8 * frame_rows * (feat // 2) * (3 * feat // 4),
        name="weights",
    )
    given = [swap(BOTH, sums[m], 8 * m) for m in (1, 2, 3)]
    final = (part_rows, 3 * feat // 4)
    mine_part, f1, f2, f3, tap_part = local_call(
        sum_kernel,
        ids,
        (sums[0], *given),
        [like(final, F32)] + [like(final, BF)] * 3 + [like((16, 8 * part_rows), F32)],
        [pltpu.VMEM(lot.shape, F32)],
        name="sums",
    )
    given = [swap(BOTH, f, 2 * m) for m, f in ((1, f1), (2, f2), (3, f3))]
    w1_grad, w2_grad = local_call(
        assembly_kernel,
        ids,
        (mine_part, *given),
        [like((part_rows, 2 * feat), F32), like((part_rows, feat), F32)],
        name="assembly",
    )
    here_taps = lax.dynamic_index_in_dim(
        tap_part.reshape(16, 8, part_rows), 2 * place + core, 1, keepdims=False
    )
    taps_grad = here_taps[:taps_count].T
    (input_grad,) = local_call(
        tail_kernel,
        ids,
        (layer_input, grad_mixed, w_pointwise1, grad_out),
        [like(square, BF)],
        flops=4 * frame_rows * feat * feat,
        name="tail",
    )
    return input_grad, w1_grad, w2_grad, taps_grad


def shards(layer_input, *rest):
    if lax.axis_size("rep") == 8 and lax.axis_size("section") == 4:
        return line_shards(layer_input, *rest)
    return plain_shards(layer_input, *rest)


def solution(mesh):
    spread = P(("rep", "section"), None)
    return jax.shard_map(
        shards,
        mesh=mesh,
        in_specs=(spread, spread, P(), P(), P(), P(), P(), P("rep", "section"), P("rep", "section"), P(), P()),
        out_specs=(spread, spread, spread, spread),
        check_vma=False,
    )
```

```python
import jax
import jax.numpy as jnp
from jax import lax
from jax.experimental import pallas as pl
from jax.experimental.pallas import tpu as pltpu
from jax.sharding import PartitionSpec as P

BF = jnp.bfloat16
F32 = jnp.float32
ROWS = (((0,), (0,)), ((), ()))
COLS = (((1,), (1,)), ((), ()))


def xor_perm(count, mask):
    return [(i, i ^ mask) for i in range(count)]


def size_of(axis):
    if isinstance(axis, tuple):
        return lax.axis_size(axis[0]) * lax.axis_size(axis[1])
    return lax.axis_size(axis)


def swap(axis, values, mask):
    return lax.ppermute(values, axis, xor_perm(size_of(axis), mask))


def xor_order(items, place):
    step = 1
    while step < len(items):
        flip = jnp.bitwise_and(place, step) > 0
        items = [jnp.where(flip, items[i ^ step], items[i]) for i in range(len(items))]
        step *= 2
    return items


def local_call(body, ids, operands, outs, scratch=(), flops=0, name=None, stay=(), leave=()):
    moved = sum(o.size * o.dtype.itemsize for o in operands) + sum(
        o.size * o.dtype.itemsize for o in outs
    )
    vmem, other = pl.BlockSpec(memory_space=pltpu.VMEM), pl.BlockSpec(memory_space=pltpu.HBM)
    return pl.pallas_call(
        body,
        out_shape=tuple(outs),
        in_specs=[pl.BlockSpec(memory_space=pltpu.SMEM)]
        + [other if i in stay else vmem for i in range(len(operands))],
        out_specs=tuple(other if i in leave else vmem for i in range(len(outs))),
        scratch_shapes=list(scratch),
        compiler_params=pltpu.CompilerParams(vmem_limit_bytes=(40 if stay or leave else 24) * 1024 * 1024),
        cost_estimate=pl.CostEstimate(flops=flops, bytes_accessed=moved, transcendentals=0),
        name=name,
    )(ids, *operands)


def like(shape, dtype):
    return jax.ShapeDtypeStruct(shape, dtype)


def aligned(index, size):
    return pl.ds(pl.multiple_of(index * size, size), size)


def routing_kernel(ids, targets, frames, pack, pick):
    here = ids[4]
    width = targets.shape[1]
    slots, rows = pack.shape
    quarter = rows // 2
    blocks = width // quarter
    capacity = slots // (2 * blocks)
    shape = (width, width)
    first, second = lax.broadcasted_iota(jnp.int32, shape, 0), lax.broadcasted_iota(jnp.int32, shape, 1)
    before = ((first < second) & (first // quarter == second // quarter)).astype(F32).astype(BF)
    names = lax.broadcasted_iota(jnp.int32, (blocks, width), 0)
    hits = (names == targets[...]).astype(F32)
    earlier = jnp.dot(hits.astype(BF), before, preferred_element_type=F32)
    rank = jnp.sum(hits * earlier, axis=0, keepdims=True)
    slot = targets[...].astype(F32) * (2 * capacity) + rank
    shape = (width, rows)
    row, col = lax.broadcasted_iota(jnp.int32, shape, 0), lax.broadcasted_iota(jnp.int32, shape, 1)
    wanted = jnp.bitwise_xor(here, col // quarter) * quarter + col % quarter
    take = (row == wanted).astype(F32).astype(BF)
    slot_of = jnp.dot(jnp.broadcast_to(slot, (8, width)).astype(BF), take, preferred_element_type=F32)[0:1, :]
    slot_of = slot_of.astype(jnp.int32) + lax.broadcasted_iota(jnp.int32, (1, rows), 1) // quarter * capacity
    slot_ids = lax.broadcasted_iota(jnp.int32, (slots, rows), 0)
    pack[...] = (slot_of == slot_ids).astype(F32).astype(BF)
    frame_rows = pick.shape[1]
    frame_ids = lax.broadcasted_iota(jnp.int32, (frame_rows, width), 0)
    at_frame = (frame_ids == frames[...]).astype(F32).astype(BF)
    block = lax.broadcasted_iota(jnp.int32, (1, width), 1) // quarter
    rank = rank.astype(jnp.int32)
    slot_ids = lax.broadcasted_iota(jnp.int32, (blocks * capacity, width), 0)
    for p in range(2):
        held = jnp.where(targets[...] == here, jnp.bitwise_xor(block, p) * capacity + rank, -1)
        in_slot = (slot_ids == held).astype(F32).astype(BF)
        pick[p] = lax.dot_general(at_frame, in_slot, COLS, preferred_element_type=F32).astype(BF)


def fill_masks(ids, masks):
    taps_count, frame_rows, _ = masks.shape
    ends = [ids[5]]
    for u in range(1, ids.shape[0] - 5):
        ends.append(ends[-1] + ids[5 + u])
    position = lax.broadcasted_iota(jnp.int32, masks.shape[1:], 0)

    def segment(at):
        return sum(jnp.where(at >= e, 1, 0) for e in ends)

    here = segment(position)
    for k in range(taps_count):
        at = position + (k - taps_count // 2)
        good = (segment(at) == here) & (at >= 0) & (at < frame_rows)
        masks[k] = jnp.where(good, 1.0, 0.0)


def clear_edges(wide):
    edge = jnp.zeros((8, wide.shape[1]), F32)
    wide[0:8, :] = edge
    wide[wide.shape[0] - 8 :, :] = edge


def standardise(x):
    as_float = x[...].astype(F32)
    centred = as_float - jnp.mean(as_float, axis=1, keepdims=True)
    inverse = lax.rsqrt(jnp.mean(centred * centred, axis=1, keepdims=True) + 1e-05)
    return centred * inverse, inverse


def forward_kernel(ids, x, w_one, taps, scale, shift, acts, mine, theirs, kept, wide, masks, flipped, halves, sems):
    core = ids[3]
    frame_rows, feat = x.shape
    taps_count = taps.shape[0]
    taps = taps[...].astype(F32)
    half = taps_count // 2
    fill_masks(ids, masks)
    normed = standardise(x)[0].astype(BF)
    clear_edges(wide)
    step = 256
    for c in range(feat // step):
        cols = slice(c * step, (c + 1) * step)
        lin = jnp.dot(normed, w_one[:, cols], preferred_element_type=F32)
        gate = jax.nn.sigmoid(
            jnp.dot(normed, w_one[:, feat + c * step : feat + (c + 1) * step], preferred_element_type=F32)
        )
        kept[0, :, cols] = lin
        kept[1, :, cols] = gate
        wide[8 : 8 + frame_rows, cols] = (lin * gate).astype(BF).astype(F32)
    for c in range(feat // 128):
        cols = slice(c * 128, (c + 1) * 128)
        total = jnp.zeros((frame_rows, 128), F32)
        for k in range(taps_count):
            start = 8 + k - half
            total = total + taps[k : k + 1, cols] * (wide[start : start + frame_rows, cols] * masks[k])
        pre = total * scale[:, cols] + shift[:, cols]
        prob = jax.nn.sigmoid(pre)
        kept[2, :, cols] = prob * (1.0 + pre * (1.0 - prob)) * scale[:, cols]
        flipped[0, cols, :] = normed[:, cols].astype(F32).T
        flipped[1, cols, :] = (pre * prob).astype(BF).astype(F32).T
    out_acts = pltpu.make_async_copy(kept, acts, sems.at[0])
    out_acts.start()
    part = feat // 32
    for h in range(2):
        for g in range(32):
            to = h * (feat // 2) + (g // 2) * part
            halves[g % 2, to : to + part, :] = flipped[h, g * part : (g + 1) * part, :].astype(BF)
    copies = [
        pltpu.make_async_copy(halves.at[core], mine, sems.at[1]),
        pltpu.make_async_copy(halves.at[1 - core], theirs, sems.at[2]),
    ]
    for copy in copies:
        copy.start()
    out_acts.wait()
    for copy in copies:
        copy.wait()


def partial_kernel(ids, *refs):
    own_rows, other_rows, *blocks = refs[:-8]
    outs, (rows, own_copy, block_copy, sems) = refs[-8:-4], refs[-4:]
    sec, z = ids[0], ids[1]
    fetch = [pltpu.make_async_copy(own_rows, own_copy, sems.at[0])]
    if len(blocks) == 3:
        fetch.append(pltpu.make_async_copy(blocks[0], block_copy, sems.at[1]))
    for copy in fetch:
        copy.start()
    quarter = outs[0].shape[0] // 2
    if len(blocks) == 2:
        middle = (z == 1) | (z == 2)
        lots = [(0, lambda: jnp.where(middle, blocks[0][...], blocks[1][...]))]
    else:
        lots = [
            (1, lambda: jnp.concatenate([blocks[1][...], blocks[2][...]], axis=0)),
            (0, lambda: block_copy[...]),
        ]
    steps = [(1, other_rows, lots[0]), (0, own_copy, lots[0])] + [
        (w, a, lot) for lot in lots[1:] for w, a in ((1, other_rows), (0, own_copy))
    ]
    for n, (w, a, (at, lot)) in enumerate(steps):
        if n == 1:
            for copy in fetch:
                copy.wait()
        lot = lot()
        first = at * block_copy.shape[0]
        rows[w, :, first : first + lot.shape[0]] = lax.dot_general(a[...], lot, COLS, preferred_element_type=F32)
    for m, out in enumerate(outs):
        q = jnp.bitwise_xor(sec, m)
        for w in range(2):
            out[w * quarter : (w + 1) * quarter, :] = rows[w, aligned(q, quarter), :].astype(out.dtype)


def packing_kernel(ids, own, r1, r2, r3, own_last, l1, l2, l3, pack, out):
    total = own[...] + r1[...].astype(F32) + r2[...].astype(F32) + r3[...].astype(F32)
    last = own_last[...] + l1[...].astype(F32) + l2[...].astype(F32) + l3[...].astype(F32)
    piece = last.shape[1]
    parts = xor_order([total[:, k * piece : (k + 1) * piece] for k in range(3)] + [last], ids[1])
    rows = jnp.concatenate(parts, axis=1).astype(BF)
    out[...] = jnp.dot(pack[...], rows, preferred_element_type=F32).astype(BF)


def module_kernel(
    ids, incoming, pick, taps, w_two, acts,
    grad_out, grad_mixed, p0, p2, p4, p6, wide_gated, wide_grad, masks, w_here, kept, sems,
):
    place = ids[2]
    fetch_w = pltpu.make_async_copy(w_two, w_here, sems.at[0])
    fetch_w.start()
    fetch_acts = pltpu.make_async_copy(acts, kept, sems.at[1])
    fetch_acts.start()
    frame_rows, feat = grad_out.shape
    taps_count = taps.shape[0]
    taps = taps[...].astype(F32)
    half = taps_count // 2
    sources, slots, width = incoming.shape
    outer = sources // 2
    piece = width // outer
    fill_masks(ids, masks)
    clear_edges(wide_gated)
    clear_edges(wide_grad)
    for p in range(2):
        rows = jnp.concatenate([incoming[2 * o + p] for o in range(outer)], axis=0)
        got = jnp.dot(pick[p], rows, preferred_element_type=F32).astype(BF)
        for o in range(outer):
            first = (2 * o + p) * piece
            grad_out[:, first : first + piece] = got[:, o * piece : (o + 1) * piece]
    fetch_acts.wait()
    fetch_w.wait()
    here = slice(8, 8 + frame_rows)
    step = 256
    for c in range(feat // step):
        cols = slice(c * step, (c + 1) * step)
        wide_gated[here, cols] = (kept[0, :, cols] * kept[1, :, cols]).astype(BF).astype(F32)
        grad_act = lax.dot_general(grad_out[...], w_here[cols, :], COLS, preferred_element_type=F32)
        wide_grad[here, cols] = grad_act * kept[2, :, cols]
    step = 128
    tap_rows = []
    for c in range(feat // step):
        cols = slice(c * step, (c + 1) * step)
        grad_conv = wide_grad[here, cols]
        total = jnp.zeros((frame_rows, step), F32)
        columns = []
        for k in range(taps_count):
            start = 8 + k - half
            window = wide_gated[start : start + frame_rows, cols] * masks[k]
            columns.append(jnp.sum(window * grad_conv, axis=0, keepdims=True))
            start = 8 + half - k
            back = 2 * half - k
            total = total + taps[k : k + 1, cols] * (wide_grad[start : start + frame_rows, cols] * masks[back])
        tap_rows.append(jnp.concatenate(columns + [jnp.zeros((16 - taps_count, step), F32)], axis=0))
        gate = kept[1, :, cols]
        first = total * gate
        grad_mixed[:, c * step : (c + 1) * step] = first.astype(BF)
        grad_mixed[:, feat + c * step : feat + (c + 1) * step] = (first * kept[0, :, cols] * (1.0 - gate)).astype(BF)
    tap_rows = jnp.concatenate(tap_rows, axis=1).astype(BF)
    w1_cols, w2_cols = feat // 2, feat // 4
    for mask, out in enumerate((p0, p2, p4, p6)):
        q = jnp.bitwise_xor(place, mask)
        out[0:frame_rows, 0:w1_cols] = grad_mixed[:, aligned(q, w1_cols)]
        out[0:frame_rows, w1_cols:] = grad_out[:, aligned(q, w2_cols)]
        for h in range(2):
            tap_at = slice(frame_rows + 16 * h, frame_rows + 16 * (h + 1))
            out[tap_at, 0:w1_cols] = tap_rows[:, h * w1_cols : (h + 1) * w1_cols]
            out[tap_at, w1_cols:] = jnp.zeros((16, w2_cols), BF)


def weights_kernel(
    ids, near, near_core, far, far_core, g0, g1, g2, g3, g4, g5, g6, g7, own, s1, s2, s3, rows, tap_sum, feats, sems
):
    z = ids[1]
    copies = []
    for n, (three, one) in enumerate(((near, near_core), (far, far_core))):
        copies.append(pltpu.make_async_copy(three.at[0], feats.at[4 * n], sems.at[3 * n]))
        copies.append(pltpu.make_async_copy(three.at[1:3], feats.at[4 * n + 2 : 4 * n + 4], sems.at[3 * n + 1]))
        copies.append(pltpu.make_async_copy(one, feats.at[4 * n + 1], sems.at[3 * n + 2]))
    for copy in copies:
        copy.start()
    gots = (g0, g1, g2, g3, g4, g5, g6, g7)
    frame_rows = feats.shape[2]
    half = feats.shape[1] // 2
    w1_cols = half
    tap_sum[...] = sum(g[frame_rows:, 0:w1_cols].astype(F32) for g in gots)
    for copy in copies:
        copy.wait()
    for cols, first in ((slice(0, w1_cols), 0), (slice(w1_cols, g0.shape[1]), half)):
        total = None
        for m in range(0, 8, 2):
            both = jnp.concatenate([gots[m][0:frame_rows, cols], gots[m + 1][0:frame_rows, cols]], axis=0)
            pair = jnp.concatenate([feats[m, first : first + half, :], feats[m + 1, first : first + half, :]], axis=1)
            term = jnp.dot(pair, both, preferred_element_type=F32)
            total = term if total is None else total + term
        rows[:, cols] = total
    block = half // 4
    for m, out in enumerate((own, s1, s2, s3)):
        o = jnp.bitwise_xor(z, m)
        out[0:block, :] = rows[aligned(o, block), :].astype(out.dtype)
        out[block:, 0 : 2 * block] = tap_sum[aligned(o // 2, 16), aligned(o % 2, 2 * block)].astype(out.dtype)
        out[block:, 2 * block :] = jnp.zeros((out.shape[0] - block, out.shape[1] - 2 * block), out.dtype)


def tail_kernel(ids, x, grad_mixed, w_one, grad_out, out):
    standard, inverse = standardise(x)
    grad_norm = lax.dot_general(grad_mixed[...], w_one[...], COLS, preferred_element_type=F32)
    grad_input = inverse * (
        grad_norm
        - jnp.mean(grad_norm, axis=1, keepdims=True)
        - standard * jnp.mean(grad_norm * standard, axis=1, keepdims=True)
    )
    out[...] = (grad_out[...].astype(F32) + grad_input).astype(BF)


def sum_kernel(ids, own, r1, r2, r3, mine, f1, f2, f3, taps, rows):
    place = ids[2]
    part = mine.shape[0]
    rows[...] = own[...] + r1[...].astype(F32) + r2[...].astype(F32) + r3[...].astype(F32)
    for m, out in enumerate((mine, f1, f2, f3)):
        out[...] = rows[aligned(jnp.bitwise_xor(place, m), part), :].astype(out.dtype)
    taps[...] = rows[4 * part :, 0 : 8 * part]


def assembly_kernel(ids, mine, r1, r2, r3, w1, w2):
    place = ids[2]
    w1_cols, w2_cols = w1.shape[1] // 4, w2.shape[1] // 4
    for m, part in enumerate((mine, r1, r2, r3)):
        q = jnp.bitwise_xor(place, m)
        w1[:, aligned(q, w1_cols)] = part[:, 0:w1_cols].astype(F32)
        w2[:, aligned(q, w2_cols)] = part[:, w1_cols:].astype(F32)


def forward_part(layer_input, lengths, w_one, conv_taps, conv_scale, conv_shift):
    row_count, feat_width = layer_input.shape
    taps_count = conv_taps.shape[0]
    half_span = taps_count // 2
    ends = [lengths[0]]
    for j in range(1, lengths.shape[0]):
        ends.append(ends[-1] + lengths[j])
    position = lax.broadcasted_iota(jnp.int32, (row_count,), 0)
    segment = sum((position >= e).astype(jnp.int32) for e in ends)
    padded_seg = jnp.pad(segment, (half_span, half_span), constant_values=-1)
    as_float = layer_input.astype(F32)
    row_mean = jnp.mean(as_float, axis=1, keepdims=True)
    centred = as_float - row_mean
    inverse = lax.rsqrt(jnp.mean(centred * centred, axis=1, keepdims=True) + 1e-05)
    standard = centred * inverse
    normed = standard.astype(BF)
    mixed = jnp.dot(normed, w_one, preferred_element_type=F32)
    linear = mixed[:, :feat_width]
    gate_prob = jax.nn.sigmoid(mixed[:, feat_width:])
    gated = (linear * gate_prob).astype(BF)
    padded_gated = jnp.pad(gated, ((half_span, half_span), (0, 0))).astype(F32)
    tap_values = conv_taps.astype(F32)
    conv_sum = jnp.zeros((row_count, feat_width), F32)
    for k in range(taps_count):
        same_utt = padded_seg[k : k + row_count] == segment
        window = jnp.where(same_utt[:, None], padded_gated[k : k + row_count], 0.0)
        conv_sum = conv_sum + tap_values[k] * window
    pre_act = conv_sum * conv_scale + conv_shift
    act_prob = jax.nn.sigmoid(pre_act)
    activated = (pre_act * act_prob).astype(BF)
    slope = act_prob * (1.0 + pre_act * (1.0 - act_prob)) * conv_scale
    return standard, inverse, normed, linear, gate_prob, padded_gated, padded_seg, segment, activated, slope


def plain_shards(
    layer_input,
    utt_frames,
    w_pointwise1,
    conv_taps,
    conv_scale,
    conv_shift,
    w_pointwise2,
    adj_grad,
    proj_weight,
    adj_target,
    adj_frame,
):
    reps = lax.axis_size("rep")
    sections = lax.axis_size("section")
    rep_here = lax.axis_index("rep")
    sec_here = lax.axis_index("section")
    block_rows = adj_grad.shape[0]
    quarter = block_rows // sections
    frame_rows, feat = layer_input.shape
    taps_count = conv_taps.shape[0]
    half_span = taps_count // 2
    capacity = max(2, 2 * quarter // reps)
    outer = reps // 2
    pair_here = rep_here % 2
    outer_here = rep_here // 2
    piece = proj_weight.shape[0]

    adj_other = swap("rep", adj_grad, 1)
    blocks = [proj_weight] + [swap("rep", proj_weight, 2 * k) for k in range(1, outer)]

    targets = adj_target[:, 0].reshape(reps, sections, quarter)
    frames = adj_frame.reshape(reps, sections, quarter)
    sec_targets = lax.dynamic_index_in_dim(targets, sec_here, 1, keepdims=False)
    sec_frames = lax.dynamic_index_in_dim(frames, sec_here, 1, keepdims=False)
    row_a = lax.broadcasted_iota(jnp.int32, (quarter, quarter), 0)
    row_b = lax.broadcasted_iota(jnp.int32, (quarter, quarter), 1)
    same = (sec_targets[:, :, None] == sec_targets[:, None, :]) & (row_b < row_a)[None]
    rank = jnp.sum(same.astype(jnp.int32), axis=2)
    mine = sec_targets == rep_here
    slots = lax.broadcasted_iota(jnp.int32, (1, capacity, 1), 1)
    hit = mine[:, None, :] & (rank[:, None, :] == slots)
    slot_frames = jnp.sum(jnp.where(hit, sec_frames[:, None, :] + 1, 0), axis=2) - 1

    pair_blocks = jnp.stack([rep_here, jnp.bitwise_xor(rep_here, 1)])
    pair_targets = jnp.concatenate([lax.dynamic_index_in_dim(sec_targets, pair_blocks[w], 0, keepdims=False) for w in range(2)])
    pair_rank = jnp.concatenate([lax.dynamic_index_in_dim(rank, pair_blocks[w], 0, keepdims=False) for w in range(2)])
    member = lax.broadcasted_iota(jnp.int32, (2 * quarter,), 0) // quarter
    slot_of = (pair_targets * 2 + member) * capacity + pair_rank
    slot_ids = lax.broadcasted_iota(jnp.int32, (reps * 2 * capacity, 2 * quarter), 0)
    pack = (slot_of[None, :] == slot_ids).astype(BF)

    standard, inverse, normed, linear, gate_prob, padded_gated, padded_seg, segment, activated, slope = forward_part(
        layer_input, utt_frames[0], w_pointwise1, conv_taps, conv_scale, conv_shift
    )
    part_rows = feat // (reps * sections)

    here = rep_here * sections + sec_here
    core = here % 2
    place = (here // 2) % 4
    BOTH = ("rep", "section")

    def core_halves(values):
        return values.reshape(frame_rows, reps * sections // 2, 2, part_rows).transpose(2, 0, 1, 3).reshape(
            2, frame_rows, feat // 2
        )

    halves = jnp.concatenate([core_halves(normed), core_halves(activated)], axis=2)
    mine_half = lax.dynamic_index_in_dim(halves, core, 0, keepdims=False)
    their_half = lax.dynamic_index_in_dim(halves, 1 - core, 0, keepdims=False)
    chip_half = jnp.concatenate([mine_half, swap(BOTH, their_half, 1)], axis=0)
    early = {0: chip_half}
    for m in (2, 4, 6):
        early[m] = swap(BOTH, chip_half, m)
    near = early[0]
    straight = jnp.concatenate([early[m][:frame_rows] for m in (2, 4, 6)], axis=0)
    across = jnp.concatenate([early[m][frame_rows:] for m in (2, 4, 6)], axis=0)

    adj_pair = jnp.concatenate([adj_grad, adj_other], axis=0)

    def section_sum(lot):
        terms = [lax.dot_general(adj_pair, b, COLS, preferred_element_type=F32).astype(BF) for b in lot]
        terms = jnp.concatenate(terms, axis=1).reshape(2, sections, quarter, len(lot) * piece)
        total = lax.dynamic_index_in_dim(terms, sec_here, 1, keepdims=False).astype(F32)
        for m in range(1, sections):
            given = lax.dynamic_index_in_dim(terms, jnp.bitwise_xor(sec_here, m), 1, keepdims=False)
            total = total + swap("section", given, m).astype(F32)
        total = total.astype(BF).reshape(2 * quarter, len(lot) * piece)
        return [total[:, i * piece : (i + 1) * piece] for i in range(len(lot))]

    feat_grad = section_sum(blocks[:-1]) + section_sum(blocks[-1:])
    feat_grad = jnp.concatenate(xor_order(feat_grad, outer_here), axis=1)
    packed = jnp.dot(pack, feat_grad, preferred_element_type=F32).astype(BF)
    outgoing = packed.reshape(reps, 2 * capacity, outer * piece)
    incoming = lax.all_to_all(outgoing, "rep", split_axis=0, concat_axis=0, tiled=True)
    incoming = incoming.reshape(outer, 2, 2 * capacity, outer * piece)
    slot_frames = slot_frames.reshape(outer, 2, capacity)
    frame_ids = lax.broadcasted_iota(jnp.int32, (frame_rows, outer * 2 * capacity), 0)
    out_halves = []
    for p in range(2):
        order = jnp.stack([slot_frames[:, p], slot_frames[:, 1 - p]], axis=1).reshape(1, -1)
        pick = (frame_ids == order).astype(BF)
        out_halves.append(
            jnp.dot(pick, incoming[:, p].reshape(-1, outer * piece), preferred_element_type=F32)
            .astype(BF)
            .reshape(frame_rows, outer, piece)
        )
    grad_out = jnp.stack(out_halves, axis=2).reshape(frame_rows, feat)

    def weight_grad(first_col, values):
        width = values.shape[1] // 4
        lots = [values[:, q * width : (q + 1) * width] for q in range(4)]
        lots = xor_order(lots, place)
        got = {0: lots[0]}
        for m in (2, 4, 6):
            got[m] = swap(BOTH, lots[m // 2], m)
        for m in (0, 2, 4, 6):
            got[m + 1] = swap(BOTH, got[m], 1)
        cols = slice(first_col, first_col + feat // 2)
        part = lax.dot_general(near[:, cols], jnp.concatenate([got[0], got[1]]), ROWS, preferred_element_type=F32)
        part += lax.dot_general(
            straight[:, cols], jnp.concatenate([got[m] for m in (2, 4, 6)]), ROWS, preferred_element_type=F32
        )
        part += lax.dot_general(
            across[:, cols], jnp.concatenate([got[m] for m in (3, 5, 7)]), ROWS, preferred_element_type=F32
        )
        part = part.reshape(outer, 4 * part_rows, width)
        total = lax.dynamic_index_in_dim(part, outer_here, 0, keepdims=False)
        sent = part.astype(BF)
        for m in range(1, outer):
            given = lax.dynamic_index_in_dim(sent, jnp.bitwise_xor(outer_here, m), 0, keepdims=False)
            total = total + swap(BOTH, given, 8 * m).astype(F32)
        total = total.astype(BF)
        lots = xor_order([total[q * part_rows : (q + 1) * part_rows] for q in range(4)], place)
        lots = [lots[0]] + [swap(BOTH, lots[m], 2 * m) for m in (1, 2, 3)]
        return jnp.concatenate(xor_order(lots, place), axis=1).astype(F32)

    w2_grad = weight_grad(feat // 2, grad_out)

    grad_act = lax.dot_general(grad_out, w_pointwise2, COLS, preferred_element_type=F32)
    grad_conv = grad_act * slope
    padded_grad = jnp.pad(grad_conv, ((half_span, half_span), (0, 0)))
    grad_gated = jnp.zeros((frame_rows, feat), F32)
    tap_values = conv_taps.astype(F32)
    columns = []
    for k in range(taps_count):
        same_utt = padded_seg[k : k + frame_rows] == segment
        window = jnp.where(same_utt[:, None], padded_gated[k : k + frame_rows], 0.0)
        columns.append(jnp.sum(window * grad_conv, axis=0))
        back = 2 * half_span - k
        back_same = padded_seg[back : back + frame_rows] == segment
        grad_gated = grad_gated + tap_values[k] * jnp.where(
            back_same[:, None], padded_grad[back : back + frame_rows], 0.0
        )
    first = grad_gated * gate_prob
    grad_mixed = jnp.concatenate([first, first * linear * (1.0 - gate_prob)], axis=1).astype(BF)
    w1_grad = weight_grad(0, grad_mixed)
    taps_term = jnp.stack(columns, axis=0).reshape(taps_count, reps * sections, part_rows)
    taps_term = jnp.pad(taps_term.transpose(1, 0, 2), ((0, 0), (0, 16 - taps_count), (0, 0))).astype(BF)
    taps_all = lax.all_to_all(taps_term, BOTH, split_axis=0, concat_axis=0, tiled=True)
    taps_grad = jnp.sum(taps_all.astype(F32), axis=0)[:taps_count].T

    grad_norm = lax.dot_general(grad_mixed, w_pointwise1, COLS, preferred_element_type=F32)
    grad_input = inverse * (
        grad_norm
        - jnp.mean(grad_norm, axis=1, keepdims=True)
        - standard * jnp.mean(grad_norm * standard, axis=1, keepdims=True)
    )
    input_grad = (grad_out.astype(F32) + grad_input).astype(BF)
    return input_grad, w1_grad, w2_grad, taps_grad


def line_shards(
    layer_input,
    utt_frames,
    w_pointwise1,
    conv_taps,
    conv_scale,
    conv_shift,
    w_pointwise2,
    adj_grad,
    proj_weight,
    adj_target,
    adj_frame,
):
    reps = lax.axis_size("rep")
    sections = lax.axis_size("section")
    rep_here = lax.axis_index("rep")
    sec_here = lax.axis_index("section")
    block_rows = adj_grad.shape[0]
    quarter = block_rows // sections
    frame_rows, feat = layer_input.shape
    taps_count = conv_taps.shape[0]
    half_span = taps_count // 2
    capacity = max(2, 2 * quarter // reps)
    outer = reps // 2
    pair_here = rep_here % 2
    outer_here = rep_here // 2
    piece = proj_weight.shape[0]

    two = swap("rep", proj_weight, 4)
    one = swap("rep", proj_weight, 2)
    adj_other = swap("rep", adj_grad, 1)
    targets = adj_target[:, 0].reshape(reps, sections, quarter)
    frames = adj_frame.reshape(reps, sections, quarter)
    sec_targets = lax.dynamic_index_in_dim(targets, sec_here, 1, keepdims=False)
    sec_frames = lax.dynamic_index_in_dim(frames, sec_here, 1, keepdims=False)
    part_rows = feat // (reps * sections)

    here = rep_here * sections + sec_here
    core = here % 2
    place = (here // 2) % 4
    BOTH = ("rep", "section")

    ids = jnp.stack([sec_here, outer_here, place, core, rep_here]).astype(jnp.int32)
    ids = jnp.concatenate([ids, utt_frames[0]])
    pack, pick = local_call(
        routing_kernel,
        ids,
        (sec_targets.reshape(1, -1), sec_frames.reshape(1, -1)),
        [like((reps * 2 * capacity, 2 * quarter), BF), like((2, frame_rows, reps * capacity), BF)],
        name="routing",
    )
    square = (frame_rows, feat)
    group = 8
    dma = pltpu.SemaphoreType.DMA
    wide = pltpu.VMEM((frame_rows + 16, feat), F32)
    mask_space = pltpu.VMEM((taps_count, frame_rows, 128), F32)
    acts, mine_half, their_half = local_call(
        forward_kernel,
        ids,
        (layer_input, w_pointwise1, conv_taps, conv_scale.reshape(1, -1), conv_shift.reshape(1, -1)),
        [like((3, *square), F32), like((feat, frame_rows), BF), like((feat, frame_rows), BF)],
        [
            pltpu.VMEM((3, *square), F32),
            wide,
            mask_space,
            pltpu.VMEM((2, feat, frame_rows), F32),
            pltpu.VMEM((2, feat, frame_rows), BF),
            dma((3,)),
        ],
        flops=4 * frame_rows * feat * feat,
        name="forward",
        leave=(0, 1, 2),
    )
    near = [mine_half, swap(BOTH, mine_half, 2), swap(BOTH, their_half, 3)]
    two, one, near = lax.optimization_barrier((two, one, near))
    near = jnp.stack(near)
    proj_again, two, one, adj_other, pack, pick, near = lax.optimization_barrier(
        (proj_weight, two, one, adj_other, pack, pick, near)
    )
    inner = lax.ppermute(proj_again, "rep", [(o * 2 + p, (3 - o) * 2 + p) for o in (1, 2) for p in (0, 1)])
    ends = lax.ppermute(two, "rep", [(o * 2 + p, (o ^ 1) * 2 + p) for o in (1, 2) for p in (0, 1)])
    far_three = swap(BOTH, near, 4)
    near_core = swap(BOTH, their_half, 1)
    far_core = swap(BOTH, their_half, 5)

    rows = 2 * quarter

    def products(name, *lot):
        cols = piece * (3 if len(lot) == 3 else 1)
        sums = local_call(
            partial_kernel,
            ids,
            (adj_grad, adj_other, *lot),
            [like((rows, cols), F32)] + [like((rows, cols), BF)] * 3,
            [pltpu.VMEM((2, block_rows, cols), F32), pltpu.VMEM(adj_grad.shape, BF), pltpu.VMEM(proj_weight.shape, BF), dma((2,))],
            stay=(0, 2) if len(lot) == 3 else (0,),
            flops=4 * block_rows * adj_grad.shape[1] * cols,
            name=name,
        )
        return [sums[0]] + [swap("section", sums[m], m) for m in (1, 2, 3)]

    lot_one = products("products", proj_weight, one, two)
    inner, ends, lot_one = lax.optimization_barrier((inner, ends, lot_one))
    lot_two = products("last_products", inner, ends)
    lot_two, far_three, far_core = lax.optimization_barrier((lot_two, far_three, far_core))
    lane = outer * piece
    (packed,) = local_call(
        packing_kernel,
        ids,
        (*lot_one, *lot_two, pack),
        [like((reps * 2 * capacity, lane), BF)],
        name="packing",
        flops=2 * pack.size * lane,
    )
    outgoing = packed.reshape(reps, 2 * capacity, lane)
    incoming = lax.all_to_all(outgoing, "rep", split_axis=0, concat_axis=0, tiled=True)
    incoming, near_core = lax.optimization_barrier((incoming, near_core))
    late = like((frame_rows + 32, 3 * feat // 4), BF)
    lot = like((frame_rows + 16, 3 * feat // 4), BF)
    grad_out, grad_mixed, p0, p2, p4, p6 = local_call(
        module_kernel,
        ids,
        (incoming, pick, conv_taps, w_pointwise2, acts),
        [like(square, BF), like((frame_rows, 2 * feat), BF)] + [late] * 4,
        [wide, wide, mask_space, pltpu.VMEM((feat, feat), BF), pltpu.VMEM((3, *square), F32), dma((2,))],
        flops=2 * frame_rows * feat * feat + 60 * frame_rows * feat,
        name="module",
        stay=(3, 4),
    )
    got = [p0, swap(BOTH, p0, 1)]
    far = [swap(BOTH, p, m) for m, p in ((2, p2), (4, p4), (6, p6))]
    for p in far:
        got += [p, swap(BOTH, p, 1)]
    sums = local_call(
        weights_kernel,
        ids,
        (near, near_core, far_three, far_core, *got),
        [like(lot.shape, F32)] + [lot] * 3,
        [
            pltpu.VMEM((feat // 2, 3 * feat // 4), F32),
            pltpu.VMEM((32, feat // 2), F32),
            pltpu.VMEM((group, feat, frame_rows), BF),
            dma((6,)),
        ],
        stay=(0, 1, 2, 3),
        flops=2 * 8 * frame_rows * (feat // 2) * (3 * feat // 4),
        name="weights",
    )
    given = [swap(BOTH, sums[m], 8 * m) for m in (1, 2, 3)]
    final = (part_rows, 3 * feat // 4)
    mine_part, f1, f2, f3, tap_part = local_call(
        sum_kernel,
        ids,
        (sums[0], *given),
        [like(final, F32)] + [like(final, BF)] * 3 + [like((16, 8 * part_rows), F32)],
        [pltpu.VMEM(lot.shape, F32)],
        name="sums",
    )
    given = [swap(BOTH, f, 2 * m) for m, f in ((1, f1), (2, f2), (3, f3))]
    w1_grad, w2_grad = local_call(
        assembly_kernel,
        ids,
        (mine_part, *given),
        [like((part_rows, 2 * feat), F32), like((part_rows, feat), F32)],
        name="assembly",
    )
    here_taps = lax.dynamic_index_in_dim(
        tap_part.reshape(16, 8, part_rows), 2 * place + core, 1, keepdims=False
    )
    taps_grad = here_taps[:taps_count].T
    (input_grad,) = local_call(
        tail_kernel,
        ids,
        (layer_input, grad_mixed, w_pointwise1, grad_out),
        [like(square, BF)],
        flops=4 * frame_rows * feat * feat,
        name="tail",
    )
    return input_grad, w1_grad, w2_grad, taps_grad


def shards(layer_input, *rest):
    if lax.axis_size("rep") == 8 and lax.axis_size("section") == 4:
        return line_shards(layer_input, *rest)
    return plain_shards(layer_input, *rest)


def solution(mesh):
    spread = P(("rep", "section"), None)
    return jax.shard_map(
        shards,
        mesh=mesh,
        in_specs=(spread, spread, P(), P(), P(), P(), P(), P("rep", "section"), P("rep", "section"), P(), P()),
        out_specs=(spread, spread, spread, spread),
        check_vma=False,
    )
```

```python
import jax
import jax.numpy as jnp
from jax import lax
from jax.experimental import pallas as pl
from jax.experimental.pallas import tpu as pltpu
from jax.sharding import PartitionSpec as P

BF = jnp.bfloat16
F32 = jnp.float32
ROWS = (((0,), (0,)), ((), ()))
COLS = (((1,), (1,)), ((), ()))


def xor_perm(count, mask):
    return [(i, i ^ mask) for i in range(count)]


def size_of(axis):
    if isinstance(axis, tuple):
        return lax.axis_size(axis[0]) * lax.axis_size(axis[1])
    return lax.axis_size(axis)


def swap(axis, values, mask):
    return lax.ppermute(values, axis, xor_perm(size_of(axis), mask))


def xor_order(items, place):
    step = 1
    while step < len(items):
        flip = jnp.bitwise_and(place, step) > 0
        items = [jnp.where(flip, items[i ^ step], items[i]) for i in range(len(items))]
        step *= 2
    return items


def local_call(body, ids, operands, outs, scratch=(), flops=0, name=None, stay=(), leave=()):
    moved = sum(o.size * o.dtype.itemsize for o in operands) + sum(
        o.size * o.dtype.itemsize for o in outs
    )
    vmem, other = pl.BlockSpec(memory_space=pltpu.VMEM), pl.BlockSpec(memory_space=pltpu.HBM)
    return pl.pallas_call(
        body,
        out_shape=tuple(outs),
        in_specs=[pl.BlockSpec(memory_space=pltpu.SMEM)]
        + [other if i in stay else vmem for i in range(len(operands))],
        out_specs=tuple(other if i in leave else vmem for i in range(len(outs))),
        scratch_shapes=list(scratch),
        compiler_params=pltpu.CompilerParams(vmem_limit_bytes=(40 if stay or leave else 24) * 1024 * 1024),
        cost_estimate=pl.CostEstimate(flops=flops, bytes_accessed=moved, transcendentals=0),
        name=name,
    )(ids, *operands)


def like(shape, dtype):
    return jax.ShapeDtypeStruct(shape, dtype)


def aligned(index, size):
    return pl.ds(pl.multiple_of(index * size, size), size)


def routing_kernel(ids, targets, frames, pack, pick):
    here = ids[4]
    width = targets.shape[1]
    slots, rows = pack.shape
    quarter = rows // 2
    blocks = width // quarter
    capacity = slots // (2 * blocks)
    shape = (width, width)
    first, second = lax.broadcasted_iota(jnp.int32, shape, 0), lax.broadcasted_iota(jnp.int32, shape, 1)
    before = ((first < second) & (first // quarter == second // quarter)).astype(F32).astype(BF)
    names = lax.broadcasted_iota(jnp.int32, (blocks, width), 0)
    hits = (names == targets[...]).astype(F32)
    earlier = jnp.dot(hits.astype(BF), before, preferred_element_type=F32)
    rank = jnp.sum(hits * earlier, axis=0, keepdims=True)
    slot = targets[...].astype(F32) * (2 * capacity) + rank
    shape = (width, rows)
    row, col = lax.broadcasted_iota(jnp.int32, shape, 0), lax.broadcasted_iota(jnp.int32, shape, 1)
    wanted = jnp.bitwise_xor(here, col // quarter) * quarter + col % quarter
    take = (row == wanted).astype(F32).astype(BF)
    slot_of = jnp.dot(jnp.broadcast_to(slot, (8, width)).astype(BF), take, preferred_element_type=F32)[0:1, :]
    slot_of = slot_of.astype(jnp.int32) + lax.broadcasted_iota(jnp.int32, (1, rows), 1) // quarter * capacity
    slot_ids = lax.broadcasted_iota(jnp.int32, (slots, rows), 0)
    pack[...] = (slot_of == slot_ids).astype(F32).astype(BF)
    frame_rows = pick.shape[1]
    frame_ids = lax.broadcasted_iota(jnp.int32, (frame_rows, width), 0)
    at_frame = (frame_ids == frames[...]).astype(F32).astype(BF)
    block = lax.broadcasted_iota(jnp.int32, (1, width), 1) // quarter
    rank = rank.astype(jnp.int32)
    slot_ids = lax.broadcasted_iota(jnp.int32, (blocks * capacity, width), 0)
    for p in range(2):
        held = jnp.where(targets[...] == here, jnp.bitwise_xor(block, p) * capacity + rank, -1)
        in_slot = (slot_ids == held).astype(F32).astype(BF)
        pick[p] = lax.dot_general(at_frame, in_slot, COLS, preferred_element_type=F32).astype(BF)


def fill_masks(ids, masks):
    taps_count, frame_rows, _ = masks.shape
    ends = [ids[5]]
    for u in range(1, ids.shape[0] - 5):
        ends.append(ends[-1] + ids[5 + u])
    position = lax.broadcasted_iota(jnp.int32, masks.shape[1:], 0)

    def segment(at):
        return sum(jnp.where(at >= e, 1, 0) for e in ends)

    here = segment(position)
    for k in range(taps_count):
        at = position + (k - taps_count // 2)
        good = (segment(at) == here) & (at >= 0) & (at < frame_rows)
        masks[k] = jnp.where(good, 1.0, 0.0)


def clear_edges(wide):
    edge = jnp.zeros((8, wide.shape[1]), F32)
    wide[0:8, :] = edge
    wide[wide.shape[0] - 8 :, :] = edge


def standardise(x):
    as_float = x[...].astype(F32)
    centred = as_float - jnp.mean(as_float, axis=1, keepdims=True)
    inverse = lax.rsqrt(jnp.mean(centred * centred, axis=1, keepdims=True) + 1e-05)
    return centred * inverse, inverse


def forward_kernel(ids, x, w_one, taps, scale, shift, acts, mine, theirs, kept, wide, masks, flipped, halves, sems):
    core = ids[3]
    frame_rows, feat = x.shape
    taps_count = taps.shape[0]
    taps = taps[...].astype(F32)
    half = taps_count // 2
    fill_masks(ids, masks)
    normed = standardise(x)[0].astype(BF)
    clear_edges(wide)
    step = 256
    for c in range(feat // step):
        cols = slice(c * step, (c + 1) * step)
        lin = jnp.dot(normed, w_one[:, cols], preferred_element_type=F32)
        gate = jax.nn.sigmoid(
            jnp.dot(normed, w_one[:, feat + c * step : feat + (c + 1) * step], preferred_element_type=F32)
        )
        kept[0, :, cols] = lin
        kept[1, :, cols] = gate
        wide[8 : 8 + frame_rows, cols] = (lin * gate).astype(BF).astype(F32)
    for c in range(feat // 128):
        cols = slice(c * 128, (c + 1) * 128)
        total = jnp.zeros((frame_rows, 128), F32)
        for k in range(taps_count):
            start = 8 + k - half
            total = total + taps[k : k + 1, cols] * (wide[start : start + frame_rows, cols] * masks[k])
        pre = total * scale[:, cols] + shift[:, cols]
        prob = jax.nn.sigmoid(pre)
        kept[2, :, cols] = prob * (1.0 + pre * (1.0 - prob)) * scale[:, cols]
        flipped[0, cols, :] = normed[:, cols].astype(F32).T
        flipped[1, cols, :] = (pre * prob).astype(BF).astype(F32).T
    out_acts = pltpu.make_async_copy(kept, acts, sems.at[0])
    out_acts.start()
    part = feat // 32
    for h in range(2):
        for g in range(32):
            to = h * (feat // 2) + (g // 2) * part
            halves[g % 2, to : to + part, :] = flipped[h, g * part : (g + 1) * part, :].astype(BF)
    copies = [
        pltpu.make_async_copy(halves.at[core], mine, sems.at[1]),
        pltpu.make_async_copy(halves.at[1 - core], theirs, sems.at[2]),
    ]
    for copy in copies:
        copy.start()
    out_acts.wait()
    for copy in copies:
        copy.wait()


def quarters_out(sec, rows, outs, first):
    quarter = outs[0].shape[0] // 2
    cols = slice(first, first + rows.shape[2])
    for m, out in enumerate(outs):
        q = jnp.bitwise_xor(sec, m)
        for w in range(2):
            out[w * quarter : (w + 1) * quarter, cols] = rows[w, aligned(q, quarter), :].astype(out.dtype)


def products_kernel(ids, own_rows, other_rows, b0, b1, b2, own, s1, s2, s3, rows, own_copy, block_copy, sems):
    fetch = [
        pltpu.make_async_copy(own_rows, own_copy, sems.at[0]),
        pltpu.make_async_copy(b0, block_copy, sems.at[1]),
    ]
    for copy in fetch:
        copy.start()
    piece = b1.shape[0]
    both = jnp.concatenate([b1[...], b2[...]], axis=0)
    rows[1, :, piece:] = lax.dot_general(other_rows[...], both, COLS, preferred_element_type=F32)
    for copy in fetch:
        copy.wait()
    rows[0, :, piece:] = lax.dot_general(own_copy[...], both, COLS, preferred_element_type=F32)
    for w, a in ((1, other_rows), (0, own_copy)):
        rows[w, :, 0:piece] = lax.dot_general(a[...], block_copy[...], COLS, preferred_element_type=F32)
    quarters_out(ids[0], rows, (own, s1, s2, s3), 0)


def last_kernel(
    ids, own_rows, other_rows, inner, ends, e0, e1, e2, e3, own, s1, s2, s3, rows, own_copy, sem
):
    fetch = pltpu.make_async_copy(own_rows, own_copy, sem)
    fetch.start()
    z = ids[1]
    block = jnp.where((z == 1) | (z == 2), inner[...], ends[...])
    rows[1] = lax.dot_general(other_rows[...], block, COLS, preferred_element_type=F32)
    fetch.wait()
    rows[0] = lax.dot_general(own_copy[...], block, COLS, preferred_element_type=F32)
    outs = (own, s1, s2, s3)
    done = e0.shape[1]
    for earlier, out in zip((e0, e1, e2, e3), outs):
        out[:, 0:done] = earlier[...]
    quarters_out(ids[0], rows, outs, done)


def packing_kernel(ids, own, r1, r2, r3, pack, out):
    total = own[...] + r1[...].astype(F32) + r2[...].astype(F32) + r3[...].astype(F32)
    piece = total.shape[1] // 4
    parts = xor_order([total[:, k * piece : (k + 1) * piece] for k in range(4)], ids[1])
    rows = jnp.concatenate(parts, axis=1).astype(BF)
    out[...] = jnp.dot(pack[...], rows, preferred_element_type=F32).astype(BF)


def module_kernel(
    ids, incoming, pick, taps, w_two, acts,
    grad_out, grad_mixed, p0, p2, p4, p6, wide_gated, wide_grad, masks, w_here, kept, sems,
):
    place = ids[2]
    fetch_w = pltpu.make_async_copy(w_two, w_here, sems.at[0])
    fetch_w.start()
    fetch_acts = pltpu.make_async_copy(acts, kept, sems.at[1])
    fetch_acts.start()
    frame_rows, feat = grad_out.shape
    taps_count = taps.shape[0]
    taps = taps[...].astype(F32)
    half = taps_count // 2
    sources, slots, width = incoming.shape
    outer = sources // 2
    piece = width // outer
    fill_masks(ids, masks)
    clear_edges(wide_gated)
    clear_edges(wide_grad)
    for p in range(2):
        rows = jnp.concatenate([incoming[2 * o + p] for o in range(outer)], axis=0)
        got = jnp.dot(pick[p], rows, preferred_element_type=F32).astype(BF)
        for o in range(outer):
            first = (2 * o + p) * piece
            grad_out[:, first : first + piece] = got[:, o * piece : (o + 1) * piece]
    fetch_acts.wait()
    fetch_w.wait()
    here = slice(8, 8 + frame_rows)
    step = 256
    for c in range(feat // step):
        cols = slice(c * step, (c + 1) * step)
        wide_gated[here, cols] = (kept[0, :, cols] * kept[1, :, cols]).astype(BF).astype(F32)
        grad_act = lax.dot_general(grad_out[...], w_here[cols, :], COLS, preferred_element_type=F32)
        wide_grad[here, cols] = grad_act * kept[2, :, cols]
    step = 128
    tap_rows = []
    for c in range(feat // step):
        cols = slice(c * step, (c + 1) * step)
        grad_conv = wide_grad[here, cols]
        total = jnp.zeros((frame_rows, step), F32)
        columns = []
        for k in range(taps_count):
            start = 8 + k - half
            window = wide_gated[start : start + frame_rows, cols] * masks[k]
            columns.append(jnp.sum(window * grad_conv, axis=0, keepdims=True))
            start = 8 + half - k
            back = 2 * half - k
            total = total + taps[k : k + 1, cols] * (wide_grad[start : start + frame_rows, cols] * masks[back])
        tap_rows.append(jnp.concatenate(columns + [jnp.zeros((16 - taps_count, step), F32)], axis=0))
        gate = kept[1, :, cols]
        first = total * gate
        grad_mixed[:, c * step : (c + 1) * step] = first.astype(BF)
        grad_mixed[:, feat + c * step : feat + (c + 1) * step] = (first * kept[0, :, cols] * (1.0 - gate)).astype(BF)
    tap_rows = jnp.concatenate(tap_rows, axis=1).astype(BF)
    w1_cols, w2_cols = feat // 2, feat // 4
    for mask, out in enumerate((p0, p2, p4, p6)):
        q = jnp.bitwise_xor(place, mask)
        out[0:frame_rows, 0:w1_cols] = grad_mixed[:, aligned(q, w1_cols)]
        out[0:frame_rows, w1_cols:] = grad_out[:, aligned(q, w2_cols)]
        for h in range(2):
            tap_at = slice(frame_rows + 16 * h, frame_rows + 16 * (h + 1))
            out[tap_at, 0:w1_cols] = tap_rows[:, h * w1_cols : (h + 1) * w1_cols]
            out[tap_at, w1_cols:] = jnp.zeros((16, w2_cols), BF)


def weights_kernel(
    ids, near, near_core, far, far_core, g0, g1, g2, g3, g4, g5, g6, g7, own, s1, s2, s3, rows, tap_sum, feats, sems
):
    z = ids[1]
    copies = []
    for n, (three, one) in enumerate(((near, near_core), (far, far_core))):
        copies.append(pltpu.make_async_copy(three.at[0], feats.at[4 * n], sems.at[3 * n]))
        copies.append(pltpu.make_async_copy(three.at[1:3], feats.at[4 * n + 2 : 4 * n + 4], sems.at[3 * n + 1]))
        copies.append(pltpu.make_async_copy(one, feats.at[4 * n + 1], sems.at[3 * n + 2]))
    for copy in copies:
        copy.start()
    gots = (g0, g1, g2, g3, g4, g5, g6, g7)
    frame_rows = feats.shape[2]
    half = feats.shape[1] // 2
    w1_cols = half
    tap_sum[...] = sum(g[frame_rows:, 0:w1_cols].astype(F32) for g in gots)
    for copy in copies:
        copy.wait()
    for cols, first in ((slice(0, w1_cols), 0), (slice(w1_cols, g0.shape[1]), half)):
        total = None
        for m in range(0, 8, 2):
            both = jnp.concatenate([gots[m][0:frame_rows, cols], gots[m + 1][0:frame_rows, cols]], axis=0)
            pair = jnp.concatenate([feats[m, first : first + half, :], feats[m + 1, first : first + half, :]], axis=1)
            term = jnp.dot(pair, both, preferred_element_type=F32)
            total = term if total is None else total + term
        rows[:, cols] = total
    block = half // 4
    for m, out in enumerate((own, s1, s2, s3)):
        o = jnp.bitwise_xor(z, m)
        out[0:block, :] = rows[aligned(o, block), :].astype(out.dtype)
        out[block:, 0 : 2 * block] = tap_sum[aligned(o // 2, 16), aligned(o % 2, 2 * block)].astype(out.dtype)
        out[block:, 2 * block :] = jnp.zeros((out.shape[0] - block, out.shape[1] - 2 * block), out.dtype)


def tail_kernel(ids, x, grad_mixed, w_one, grad_out, out):
    standard, inverse = standardise(x)
    grad_norm = lax.dot_general(grad_mixed[...], w_one[...], COLS, preferred_element_type=F32)
    grad_input = inverse * (
        grad_norm
        - jnp.mean(grad_norm, axis=1, keepdims=True)
        - standard * jnp.mean(grad_norm * standard, axis=1, keepdims=True)
    )
    out[...] = (grad_out[...].astype(F32) + grad_input).astype(BF)


def sum_kernel(ids, own, r1, r2, r3, mine, f1, f2, f3, taps, rows):
    place = ids[2]
    part = mine.shape[0]
    rows[...] = own[...] + r1[...].astype(F32) + r2[...].astype(F32) + r3[...].astype(F32)
    for m, out in enumerate((mine, f1, f2, f3)):
        out[...] = rows[aligned(jnp.bitwise_xor(place, m), part), :].astype(out.dtype)
    taps[...] = rows[4 * part :, 0 : 8 * part]


def assembly_kernel(ids, mine, r1, r2, r3, w1, w2):
    place = ids[2]
    w1_cols, w2_cols = w1.shape[1] // 4, w2.shape[1] // 4
    for m, part in enumerate((mine, r1, r2, r3)):
        q = jnp.bitwise_xor(place, m)
        w1[:, aligned(q, w1_cols)] = part[:, 0:w1_cols].astype(F32)
        w2[:, aligned(q, w2_cols)] = part[:, w1_cols:].astype(F32)


def forward_part(layer_input, lengths, w_one, conv_taps, conv_scale, conv_shift):
    row_count, feat_width = layer_input.shape
    taps_count = conv_taps.shape[0]
    half_span = taps_count // 2
    ends = [lengths[0]]
    for j in range(1, lengths.shape[0]):
        ends.append(ends[-1] + lengths[j])
    position = lax.broadcasted_iota(jnp.int32, (row_count,), 0)
    segment = sum((position >= e).astype(jnp.int32) for e in ends)
    padded_seg = jnp.pad(segment, (half_span, half_span), constant_values=-1)
    as_float = layer_input.astype(F32)
    row_mean = jnp.mean(as_float, axis=1, keepdims=True)
    centred = as_float - row_mean
    inverse = lax.rsqrt(jnp.mean(centred * centred, axis=1, keepdims=True) + 1e-05)
    standard = centred * inverse
    normed = standard.astype(BF)
    mixed = jnp.dot(normed, w_one, preferred_element_type=F32)
    linear = mixed[:, :feat_width]
    gate_prob = jax.nn.sigmoid(mixed[:, feat_width:])
    gated = (linear * gate_prob).astype(BF)
    padded_gated = jnp.pad(gated, ((half_span, half_span), (0, 0))).astype(F32)
    tap_values = conv_taps.astype(F32)
    conv_sum = jnp.zeros((row_count, feat_width), F32)
    for k in range(taps_count):
        same_utt = padded_seg[k : k + row_count] == segment
        window = jnp.where(same_utt[:, None], padded_gated[k : k + row_count], 0.0)
        conv_sum = conv_sum + tap_values[k] * window
    pre_act = conv_sum * conv_scale + conv_shift
    act_prob = jax.nn.sigmoid(pre_act)
    activated = (pre_act * act_prob).astype(BF)
    slope = act_prob * (1.0 + pre_act * (1.0 - act_prob)) * conv_scale
    return standard, inverse, normed, linear, gate_prob, padded_gated, padded_seg, segment, activated, slope


def plain_shards(
    layer_input,
    utt_frames,
    w_pointwise1,
    conv_taps,
    conv_scale,
    conv_shift,
    w_pointwise2,
    adj_grad,
    proj_weight,
    adj_target,
    adj_frame,
):
    reps = lax.axis_size("rep")
    sections = lax.axis_size("section")
    rep_here = lax.axis_index("rep")
    sec_here = lax.axis_index("section")
    block_rows = adj_grad.shape[0]
    quarter = block_rows // sections
    frame_rows, feat = layer_input.shape
    taps_count = conv_taps.shape[0]
    half_span = taps_count // 2
    capacity = max(2, 2 * quarter // reps)
    outer = reps // 2
    pair_here = rep_here % 2
    outer_here = rep_here // 2
    piece = proj_weight.shape[0]

    adj_other = swap("rep", adj_grad, 1)
    blocks = [proj_weight] + [swap("rep", proj_weight, 2 * k) for k in range(1, outer)]

    targets = adj_target[:, 0].reshape(reps, sections, quarter)
    frames = adj_frame.reshape(reps, sections, quarter)
    sec_targets = lax.dynamic_index_in_dim(targets, sec_here, 1, keepdims=False)
    sec_frames = lax.dynamic_index_in_dim(frames, sec_here, 1, keepdims=False)
    row_a = lax.broadcasted_iota(jnp.int32, (quarter, quarter), 0)
    row_b = lax.broadcasted_iota(jnp.int32, (quarter, quarter), 1)
    same = (sec_targets[:, :, None] == sec_targets[:, None, :]) & (row_b < row_a)[None]
    rank = jnp.sum(same.astype(jnp.int32), axis=2)
    mine = sec_targets == rep_here
    slots = lax.broadcasted_iota(jnp.int32, (1, capacity, 1), 1)
    hit = mine[:, None, :] & (rank[:, None, :] == slots)
    slot_frames = jnp.sum(jnp.where(hit, sec_frames[:, None, :] + 1, 0), axis=2) - 1

    pair_blocks = jnp.stack([rep_here, jnp.bitwise_xor(rep_here, 1)])
    pair_targets = jnp.concatenate([lax.dynamic_index_in_dim(sec_targets, pair_blocks[w], 0, keepdims=False) for w in range(2)])
    pair_rank = jnp.concatenate([lax.dynamic_index_in_dim(rank, pair_blocks[w], 0, keepdims=False) for w in range(2)])
    member = lax.broadcasted_iota(jnp.int32, (2 * quarter,), 0) // quarter
    slot_of = (pair_targets * 2 + member) * capacity + pair_rank
    slot_ids = lax.broadcasted_iota(jnp.int32, (reps * 2 * capacity, 2 * quarter), 0)
    pack = (slot_of[None, :] == slot_ids).astype(BF)

    standard, inverse, normed, linear, gate_prob, padded_gated, padded_seg, segment, activated, slope = forward_part(
        layer_input, utt_frames[0], w_pointwise1, conv_taps, conv_scale, conv_shift
    )
    part_rows = feat // (reps * sections)

    here = rep_here * sections + sec_here
    core = here % 2
    place = (here // 2) % 4
    BOTH = ("rep", "section")

    def core_halves(values):
        return values.reshape(frame_rows, reps * sections // 2, 2, part_rows).transpose(2, 0, 1, 3).reshape(
            2, frame_rows, feat // 2
        )

    halves = jnp.concatenate([core_halves(normed), core_halves(activated)], axis=2)
    mine_half = lax.dynamic_index_in_dim(halves, core, 0, keepdims=False)
    their_half = lax.dynamic_index_in_dim(halves, 1 - core, 0, keepdims=False)
    chip_half = jnp.concatenate([mine_half, swap(BOTH, their_half, 1)], axis=0)
    early = {0: chip_half}
    for m in (2, 4, 6):
        early[m] = swap(BOTH, chip_half, m)
    near = early[0]
    straight = jnp.concatenate([early[m][:frame_rows] for m in (2, 4, 6)], axis=0)
    across = jnp.concatenate([early[m][frame_rows:] for m in (2, 4, 6)], axis=0)

    adj_pair = jnp.concatenate([adj_grad, adj_other], axis=0)

    def section_sum(lot):
        terms = [lax.dot_general(adj_pair, b, COLS, preferred_element_type=F32).astype(BF) for b in lot]
        terms = jnp.concatenate(terms, axis=1).reshape(2, sections, quarter, len(lot) * piece)
        total = lax.dynamic_index_in_dim(terms, sec_here, 1, keepdims=False).astype(F32)
        for m in range(1, sections):
            given = lax.dynamic_index_in_dim(terms, jnp.bitwise_xor(sec_here, m), 1, keepdims=False)
            total = total + swap("section", given, m).astype(F32)
        total = total.astype(BF).reshape(2 * quarter, len(lot) * piece)
        return [total[:, i * piece : (i + 1) * piece] for i in range(len(lot))]

    feat_grad = section_sum(blocks[:-1]) + section_sum(blocks[-1:])
    feat_grad = jnp.concatenate(xor_order(feat_grad, outer_here), axis=1)
    packed = jnp.dot(pack, feat_grad, preferred_element_type=F32).astype(BF)
    outgoing = packed.reshape(reps, 2 * capacity, outer * piece)
    incoming = lax.all_to_all(outgoing, "rep", split_axis=0, concat_axis=0, tiled=True)
    incoming = incoming.reshape(outer, 2, 2 * capacity, outer * piece)
    slot_frames = slot_frames.reshape(outer, 2, capacity)
    frame_ids = lax.broadcasted_iota(jnp.int32, (frame_rows, outer * 2 * capacity), 0)
    out_halves = []
    for p in range(2):
        order = jnp.stack([slot_frames[:, p], slot_frames[:, 1 - p]], axis=1).reshape(1, -1)
        pick = (frame_ids == order).astype(BF)
        out_halves.append(
            jnp.dot(pick, incoming[:, p].reshape(-1, outer * piece), preferred_element_type=F32)
            .astype(BF)
            .reshape(frame_rows, outer, piece)
        )
    grad_out = jnp.stack(out_halves, axis=2).reshape(frame_rows, feat)

    def weight_grad(first_col, values):
        width = values.shape[1] // 4
        lots = [values[:, q * width : (q + 1) * width] for q in range(4)]
        lots = xor_order(lots, place)
        got = {0: lots[0]}
        for m in (2, 4, 6):
            got[m] = swap(BOTH, lots[m // 2], m)
        for m in (0, 2, 4, 6):
            got[m + 1] = swap(BOTH, got[m], 1)
        cols = slice(first_col, first_col + feat // 2)
        part = lax.dot_general(near[:, cols], jnp.concatenate([got[0], got[1]]), ROWS, preferred_element_type=F32)
        part += lax.dot_general(
            straight[:, cols], jnp.concatenate([got[m] for m in (2, 4, 6)]), ROWS, preferred_element_type=F32
        )
        part += lax.dot_general(
            across[:, cols], jnp.concatenate([got[m] for m in (3, 5, 7)]), ROWS, preferred_element_type=F32
        )
        part = part.reshape(outer, 4 * part_rows, width)
        total = lax.dynamic_index_in_dim(part, outer_here, 0, keepdims=False)
        sent = part.astype(BF)
        for m in range(1, outer):
            given = lax.dynamic_index_in_dim(sent, jnp.bitwise_xor(outer_here, m), 0, keepdims=False)
            total = total + swap(BOTH, given, 8 * m).astype(F32)
        total = total.astype(BF)
        lots = xor_order([total[q * part_rows : (q + 1) * part_rows] for q in range(4)], place)
        lots = [lots[0]] + [swap(BOTH, lots[m], 2 * m) for m in (1, 2, 3)]
        return jnp.concatenate(xor_order(lots, place), axis=1).astype(F32)

    w2_grad = weight_grad(feat // 2, grad_out)

    grad_act = lax.dot_general(grad_out, w_pointwise2, COLS, preferred_element_type=F32)
    grad_conv = grad_act * slope
    padded_grad = jnp.pad(grad_conv, ((half_span, half_span), (0, 0)))
    grad_gated = jnp.zeros((frame_rows, feat), F32)
    tap_values = conv_taps.astype(F32)
    columns = []
    for k in range(taps_count):
        same_utt = padded_seg[k : k + frame_rows] == segment
        window = jnp.where(same_utt[:, None], padded_gated[k : k + frame_rows], 0.0)
        columns.append(jnp.sum(window * grad_conv, axis=0))
        back = 2 * half_span - k
        back_same = padded_seg[back : back + frame_rows] == segment
        grad_gated = grad_gated + tap_values[k] * jnp.where(
            back_same[:, None], padded_grad[back : back + frame_rows], 0.0
        )
    first = grad_gated * gate_prob
    grad_mixed = jnp.concatenate([first, first * linear * (1.0 - gate_prob)], axis=1).astype(BF)
    w1_grad = weight_grad(0, grad_mixed)
    taps_term = jnp.stack(columns, axis=0).reshape(taps_count, reps * sections, part_rows)
    taps_term = jnp.pad(taps_term.transpose(1, 0, 2), ((0, 0), (0, 16 - taps_count), (0, 0))).astype(BF)
    taps_all = lax.all_to_all(taps_term, BOTH, split_axis=0, concat_axis=0, tiled=True)
    taps_grad = jnp.sum(taps_all.astype(F32), axis=0)[:taps_count].T

    grad_norm = lax.dot_general(grad_mixed, w_pointwise1, COLS, preferred_element_type=F32)
    grad_input = inverse * (
        grad_norm
        - jnp.mean(grad_norm, axis=1, keepdims=True)
        - standard * jnp.mean(grad_norm * standard, axis=1, keepdims=True)
    )
    input_grad = (grad_out.astype(F32) + grad_input).astype(BF)
    return input_grad, w1_grad, w2_grad, taps_grad


def line_shards(
    layer_input,
    utt_frames,
    w_pointwise1,
    conv_taps,
    conv_scale,
    conv_shift,
    w_pointwise2,
    adj_grad,
    proj_weight,
    adj_target,
    adj_frame,
):
    reps = lax.axis_size("rep")
    sections = lax.axis_size("section")
    rep_here = lax.axis_index("rep")
    sec_here = lax.axis_index("section")
    block_rows = adj_grad.shape[0]
    quarter = block_rows // sections
    frame_rows, feat = layer_input.shape
    taps_count = conv_taps.shape[0]
    half_span = taps_count // 2
    capacity = max(2, 2 * quarter // reps)
    outer = reps // 2
    pair_here = rep_here % 2
    outer_here = rep_here // 2
    piece = proj_weight.shape[0]

    two = swap("rep", proj_weight, 4)
    one = swap("rep", proj_weight, 2)
    adj_other = swap("rep", adj_grad, 1)
    targets = adj_target[:, 0].reshape(reps, sections, quarter)
    frames = adj_frame.reshape(reps, sections, quarter)
    sec_targets = lax.dynamic_index_in_dim(targets, sec_here, 1, keepdims=False)
    sec_frames = lax.dynamic_index_in_dim(frames, sec_here, 1, keepdims=False)
    part_rows = feat // (reps * sections)

    here = rep_here * sections + sec_here
    core = here % 2
    place = (here // 2) % 4
    BOTH = ("rep", "section")

    ids = jnp.stack([sec_here, outer_here, place, core, rep_here]).astype(jnp.int32)
    ids = jnp.concatenate([ids, utt_frames[0]])
    pack, pick = local_call(
        routing_kernel,
        ids,
        (sec_targets.reshape(1, -1), sec_frames.reshape(1, -1)),
        [like((reps * 2 * capacity, 2 * quarter), BF), like((2, frame_rows, reps * capacity), BF)],
        name="routing",
    )
    square = (frame_rows, feat)
    group = 8
    dma = pltpu.SemaphoreType.DMA
    wide = pltpu.VMEM((frame_rows + 16, feat), F32)
    mask_space = pltpu.VMEM((taps_count, frame_rows, 128), F32)
    acts, mine_half, their_half = local_call(
        forward_kernel,
        ids,
        (layer_input, w_pointwise1, conv_taps, conv_scale.reshape(1, -1), conv_shift.reshape(1, -1)),
        [like((3, *square), F32), like((feat, frame_rows), BF), like((feat, frame_rows), BF)],
        [
            pltpu.VMEM((3, *square), F32),
            wide,
            mask_space,
            pltpu.VMEM((2, feat, frame_rows), F32),
            pltpu.VMEM((2, feat, frame_rows), BF),
            dma((3,)),
        ],
        flops=4 * frame_rows * feat * feat,
        name="forward",
        leave=(0, 1, 2),
    )
    near = [mine_half, swap(BOTH, mine_half, 2), swap(BOTH, their_half, 3)]
    two, one, near = lax.optimization_barrier((two, one, near))
    near = jnp.stack(near)
    proj_again, two, one, adj_other, pack, pick, near = lax.optimization_barrier(
        (proj_weight, two, one, adj_other, pack, pick, near)
    )
    inner = lax.ppermute(proj_again, "rep", [(o * 2 + p, (3 - o) * 2 + p) for o in (1, 2) for p in (0, 1)])
    ends = lax.ppermute(two, "rep", [(o * 2 + p, (o ^ 1) * 2 + p) for o in (1, 2) for p in (0, 1)])
    far_three = swap(BOTH, near, 4)
    near_core = swap(BOTH, their_half, 1)
    far_core = swap(BOTH, their_half, 5)

    rows = 2 * quarter

    def products(body, name, cols, done, operands, stay, scratch):
        return local_call(
            body,
            ids,
            (adj_grad, adj_other, *operands),
            [like((rows, done + cols), F32)] + [like((rows, done + cols), BF)] * 3,
            [pltpu.VMEM((2, block_rows, cols), F32), pltpu.VMEM(adj_grad.shape, BF), *scratch],
            stay=stay,
            flops=4 * block_rows * adj_grad.shape[1] * cols,
            name=name,
        )

    sums = products(
        products_kernel, "products", 3 * piece, 0, (proj_weight, one, two), (0, 2), (pltpu.VMEM(proj_weight.shape, BF), dma((2,)))
    )
    inner, ends, sums, near_core = lax.optimization_barrier((inner, ends, sums, near_core))
    sums = products(last_kernel, "last_products", piece, 3 * piece, (inner, ends, *sums), (0,), (dma,))
    given = [swap("section", sums[m], m) for m in (1, 2, 3)]
    given, far_three, far_core = lax.optimization_barrier((given, far_three, far_core))
    lane = outer * piece
    (packed,) = local_call(
        packing_kernel,
        ids,
        (sums[0], *given, pack),
        [like((reps * 2 * capacity, lane), BF)],
        name="packing",
        flops=2 * pack.size * lane,
    )
    outgoing = packed.reshape(reps, 2 * capacity, lane)
    incoming = lax.all_to_all(outgoing, "rep", split_axis=0, concat_axis=0, tiled=True)
    late = like((frame_rows + 32, 3 * feat // 4), BF)
    lot = like((frame_rows + 16, 3 * feat // 4), BF)
    grad_out, grad_mixed, p0, p2, p4, p6 = local_call(
        module_kernel,
        ids,
        (incoming, pick, conv_taps, w_pointwise2, acts),
        [like(square, BF), like((frame_rows, 2 * feat), BF)] + [late] * 4,
        [wide, wide, mask_space, pltpu.VMEM((feat, feat), BF), pltpu.VMEM((3, *square), F32), dma((2,))],
        flops=2 * frame_rows * feat * feat + 60 * frame_rows * feat,
        name="module",
        stay=(3, 4),
    )
    got = [p0, swap(BOTH, p0, 1)]
    far = [swap(BOTH, p, m) for m, p in ((2, p2), (4, p4), (6, p6))]
    for p in far:
        got += [p, swap(BOTH, p, 1)]
    sums = local_call(
        weights_kernel,
        ids,
        (near, near_core, far_three, far_core, *got),
        [like(lot.shape, F32)] + [lot] * 3,
        [
            pltpu.VMEM((feat // 2, 3 * feat // 4), F32),
            pltpu.VMEM((32, feat // 2), F32),
            pltpu.VMEM((group, feat, frame_rows), BF),
            dma((6,)),
        ],
        stay=(0, 1, 2, 3),
        flops=2 * 8 * frame_rows * (feat // 2) * (3 * feat // 4),
        name="weights",
    )
    given = [swap(BOTH, sums[m], 8 * m) for m in (1, 2, 3)]
    final = (part_rows, 3 * feat // 4)
    mine_part, f1, f2, f3, tap_part = local_call(
        sum_kernel,
        ids,
        (sums[0], *given),
        [like(final, F32)] + [like(final, BF)] * 3 + [like((16, 8 * part_rows), F32)],
        [pltpu.VMEM(lot.shape, F32)],
        name="sums",
    )
    given = [swap(BOTH, f, 2 * m) for m, f in ((1, f1), (2, f2), (3, f3))]
    w1_grad, w2_grad = local_call(
        assembly_kernel,
        ids,
        (mine_part, *given),
        [like((part_rows, 2 * feat), F32), like((part_rows, feat), F32)],
        name="assembly",
    )
    here_taps = lax.dynamic_index_in_dim(
        tap_part.reshape(16, 8, part_rows), 2 * place + core, 1, keepdims=False
    )
    taps_grad = here_taps[:taps_count].T
    (input_grad,) = local_call(
        tail_kernel,
        ids,
        (layer_input, grad_mixed, w_pointwise1, grad_out),
        [like(square, BF)],
        flops=4 * frame_rows * feat * feat,
        name="tail",
    )
    return input_grad, w1_grad, w2_grad, taps_grad


def shards(layer_input, *rest):
    if lax.axis_size("rep") == 8 and lax.axis_size("section") == 4:
        return line_shards(layer_input, *rest)
    return plain_shards(layer_input, *rest)


def solution(mesh):
    spread = P(("rep", "section"), None)
    return jax.shard_map(
        shards,
        mesh=mesh,
        in_specs=(spread, spread, P(), P(), P(), P(), P(), P("rep", "section"), P("rep", "section"), P(), P()),
        out_specs=(spread, spread, spread, spread),
        check_vma=False,
    )
```
